256 devices in a mesh: row: 32 (over y, z_lo, core), col: 8 (over z_hi, x).
Axes of the slice: x: 4, y: 4, z: 8 (z_hi: 2, z_lo: 4; z = z_hi * 4 + z_lo), core: 2. Of those that a mesh axis runs over, the one named last changes fastest.
Arguments:
- views: bfloat16 [81, 2048, 2048], P(None, 'row', 'col'), may hold values from -6 to 6
Outputs:
- increment: float32 [2048, 2048], P('row', 'col')
- residual: float32 [2048, 2048], P('row', 'col')
The draws below stay inside these ranges and needn't reach their ends.
All inputs are finite; a program needn't handle non-finite values.
Results may differ from the reference program's by a relative error of at most 0.0005.
Values may be sent and summed in bfloat16 or wider, within the bound.
No kernel may reach another device: no remote copies, remote signals or barrier semaphores. Data moves between devices by JAX's collectives and lax.ppermute only.
A program may use at most 64 MiB of HBM per device.

```python
import jax
import jax.numpy as jnp

ANG = 9
VIEWS = 81
D0 = 3
HALO = 13
ITERS = 2
NR = 2048
NC = 2048


def levels(own_key, extent, split, least, high):
    factor_of = 1.0
    for axis_at, shards_of in split:
        draws = jax.random.uniform(jax.random.fold_in(jax.random.fold_in(own_key, 6), axis_at), (shards_of,), jnp.float32, least / len(split), high / len(split))
        factor_of = factor_of * jnp.repeat(jnp.exp(draws), extent[axis_at] // shards_of).reshape((-1,) + (1,) * (len(extent) - 1 - axis_at))
    return factor_of


def scatter_about(own_key, dims, scale, most, cuts=(), kind=jnp.bfloat16):
    loudness = levels(own_key, dims, cuts, -0.22, 0.18) if cuts else 1.0
    result = jax.random.normal(own_key, dims, jnp.float32) * scale * loudness
    return jnp.minimum(jnp.maximum(result, -most), most).astype(kind)


def setup_inputs(seed: int = 0) -> dict:
    key_of = jax.random.split(jax.random.key(seed), 2)
    views = scatter_about(key_of[0], (VIEWS, NR, NC), 1.0, 6.0, ((1, 32), (2, 8)))
    return {"views": views}


smooth_weight = 2.0
damping = 0.1

def edge_weights(center):
    padded = jnp.pad(center, 1)
    across = padded[1:-1, 1:] - padded[1:-1, :-1]
    vertical = padded[1:, 1:-1] - padded[:-1, 1:-1]
    columns = jnp.arange(NC + 1)
    row_index = jnp.arange(NR + 1)
    horiz = jnp.where(((columns >= 1) & (columns <= NC - 1))[None, :], jnp.exp(-across * across), 0.0)
    verti = jnp.where(((row_index >= 1) & (row_index <= NR - 1))[:, None], jnp.exp(-vertical * vertical), 0.0)
    return (horiz, verti)

def apply_operator(field, coeff, horiz, verti):
    padded = jnp.pad(field, 1)
    edges = horiz[:, 1:] * (field - padded[1:-1, 2:]) + horiz[:, :-1] * (field - padded[1:-1, :-2])
    edges = edges + verti[1:] * (field - padded[2:, 1:-1]) + verti[:-1] * (field - padded[:-2, 1:-1])
    return coeff * field + smooth_weight * edges

def reference(views):
    padded = jnp.pad(views, ((0, 0), (HALO, HALO), (HALO, HALO)))
    center = views[VIEWS // 2].astype(jnp.float32)
    data_sum = jnp.zeros((NR, NC), jnp.float32)
    source_sum = jnp.zeros((NR, NC), jnp.float32)
    for index in range(VIEWS):
        srow = index // ANG - ANG // 2
        tcol = index % ANG - ANG // 2
        top = HALO + D0 * srow
        left = HALO + D0 * tcol
        image = padded[index].astype(jnp.float32)
        warped = image[top:top + NR, left:left + NC]
        down_diff = 0.5 * (image[top + 1:top + 1 + NR, left:left + NC] - image[top - 1:top - 1 + NR, left:left + NC])
        side_diff = 0.5 * (image[top:top + NR, left + 1:left + 1 + NC] - image[top:top + NR, left - 1:left - 1 + NC])
        slope = srow * down_diff + tcol * side_diff
        error = warped - center
        robust = 1.0 / jnp.sqrt(1.0 + error * error)
        data_sum = data_sum + robust * slope * slope
        source_sum = source_sum - robust * slope * error
    coeff = damping + data_sum / VIEWS
    source = source_sum / VIEWS
    horiz, verti = edge_weights(center)
    precond = coeff + smooth_weight * (horiz[:, 1:] + horiz[:, :-1] + verti[1:] + verti[:-1])
    solution = jnp.zeros_like(source)
    residual = source
    zed = residual / precond
    direction = zed
    inner_now = jnp.sum(residual * zed)
    for step in range(ITERS):
        image_dir = apply_operator(direction, coeff, horiz, verti)
        step_size = inner_now / jnp.sum(direction * image_dir)
        solution = solution + step_size * direction
        residual = residual - step_size * image_dir
        zed = residual / precond
        inner_next = jnp.sum(residual * zed)
        direction = zed + inner_next / inner_now * direction
        inner_now = inner_next
    return (solution, residual)
```

```python
import functools

import jax
import jax.numpy as jnp
import ml_dtypes
import numpy as np
from jax import lax
from jax.experimental import pallas as pl
from jax.experimental.pallas import tpu as pltpu
from jax.sharding import PartitionSpec as P

ANG = 9
VIEWS = 81
HALF = ANG // 2
D0 = 3
ROWS = 64
COLS = 256
EDGE = 16
OUT = 72
SLAB = 96
PACKED = ANG * ROWS + 10 * EDGE
LANES = 128
SMOOTH = 2.0
DAMPING = 0.1
ALL = ("row", "col")
F32 = jnp.float32


def lane_first(t, c):
    return D0 * t * (t + 1) // 2 + c


def lane_last(t, c):
    a = abs(t)
    return 64 + D0 * a * (a + 1) // 2 + c - (COLS - D0 * a - D0)


def ghost_source(t, c):
    if c < 0:
        return lane_last(t, COLS + c)
    if c >= COLS:
        return 2 * LANES + lane_first(t, c - COLS)
    if t >= 0 and c <= D0 * t + D0 - 1:
        return LANES + lane_first(t, c)
    return LANES + lane_last(t, c)


def tables():
    pack = np.zeros((ANG, COLS, LANES), np.float32)
    for t in range(-HALF, HALF + 1):
        if t >= 0:
            for c in range(D0 * t + D0):
                pack[t + HALF, c, lane_first(t, c)] = 1
        if t <= 0:
            for c in range(COLS - D0 * abs(t) - D0, COLS):
                pack[t + HALF, c, lane_last(t, c)] = 1
    inner = np.zeros((2, HALF, COLS, 2 * LANES), np.float32)
    outer = np.zeros((2, HALF, COLS, 2 * LANES), np.float32)
    for a in range(1, HALF + 1):
        for sign in (0, 1):
            t = a if sign else -a
            for j in range(LANES):
                for shift, out, value in ((0, 0, 1), (1, LANES, t), (-1, LANES, -t)):
                    c = j + D0 * t + shift
                    inner[sign, a - 1, c if sign else c + LANES, j + out] += value
                    if sign:
                        k = c if c < LANES else LANES + lane_first(t, c - LANES)
                    else:
                        k = LANES + c if c >= 0 else lane_last(t, COLS + c)
                    outer[sign, a - 1, k, j + out] += value
    ghost = np.zeros((3 * LANES, 2 * LANES), np.float32)
    center = np.zeros((3 * LANES, 2 * LANES), np.float32)
    for t in range(-HALF, HALF + 1):
        for g, col in enumerate((-2, -1, COLS, COLS + 1)):
            lane = (4 * (t + HALF) + g - 2) % LANES
            c = col + D0 * t
            ghost[ghost_source(t, c), lane] += 1
            if t:
                ghost[ghost_source(t, c + 1), LANES + lane] += t
                ghost[ghost_source(t, c - 1), LANES + lane] -= t
            center[ghost_source(0, col), lane] = 1
    for col in (-3, -2, -1, COLS, COLS + 1, COLS + 2):
        center[ghost_source(0, col), LANES + (col % (3 * LANES)) % LANES] = 1
    return tuple(x.astype(ml_dtypes.bfloat16) for x in (pack, inner, outer, ghost, center))


def dot(a, b):
    return jnp.dot(a, b, preferred_element_type=F32)


def pack_own(views, pack, out):
    for si in range(ANG):
        total = dot(views[si * ANG], pack[0])
        for ti in range(1, ANG):
            total = total + dot(views[si * ANG + ti], pack[ti])
        out[si * ROWS : (si + 1) * ROWS, :] = total.astype(jnp.bfloat16)


def pack_edges(above, below, pack, own, out):
    out[: ANG * ROWS, :] = own[...]
    for side, ref in enumerate((above, below)):
        for i in range(HALF + 1):
            total = dot(ref[i * ANG], pack[0])
            for ti in range(1, ANG):
                total = total + dot(ref[i * ANG + ti], pack[ti])
            at = ANG * ROWS + side * 5 * EDGE + i * EDGE
            out[at : at + EDGE, :] = total.astype(jnp.bfloat16)


def pieces(s):
    if s > 0:
        return (("own", 0), ("below", ROWS))
    if s < 0:
        return (("above", 0), ("own", EDGE))
    return (("above", 0), ("own", EDGE), ("below", EDGE + ROWS))


def first_row(s):
    return D0 * s - 2 if s > 0 else EDGE - 2 + D0 * s


def packed_rows(kind, s):
    if kind == "own":
        return (s + HALF) * ROWS, ROWS
    if kind == "above":
        return ANG * ROWS + (s + HALF) * EDGE, EDGE
    return ANG * ROWS + 5 * EDGE + s * EDGE, EDGE


def view_rows(kind, s, ti, views, above, below):
    if kind == "own":
        return views.at[(s + HALF) * ANG + ti]
    if kind == "above":
        return above.at[(s + HALF) * ANG + ti]
    return below.at[s * ANG + ti]


def accumulate(s, warped, side, center, data, source):
    at = first_row(s)
    value = warped[pl.ds(at, OUT), :]
    slope = float(s) * (warped[pl.ds(at + 1, OUT), :] - warped[pl.ds(at - 1, OUT), :])
    if side is not None:
        side_part = side[pl.ds(at, OUT), :]
        slope = slope + side_part if s else side_part
    error = value - center
    robust = lax.rsqrt(1.0 + error * error)
    weighted = robust * slope
    return data + weighted * slope, source + weighted * error


def fill(slab, at, array):
    slab[pl.ds(at, array.shape[0]), :] = array


def zero_tails(slabs):
    for i in range(ANG):
        slabs[i, pl.ds(SLAB - EDGE, EDGE), :] = jnp.zeros((EDGE, LANES), F32)


def shifted_views(ti, matrix, lhs, center, warped, side, data, source):
    for s in range(-HALF, HALF + 1):
        w, d = warped.at[s + HALF], side.at[s + HALF]
        for kind, at in pieces(s):
            both = dot(lhs(kind, s, ti), matrix)
            fill(w, at, both[:, :LANES])
            fill(d, at, both[:, LANES:])
        data, source = accumulate(s, w, d, center, data, source)
    return data, source


def inner_sums(views, above, below, inner, data_out, source_out, warped, side, center_ref):
    zero_tails(warped)
    zero_tails(side)
    zero = jnp.zeros((OUT, LANES), F32)
    for tile in (0, 1):
        lanes = slice(tile * LANES, (tile + 1) * LANES)
        for s in (0, -4, -3, -2, -1, 1, 2, 3, 4):
            for kind, at in pieces(s):
                ref = view_rows(kind, s, HALF, views, above, below)
                fill(warped.at[s + HALF], at, ref[:, lanes].astype(F32))
            if s == 0:
                center_ref[...] = warped[HALF, pl.ds(first_row(0), OUT), :]
                data = source = zero
            data, source = accumulate(
                s, warped.at[s + HALF], None, center_ref[...], data, source
            )
        data_out[tile] = data
        source_out[tile] = source
        sign = 1 - tile

        def body(a, carry, tile=tile, sign=sign):
            ti = HALF + 1 + a if sign else HALF - 1 - a
            data, source = shifted_views(
                ti,
                inner[sign, a],
                lambda kind, s, ti: view_rows(kind, s, ti, views, above, below)[...],
                center_ref[...],
                warped,
                side,
                zero,
                zero,
            )
            data_out[tile] += data
            source_out[tile] += source
            return carry

        lax.fori_loop(0, HALF, body, 0)


def outer_sums(
    total_rows,
    total_cols,
    views,
    above,
    below,
    own,
    left,
    right,
    data_in,
    source_in,
    outer,
    ghost,
    ghost_center,
    zed_out,
    near_out,
    next_out,
    precond_out,
    message,
    data_acc,
    source_acc,
    warped,
    side,
    center_ref,
    center_slab,
):
    zero_tails(warped)
    zero_tails(side)
    zero = jnp.zeros((OUT, LANES), F32)
    for kind, at in pieces(0):
        ref = view_rows(kind, 0, HALF, views, above, below)
        fill(center_slab.at[0], at, ref[:, :LANES].astype(F32))
        fill(center_slab.at[1], at, ref[:, LANES:].astype(F32))
        row, count = packed_rows(kind, 0)
        lhs = jnp.concatenate([x[pl.ds(row, count), :] for x in (left, own, right)], axis=1)
        both = dot(lhs, ghost_center[...])
        fill(warped.at[HALF], at, both[:, :LANES])
        fill(center_slab.at[2], at, both[:, LANES:])
    for tile in (0, 1):
        data_acc[tile] = data_in[tile]
        source_acc[tile] = source_in[tile]
    center_ref[...] = warped[HALF, pl.ds(first_row(0), OUT), :]
    data = source = zero
    for s in range(-HALF, HALF + 1):
        w, d = warped.at[s + HALF], side.at[s + HALF]
        for kind, at in pieces(s):
            row, count = packed_rows(kind, s)
            lhs = jnp.concatenate([x[pl.ds(row, count), :] for x in (left, own, right)], axis=1)
            both = dot(lhs, ghost[...])
            fill(w, at, both[:, :LANES])
            fill(d, at, both[:, LANES:])
        data, source = accumulate(s, w, d, center_ref[...], data, source)
    for step in (4, 8, 16, 32):
        data = data + pltpu.roll(data, LANES - step, 1)
        source = source + pltpu.roll(source, LANES - step, 1)
    data_acc[2] = data
    source_acc[2] = source
    for tile in (0, 1):
        sign = tile
        center_ref[...] = center_slab[tile, pl.ds(first_row(0), OUT), :]

        def lhs_of(kind, s, ti, sign=sign):
            ref = view_rows(kind, s, ti, views, above, below)
            row, count = packed_rows(kind, s)
            if sign:
                return jnp.concatenate([ref[:, LANES:], right[pl.ds(row, count), :]], axis=1)
            return jnp.concatenate([left[pl.ds(row, count), :], ref[:, :LANES]], axis=1)

        def body(a, carry, tile=tile, sign=sign, lhs_of=lhs_of):
            ti = HALF + 1 + a if sign else HALF - 1 - a
            data, source = shifted_views(
                ti, outer[sign, a], lhs_of, center_ref[...], warped, side, zero, zero
            )
            data_acc[tile] += data
            source_acc[tile] += source
            return carry

        lax.fori_loop(0, HALF, body, 0)

    def joined(ref):
        return jnp.concatenate([ref[0], ref[1], ref[2]], axis=1)

    wide = 3 * LANES

    def before(x):
        return pltpu.roll(x, 1, 1)

    def after(x):
        return pltpu.roll(x, wide - 1, 1)

    def over(x):
        return pltpu.roll(x, 1, 0)

    def under(x):
        return pltpu.roll(x, OUT - 1, 0)

    at = first_row(0)
    here = jnp.concatenate([center_slab[i, pl.ds(at, OUT), :] for i in range(3)], axis=1)
    higher = jnp.concatenate([center_slab[i, pl.ds(at - 1, OUT), :] for i in range(3)], axis=1)
    lane = lax.broadcasted_iota(jnp.int32, (OUT, wide), 1)
    local_row = lax.broadcasted_iota(jnp.int32, (OUT, wide), 0) - 2
    column = jnp.where(lane < wide - 64, lane, lane - wide) + lax.axis_index("col") * COLS
    row = local_row + lax.axis_index("row") * ROWS
    across = here - before(here)
    vertical = here - higher
    h_left = jnp.where((column >= 1) & (column <= total_cols - 1), jnp.exp(-across * across), 0.0)
    v_up = jnp.where((row >= 1) & (row <= total_rows - 1), jnp.exp(-vertical * vertical), 0.0)
    h_right = after(h_left)
    v_down = under(v_up)
    coeff = DAMPING + joined(data_acc) * (0.25 / VIEWS)
    source = joined(source_acc) * (-0.5 / VIEWS)
    precond = coeff + SMOOTH * (h_left + h_right + v_up + v_down)
    inverse = 1.0 / precond

    def neighbours(x):
        total = h_left * before(x) + h_right * after(x) + v_up * over(x) + v_down * under(x)
        return SMOOTH * inverse * total

    zed = source * inverse
    near = neighbours(zed)
    nxt = neighbours(near)

    def block(x):
        return x[:, :COLS]

    zed, near, nxt, precond = block(zed), block(near), block(nxt), block(precond)
    zed_out[...] = zed
    near_out[...] = near
    next_out[...] = nxt
    precond_out[...] = precond
    mine = (block(local_row) >= 0) & (block(local_row) < ROWS)

    def inner(x, y):
        return jnp.sum(jnp.where(mine, precond * x * y, 0.0), keepdims=True)

    zz = inner(zed, zed)
    zn = inner(zed, near)
    kappa = jnp.clip(zn / jnp.where(zz > 0, zz, 1.0), -1.0, 1.0)
    y = near - kappa * zed
    g = nxt - kappa * near
    numbers = (
        (0, inner(y, y)),
        (1, inner(y, g)),
        (32, 2.0 * inner(y, zed)),
        (33, inner(y, near) + inner(zed, g)),
        (64, zz),
        (65, zn),
        (96, kappa),
        (97, kappa),
    )
    place = lax.broadcasted_iota(jnp.int32, (1, LANES), 1)
    out = jnp.zeros((1, LANES), F32)
    for where, number in numbers:
        out = jnp.where(place == where, number, out)
    message[...] = out


def finish(messages, zed_ref, near_ref, next_ref, precond_ref, increment, residual):
    all_of = messages[...]
    total = jnp.sum(all_of, axis=0, keepdims=True)
    zz = total[:, 64:65]
    zn = total[:, 65:66]
    kappa = zn / zz
    delta = pltpu.roll(all_of, 32, 1) - kappa
    linear = pltpu.roll(all_of, 96, 1)
    quad = pltpu.roll(all_of, 64, 1)
    moved = jnp.sum(all_of + delta * (linear + delta * quad), axis=0, keepdims=True)
    yy = moved[:, 0:1]
    yny = moved[:, 1:2]
    step0 = zz / (zz - zn)
    beta = step0 * step0 * yy / zz
    step1 = yy / (yy - yny - step0 * yy * yy / zz)
    rows = pl.ds(2, ROWS)
    zed = zed_ref[rows, :]
    near = near_ref[rows, :]
    nxt = next_ref[rows, :]
    y = near - kappa * zed
    g = nxt - kappa * near
    increment[...] = step0 * zed + step1 * (step0 * y + beta * zed)
    residual[...] = precond_ref[rows, :] * (
        step0 * y - step1 * (step0 * (y - g) + beta * (zed - near))
    )


def call(kernel, outs, scratch=(), name=None):
    return pl.pallas_call(
        kernel,
        out_shape=outs,
        scratch_shapes=list(scratch),
        compiler_params=pltpu.CompilerParams(vmem_limit_bytes=24 * 1024 * 1024),
        name=name,
    )


def shards(views):
    rows, cols = lax.axis_size("row"), lax.axis_size("col")
    pack, inner, outer, ghost, center = (jnp.asarray(x) for x in tables())
    bf16 = jnp.bfloat16
    struct = jax.ShapeDtypeStruct

    def towards(array, axis, step):
        n = lax.axis_size(axis)
        pairs = [(i, i + step) for i in range(n) if 0 <= i + step < n]
        return lax.ppermute(array, axis, pairs)

    below = towards(views[HALF * ANG :, :EDGE, :], "row", -1)
    above = towards(views[: (HALF + 1) * ANG, ROWS - EDGE :, :], "row", 1)
    own = call(pack_own, struct((ANG * ROWS, LANES), bf16), name="pack_own")(views, pack)
    own = call(pack_edges, struct((PACKED, LANES), bf16), name="pack_edges")(
        above, below, pack, own
    )
    left = towards(own, "col", 1)
    right = towards(own, "col", -1)
    slab = pltpu.VMEM((ANG, SLAB, LANES), F32)
    tile = pltpu.VMEM((OUT, LANES), F32)
    sums = struct((2, OUT, LANES), F32)
    data, source = call(inner_sums, (sums, sums), (slab, slab, tile), name="inner_sums")(
        views, above, below, inner
    )
    field = struct((OUT, COLS), F32)
    acc = pltpu.VMEM((3, OUT, LANES), F32)
    zed, near, nxt, precond, message = call(
        functools.partial(outer_sums, rows * ROWS, cols * COLS),
        (field, field, field, field, struct((1, LANES), F32)),
        (acc, acc, slab, slab, tile, pltpu.VMEM((3, SLAB, LANES), F32)),
        name="outer_sums",
    )(views, above, below, own, left, right, data, source, outer, ghost, center)
    n = rows * cols
    messages = lax.all_to_all(
        jnp.broadcast_to(message[None], (n, 1, LANES)), ALL, 0, 0, tiled=True
    ).reshape(n, LANES)
    block = struct((ROWS, COLS), F32)
    return call(finish, (block, block), name="finish")(messages, zed, near, nxt, precond)


def solution(mesh):
    return jax.shard_map(
        shards,
        mesh=mesh,
        in_specs=(P(None, "row", "col"),),
        out_specs=(P("row", "col"), P("row", "col")),
        check_vma=False,
    )
```

```python
import functools

import jax
import jax.numpy as jnp
import ml_dtypes
import numpy as np
from jax import lax
from jax.experimental import pallas as pl
from jax.experimental.pallas import tpu as pltpu
from jax.sharding import PartitionSpec as P

ANG = 9
VIEWS = 81
HALF = ANG // 2
D0 = 3
ROWS = 64
COLS = 256
EDGE = 16
OUT = 72
SLAB = 96
PIECES = 3
PACKED = ANG * ROWS + 2 * PIECES * EDGE
PAIRS = ((-4, -3), (-2, -1), (1, 2), (3, 4), (0, 0))
SENT = len(PAIRS) * ROWS + PIECES * EDGE
LANES = 128
SMOOTH = 2.0
DAMPING = 0.1
ALL = ("row", "col")
F32 = jnp.float32


def lane_first(t, c):
    return D0 * t * (t + 1) // 2 + c


def lane_last(t, c):
    a = abs(t)
    return 64 + D0 * a * (a + 1) // 2 + c - (COLS - D0 * a - D0)


def ghost_source(t, c):
    if c < 0:
        return lane_last(t, COLS + c)
    if c >= COLS:
        return 2 * LANES + lane_first(t, c - COLS)
    if t >= 0 and c <= D0 * t + D0 - 1:
        return LANES + lane_first(t, c)
    return LANES + lane_last(t, c)


def tables():
    inner = np.zeros((2, HALF, COLS, 2 * LANES), np.float32)
    outer = np.zeros((2, HALF, COLS, 2 * LANES), np.float32)
    for a in range(1, HALF + 1):
        for sign in (0, 1):
            t = a if sign else -a
            for j in range(LANES):
                for shift, out, value in ((0, 0, 1), (1, LANES, t), (-1, LANES, -t)):
                    c = j + D0 * t + shift
                    inner[sign, a - 1, c if sign else c + LANES, j + out] += value
                    if sign:
                        k = c if c < LANES else LANES + lane_first(t, c - LANES)
                    else:
                        k = LANES + c if c >= 0 else lane_last(t, COLS + c)
                    outer[sign, a - 1, k, j + out] += value
    ghost = np.zeros((3 * LANES, 2 * LANES), np.float32)
    center = np.zeros((3 * LANES, 2 * LANES), np.float32)
    for t in range(-HALF, HALF + 1):
        for g, col in enumerate((-2, -1, COLS, COLS + 1)):
            lane = (4 * (t + HALF) + g - 2) % LANES
            c = col + D0 * t
            ghost[ghost_source(t, c), lane] += 1
            if t:
                ghost[ghost_source(t, c + 1), LANES + lane] += t
                ghost[ghost_source(t, c - 1), LANES + lane] -= t
            center[ghost_source(0, col), lane] = 1
    for col in (-3, -2, -1, COLS, COLS + 1, COLS + 2):
        center[ghost_source(0, col), LANES + (col % (3 * LANES)) % LANES] = 1
    return tuple(x.astype(ml_dtypes.bfloat16) for x in (inner, outer, ghost, center))


def dot(a, b):
    return jnp.dot(a, b, preferred_element_type=F32)


def is_even(axis):
    return lax.rem(lax.axis_index(axis), 2) == 0


def pack_rows(views, send_pair, send_next, local, sems):
    order = (4, 3, 0, 2, 1, -4, -3, -2, -1)
    copies = {}
    for s in order:
        span = pl.ds((s + HALF) * ANG, ANG)
        copies[s] = pltpu.make_async_copy(
            views.at[span], local.at[span], sems.at[s + HALF]
        )
        copies[s].start()
    even = is_even("row")
    index = lax.broadcasted_iota(jnp.int32, (EDGE, COLS), 0)

    def put(ups, q, ti, rows):
        rows = rows.astype(jnp.bfloat16)

        @pl.when(even == ups)
        def _():
            send_next[q * ANG + ti] = rows

        @pl.when(even != ups)
        def _():
            send_pair[q * ANG + ti] = rows

    for s in order:
        copies[s].wait()
        if s in (3, 2, -4):
            continue
        for ti in range(ANG):

            def rows_of(s, start):
                return local[(s + HALF) * ANG + ti, pl.ds(start, EDGE), :].astype(F32)

            first = functools.partial(rows_of, start=0)
            last = functools.partial(rows_of, start=ROWS - EDGE)
            if s == 4:
                put(True, 0, ti, first(4))
            elif s == 0:
                put(True, 1, ti, jnp.where(index < 12, first(3), pltpu.roll(first(0), 12, 0)))
            elif s == 1:
                put(True, 2, ti, jnp.where(index < 9, first(2), pltpu.roll(first(1), 9, 0)))
            elif s == -3:
                put(False, 0, ti, last(-4))
                put(False, 1, ti, jnp.where(index < 4, pltpu.roll(last(0), 4, 0), last(-3)))
            elif s == -1:
                put(False, 2, ti, jnp.where(index < 7, pltpu.roll(last(-1), 7, 0), last(-2)))


PLACES = {
    ("above", 0): ((-4, 0),),
    ("above", 1): ((-3, 0), (0, 12)),
    ("above", 2): ((-2, 0), (-1, 9)),
    ("below", 0): ((4, ROWS),),
    ("below", 1): ((3, ROWS), (0, EDGE + ROWS - 12)),
    ("below", 2): ((2, ROWS), (1, ROWS - 9)),
}


def packed_piece(side, q):
    return ANG * ROWS + ((0 if side == "above" else PIECES) + q) * EDGE


def share(first_of, second_of, to_left, to_right, at):
    low = lax.broadcasted_iota(jnp.int32, first_of.shape, 1) < 64
    turned = pltpu.roll(second_of, 64, 1)
    to_left[pl.ds(at, first_of.shape[0]), :] = jnp.where(low, first_of, turned).astype(
        jnp.bfloat16
    )
    turned = pltpu.roll(first_of, 64, 1)
    to_right[pl.ds(at, first_of.shape[0]), :] = jnp.where(low, turned, second_of).astype(
        jnp.bfloat16
    )


def pack_own(views, own, to_left, to_right, pack):
    column = lax.broadcasted_iota(jnp.int32, (COLS, LANES), 0)
    lane = lax.broadcasted_iota(jnp.int32, (COLS, LANES), 1)
    for t in range(-HALF, HALF + 1):
        hit = jnp.zeros((COLS, LANES), F32)
        if t >= 0:
            bound = D0 * t + D0
            hit = jnp.where((column < bound) & (lane - column == lane_first(t, 0)), 1.0, hit)
        if t <= 0:
            start = COLS - D0 * abs(t) - D0
            apart = lane_last(t, start) - start
            hit = jnp.where((column >= start) & (lane - column == apart), 1.0, hit)
        pack[t + HALF] = hit.astype(jnp.bfloat16)
    for p, pair in enumerate(PAIRS):
        both = []
        for s in pair:
            total = dot(views[(s + HALF) * ANG], pack[0])
            for ti in range(1, ANG):
                total = total + dot(views[(s + HALF) * ANG + ti], pack[ti])
            own[(s + HALF) * ROWS : (s + HALF + 1) * ROWS, :] = total.astype(jnp.bfloat16)
            both.append(total)
        share(both[0], both[1], to_left, to_right, p * ROWS)


def pack_edges(
    got_pair, got_next, pack, own_in, left_in, right_in,
    above, below, own, send_pair, send_next, to_left, to_right,
):
    even = is_even("row")

    @pl.when(even)
    def _():
        below[...] = got_pair[...]
        above[...] = got_next[...]

    @pl.when(jnp.logical_not(even))
    def _():
        below[...] = got_next[...]
        above[...] = got_pair[...]

    own[: ANG * ROWS, :] = own_in[...]
    for q in range(PIECES):
        both = []
        for side, ref in (("above", above), ("below", below)):
            total = dot(ref[q * ANG], pack[0])
            for ti in range(1, ANG):
                total = total + dot(ref[q * ANG + ti], pack[ti])
            own[pl.ds(packed_piece(side, q), EDGE), :] = total.astype(jnp.bfloat16)
            both.append(total)
        share(both[0], both[1], to_left, to_right, q * EDGE)
    rows = len(PAIRS) * ROWS
    even = is_even("col")

    def send(out, block, piece):
        out[:rows, :] = block[...]
        out[rows:, :] = piece[...]

    @pl.when(even)
    def _():
        send(send_pair, right_in, to_right)
        send(send_next, left_in, to_left)

    @pl.when(jnp.logical_not(even))
    def _():
        send(send_pair, left_in, to_left)
        send(send_next, right_in, to_right)


def unshare(source, high, out):
    def move(at, to, count, half):
        rows = source[pl.ds(at, count), :]
        if half != high:
            rows = pltpu.roll(rows.astype(F32), 64, 1).astype(jnp.bfloat16)
        out[pl.ds(to, count), :] = rows

    for p, pair in enumerate(PAIRS):
        for half, s in enumerate(pair):
            if s or not half:
                move(p * ROWS, (s + HALF) * ROWS, ROWS, half)
    for q in range(PIECES):
        for half, side in enumerate(("above", "below")):
            move(len(PAIRS) * ROWS + q * EDGE, packed_piece(side, q), EDGE, half)


def first_row(s):
    return D0 * s - 2 if s > 0 else EDGE - 2 + D0 * s


def own_row(s):
    return 0 if s > 0 else EDGE


def accumulate(s, warped, side, center, data, source):
    at = first_row(s)
    value = warped[pl.ds(at, OUT), :]
    slope = float(s) * (warped[pl.ds(at + 1, OUT), :] - warped[pl.ds(at - 1, OUT), :])
    if side is not None:
        side_part = side[pl.ds(at, OUT), :]
        slope = slope + side_part if s else side_part
    error = value - center
    robust = lax.rsqrt(1.0 + error * error)
    weighted = robust * slope
    return data + weighted * slope, source + weighted * error


def fill(slab, at, array):
    slab[pl.ds(at, array.shape[0]), :] = array


def zero_tails(slabs):
    for i in range(ANG):
        slabs[i, pl.ds(ROWS, SLAB - ROWS), :] = jnp.zeros((SLAB - ROWS, LANES), F32)


def fill_pieces(parts_of, outs):
    for (side, q), places in PLACES.items():
        parts = parts_of(side, q)
        for s, at in places:
            for out, part in zip(outs, parts):
                fill(out.at[s + HALF], at, part)


def halves(both):
    return both[:, :LANES], both[:, LANES:]


def shifted_views(matrix, own, piece, center, warped, side, data, source):
    fill_pieces(lambda name, q: halves(dot(piece(name, q), matrix)), (warped, side))
    for s in range(-HALF, HALF + 1):
        w, d = warped.at[s + HALF], side.at[s + HALF]
        both = dot(own(s), matrix)
        fill(w, own_row(s), both[:, :LANES])
        fill(d, own_row(s), both[:, LANES:])
        data, source = accumulate(s, w, d, center, data, source)
    return data, source


def inner_sums(views, above, below, inner, data_out, source_out, warped, side, center_ref):
    zero_tails(warped)
    zero_tails(side)
    zero = jnp.zeros((OUT, LANES), F32)
    edges = {"above": above, "below": below}
    for tile in (0, 1):
        lanes = slice(tile * LANES, (tile + 1) * LANES)
        fill_pieces(
            lambda name, q: (edges[name][q * ANG + HALF][:, lanes].astype(F32),), (warped,)
        )
        data = source = zero
        for s in (0, -4, -3, -2, -1, 1, 2, 3, 4):
            w = warped.at[s + HALF]
            fill(w, own_row(s), views[(s + HALF) * ANG + HALF][:, lanes].astype(F32))
            if s == 0:
                center_ref[...] = w[pl.ds(first_row(0), OUT), :]
            data, source = accumulate(s, w, None, center_ref[...], data, source)
        data_out[tile] = data
        source_out[tile] = source
        sign = 1 - tile

        def body(a, carry, tile=tile, sign=sign):
            ti = HALF + 1 + a if sign else HALF - 1 - a
            data, source = shifted_views(
                inner[sign, a],
                lambda s: views[(s + HALF) * ANG + ti],
                lambda name, q: edges[name][q * ANG + ti],
                center_ref[...],
                warped,
                side,
                zero,
                zero,
            )
            data_out[tile] += data
            source_out[tile] += source
            return carry

        lax.fori_loop(0, HALF, body, 0)


def outer_sums(
    total_rows,
    total_cols,
    views,
    above,
    below,
    own,
    got_pair,
    got_next,
    data_in,
    source_in,
    outer,
    ghost,
    ghost_center,
    zed_out,
    near_out,
    next_out,
    precond_out,
    message,
    data_acc,
    source_acc,
    warped,
    side,
    center_ref,
    center_slab,
    left,
    right,
):
    even = is_even("col")

    @pl.when(even)
    def _():
        unshare(got_next, 1, left)
        unshare(got_pair, 0, right)

    @pl.when(jnp.logical_not(even))
    def _():
        unshare(got_pair, 1, left)
        unshare(got_next, 0, right)

    edges = {"above": above, "below": below}
    zero_tails(warped)
    zero_tails(side)
    zero = jnp.zeros((OUT, LANES), F32)

    def ghost_rows(row, count):
        return jnp.concatenate([x[pl.ds(row, count), :] for x in (left, own, right)], axis=1)

    def fill_center(at, ref, row, count):
        fill(center_slab.at[0], at, ref[:, :LANES].astype(F32))
        fill(center_slab.at[1], at, ref[:, LANES:].astype(F32))
        both = dot(ghost_rows(row, count), ghost_center[...])
        fill(warped.at[HALF], at, both[:, :LANES])
        fill(center_slab.at[2], at, both[:, LANES:])

    for name in ("above", "below"):
        fill_center(PLACES[name, 1][1][1], edges[name][ANG + HALF], packed_piece(name, 1), EDGE)
    fill_center(EDGE, views[HALF * ANG + HALF], HALF * ROWS, ROWS)
    for tile in (0, 1):
        data_acc[tile] = data_in[tile]
        source_acc[tile] = source_in[tile]
    center_ref[...] = warped[HALF, pl.ds(first_row(0), OUT), :]
    data, source = shifted_views(
        ghost[...],
        lambda s: ghost_rows((s + HALF) * ROWS, ROWS),
        lambda name, q: ghost_rows(packed_piece(name, q), EDGE),
        center_ref[...],
        warped,
        side,
        zero,
        zero,
    )
    for step in (4, 8, 16, 32):
        data = data + pltpu.roll(data, LANES - step, 1)
        source = source + pltpu.roll(source, LANES - step, 1)
    data_acc[2] = data
    source_acc[2] = source
    for tile in (0, 1):
        sign = tile
        center_ref[...] = center_slab[tile, pl.ds(first_row(0), OUT), :]

        def lhs(ref, row, sign=sign):
            count = ref.shape[0]
            if sign:
                return jnp.concatenate([ref[:, LANES:], right[pl.ds(row, count), :]], axis=1)
            return jnp.concatenate([left[pl.ds(row, count), :], ref[:, :LANES]], axis=1)

        def body(a, carry, tile=tile, sign=sign, lhs=lhs):
            ti = HALF + 1 + a if sign else HALF - 1 - a
            data, source = shifted_views(
                outer[sign, a],
                lambda s: lhs(views.at[(s + HALF) * ANG + ti], (s + HALF) * ROWS),
                lambda name, q: lhs(edges[name].at[q * ANG + ti], packed_piece(name, q)),
                center_ref[...],
                warped,
                side,
                zero,
                zero,
            )
            data_acc[tile] += data
            source_acc[tile] += source
            return carry

        lax.fori_loop(0, HALF, body, 0)

    def joined(ref):
        return jnp.concatenate([ref[0], ref[1], ref[2]], axis=1)

    wide = 3 * LANES

    def before(x):
        return pltpu.roll(x, 1, 1)

    def after(x):
        return pltpu.roll(x, wide - 1, 1)

    def over(x):
        return pltpu.roll(x, 1, 0)

    def under(x):
        return pltpu.roll(x, OUT - 1, 0)

    at = first_row(0)
    here = jnp.concatenate([center_slab[i, pl.ds(at, OUT), :] for i in range(3)], axis=1)
    higher = jnp.concatenate([center_slab[i, pl.ds(at - 1, OUT), :] for i in range(3)], axis=1)
    lane = lax.broadcasted_iota(jnp.int32, (OUT, wide), 1)
    local_row = lax.broadcasted_iota(jnp.int32, (OUT, wide), 0) - 2
    column = jnp.where(lane < wide - 64, lane, lane - wide) + lax.axis_index("col") * COLS
    row = local_row + lax.axis_index("row") * ROWS
    across = here - before(here)
    vertical = here - higher
    h_left = jnp.where((column >= 1) & (column <= total_cols - 1), jnp.exp(-across * across), 0.0)
    v_up = jnp.where((row >= 1) & (row <= total_rows - 1), jnp.exp(-vertical * vertical), 0.0)
    h_right = after(h_left)
    v_down = under(v_up)
    coeff = DAMPING + joined(data_acc) * (0.25 / VIEWS)
    source = joined(source_acc) * (-0.5 / VIEWS)
    precond = coeff + SMOOTH * (h_left + h_right + v_up + v_down)
    inverse = 1.0 / precond

    def neighbours(x):
        total = h_left * before(x) + h_right * after(x) + v_up * over(x) + v_down * under(x)
        return SMOOTH * inverse * total

    zed = source * inverse
    near = neighbours(zed)
    nxt = neighbours(near)

    def block(x):
        return x[:, :COLS]

    zed, near, nxt, precond = block(zed), block(near), block(nxt), block(precond)
    zed_out[...] = zed
    near_out[...] = near
    next_out[...] = nxt
    precond_out[...] = precond
    mine = (block(local_row) >= 0) & (block(local_row) < ROWS)

    def inner(x, y):
        return jnp.sum(jnp.where(mine, precond * x * y, 0.0), keepdims=True)

    zz = inner(zed, zed)
    zn = inner(zed, near)
    kappa = jnp.clip(zn / jnp.where(zz > 0, zz, 1.0), -1.0, 1.0)
    y = near - kappa * zed
    g = nxt - kappa * near
    numbers = (
        (0, inner(y, y)),
        (1, inner(y, g)),
        (32, 2.0 * inner(y, zed)),
        (33, inner(y, near) + inner(zed, g)),
        (64, zz),
        (65, zn),
        (96, kappa),
        (97, kappa),
    )
    place = lax.broadcasted_iota(jnp.int32, (1, LANES), 1)
    out = jnp.zeros((1, LANES), F32)
    for where, number in numbers:
        out = jnp.where(place == where, number, out)
    message[...] = out


def finish(messages, zed_ref, near_ref, next_ref, precond_ref, increment, residual):
    all_of = messages[...]
    total = jnp.sum(all_of, axis=0, keepdims=True)
    zz = total[:, 64:65]
    zn = total[:, 65:66]
    kappa = zn / zz
    delta = pltpu.roll(all_of, 32, 1) - kappa
    linear = pltpu.roll(all_of, 96, 1)
    quad = pltpu.roll(all_of, 64, 1)
    moved = jnp.sum(all_of + delta * (linear + delta * quad), axis=0, keepdims=True)
    yy = moved[:, 0:1]
    yny = moved[:, 1:2]
    step0 = zz / (zz - zn)
    beta = step0 * step0 * yy / zz
    step1 = yy / (yy - yny - step0 * yy * yy / zz)
    rows = pl.ds(2, ROWS)
    zed = zed_ref[rows, :]
    near = near_ref[rows, :]
    nxt = next_ref[rows, :]
    y = near - kappa * zed
    g = nxt - kappa * near
    increment[...] = step0 * zed + step1 * (step0 * y + beta * zed)
    residual[...] = precond_ref[rows, :] * (
        step0 * y - step1 * (step0 * (y - g) + beta * (zed - near))
    )


def call(kernel, outs, scratch=(), name=None, **more):
    return pl.pallas_call(
        kernel,
        out_shape=outs,
        scratch_shapes=list(scratch),
        compiler_params=pltpu.CompilerParams(vmem_limit_bytes=24 * 1024 * 1024),
        name=name,
        **more,
    )


def swap(array, axis, start):
    pairs = []
    for i in range(start, lax.axis_size(axis) - 1, 2):
        pairs += [(i, i + 1), (i + 1, i)]
    return lax.ppermute(array, axis, pairs)


def shards(views):
    rows, cols = lax.axis_size("row"), lax.axis_size("col")
    inner, outer, ghost, center = (jnp.asarray(x) for x in tables())
    bf16 = jnp.bfloat16
    struct = jax.ShapeDtypeStruct

    edge = struct((PIECES * ANG, EDGE, COLS), bf16)
    pair, after, views = call(
        pack_rows,
        (edge, edge, struct(views.shape, bf16)),
        (pltpu.SemaphoreType.DMA((ANG,)),),
        name="pack_rows",
        in_specs=[pl.BlockSpec(memory_space=pltpu.HBM)],
    )(views)
    pair = swap(pair, "row", 0)
    after = swap(after, "row", 1)
    shared = struct((len(PAIRS) * ROWS, LANES), bf16)
    own, to_left, to_right, pack = call(
        pack_own,
        (struct((ANG * ROWS, LANES), bf16), shared, shared, struct((ANG, COLS, LANES), bf16)),
        name="pack_own",
    )(views)
    sent = struct((SENT, LANES), bf16)
    small = pltpu.VMEM((PIECES * EDGE, LANES), bf16)
    above, below, own, pair, after = call(
        pack_edges,
        (edge, edge, struct((PACKED, LANES), bf16), sent, sent),
        (small, small),
        name="pack_edges",
    )(pair, after, pack, own, to_left, to_right)
    pair = swap(pair, "col", 0)
    after = swap(after, "col", 1)
    slab = pltpu.VMEM((ANG, SLAB, LANES), F32)
    tile = pltpu.VMEM((OUT, LANES), F32)
    sums = struct((2, OUT, LANES), F32)
    data, source = call(inner_sums, (sums, sums), (slab, slab, tile), name="inner_sums")(
        views, above, below, inner
    )
    field = struct((OUT, COLS), F32)
    acc = pltpu.VMEM((3, OUT, LANES), F32)
    zed, near, nxt, precond, message = call(
        functools.partial(outer_sums, rows * ROWS, cols * COLS),
        (field, field, field, field, struct((1, LANES), F32)),
        (
            acc,
            acc,
            slab,
            slab,
            tile,
            pltpu.VMEM((3, SLAB, LANES), F32),
            pltpu.VMEM((PACKED, LANES), bf16),
            pltpu.VMEM((PACKED, LANES), bf16),
        ),
        name="outer_sums",
    )(views, above, below, own, pair, after, data, source, outer, ghost, center)
    n = rows * cols
    messages = lax.all_to_all(
        jnp.broadcast_to(message[None], (n, 1, LANES)), ALL, 0, 0, tiled=True
    ).reshape(n, LANES)
    block = struct((ROWS, COLS), F32)
    return call(finish, (block, block), name="finish")(messages, zed, near, nxt, precond)


def solution(mesh):
    return jax.shard_map(
        shards,
        mesh=mesh,
        in_specs=(P(None, "row", "col"),),
        out_specs=(P("row", "col"), P("row", "col")),
        check_vma=False,
    )
```

```python
import functools

import jax
import jax.numpy as jnp
import ml_dtypes
import numpy as np
from jax import lax
from jax.experimental import pallas as pl
from jax.experimental.pallas import tpu as pltpu
from jax.sharding import PartitionSpec as P

ANG = 9
VIEWS = 81
HALF = ANG // 2
D0 = 3
ROWS = 64
COLS = 256
EDGE = 16
OUT = 72
SLAB = 96
PIECES = 3
PACKED = ANG * ROWS + 2 * PIECES * EDGE
PAIRS = ((-4, -3), (-2, -1), (1, 2), (3, 4), (0, 0))
SHARED = len(PAIRS) * ROWS
LANES = 128
SMOOTH = 2.0
DAMPING = 0.1
ALL = ("row", "col")
F32 = jnp.float32


def lane_first(t, c):
    return D0 * t * (t + 1) // 2 + c


def lane_last(t, c):
    a = abs(t)
    return 64 + D0 * a * (a + 1) // 2 + c - (COLS - D0 * a - D0)


def ghost_source(t, c):
    if c < 0:
        return lane_last(t, COLS + c)
    if c >= COLS:
        return 2 * LANES + lane_first(t, c - COLS)
    if t >= 0 and c <= D0 * t + D0 - 1:
        return LANES + lane_first(t, c)
    return LANES + lane_last(t, c)


def tables():
    inner = np.zeros((2, HALF, COLS, 2 * LANES), np.float32)
    outer = np.zeros((2, HALF, COLS, 2 * LANES), np.float32)
    for a in range(1, HALF + 1):
        for sign in (0, 1):
            t = a if sign else -a
            for j in range(LANES):
                for shift, out, value in ((0, 0, 1), (1, LANES, t), (-1, LANES, -t)):
                    c = j + D0 * t + shift
                    inner[sign, a - 1, c if sign else c + LANES, j + out] += value
                    if sign:
                        k = c if c < LANES else LANES + lane_first(t, c - LANES)
                    else:
                        k = LANES + c if c >= 0 else lane_last(t, COLS + c)
                    outer[sign, a - 1, k, j + out] += value
    ghost = np.zeros((3 * LANES, 2 * LANES), np.float32)
    center = np.zeros((3 * LANES, 2 * LANES), np.float32)
    for t in range(-HALF, HALF + 1):
        for g, col in enumerate((-2, -1, COLS, COLS + 1)):
            lane = (4 * (t + HALF) + g - 2) % LANES
            c = col + D0 * t
            ghost[ghost_source(t, c), lane] += 1
            if t:
                ghost[ghost_source(t, c + 1), LANES + lane] += t
                ghost[ghost_source(t, c - 1), LANES + lane] -= t
            center[ghost_source(0, col), lane] = 1
    for col in (-3, -2, -1, COLS, COLS + 1, COLS + 2):
        center[ghost_source(0, col), LANES + (col % (3 * LANES)) % LANES] = 1
    return tuple(x.astype(ml_dtypes.bfloat16) for x in (inner, outer, ghost, center))


def dot(a, b):
    return jnp.dot(a, b, preferred_element_type=F32)


def is_even(axis):
    return lax.rem(lax.axis_index(axis), 2) == 0


def pack_rows(views, send_pair, send_next, ups_out, downs_out):
    even = is_even("row")
    index = lax.broadcasted_iota(jnp.int32, (EDGE, COLS), 0)

    def put(ups, q, ti, rows):
        (ups_out if ups else downs_out)[q * ANG + ti] = rows.astype(jnp.bfloat16)

    for ti in range(ANG):

        def rows_of(s, start, ti=ti):
            return views[(s + HALF) * ANG + ti, pl.ds(start, EDGE), :].astype(F32)

        first = functools.partial(rows_of, start=0)
        last = functools.partial(rows_of, start=ROWS - EDGE)
        put(True, 0, ti, first(4))
        put(True, 1, ti, jnp.where(index < 12, first(3), pltpu.roll(first(0), 12, 0)))
        put(True, 2, ti, jnp.where(index < 9, first(2), pltpu.roll(first(1), 9, 0)))
        put(False, 0, ti, last(-4))
        put(False, 1, ti, jnp.where(index < 4, pltpu.roll(last(0), 4, 0), last(-3)))
        put(False, 2, ti, jnp.where(index < 7, pltpu.roll(last(-1), 7, 0), last(-2)))

    @pl.when(even)
    def _():
        send_pair[...] = downs_out[...]
        send_next[...] = ups_out[...]

    @pl.when(jnp.logical_not(even))
    def _():
        send_pair[...] = ups_out[...]
        send_next[...] = downs_out[...]


PLACES = {
    ("above", 0): ((-4, 0),),
    ("above", 1): ((-3, 0), (0, 12)),
    ("above", 2): ((-2, 0), (-1, 9)),
    ("below", 0): ((4, ROWS),),
    ("below", 1): ((3, ROWS), (0, EDGE + ROWS - 12)),
    ("below", 2): ((2, ROWS), (1, ROWS - 9)),
}


def packed_piece(side, q):
    return ANG * ROWS + ((0 if side == "above" else PIECES) + q) * EDGE


def share(first_of, second_of, to_left, to_right, at):
    low = lax.broadcasted_iota(jnp.int32, first_of.shape, 1) < 64
    turned = pltpu.roll(second_of, 64, 1)
    to_left[pl.ds(at, first_of.shape[0]), :] = jnp.where(low, first_of, turned).astype(
        jnp.bfloat16
    )
    turned = pltpu.roll(first_of, 64, 1)
    to_right[pl.ds(at, first_of.shape[0]), :] = jnp.where(low, turned, second_of).astype(
        jnp.bfloat16
    )


def by_pair(to_left, to_right, send_pair, send_next):
    even = is_even("col")

    @pl.when(even)
    def _():
        send_pair[...] = to_right[...]
        send_next[...] = to_left[...]

    @pl.when(jnp.logical_not(even))
    def _():
        send_pair[...] = to_left[...]
        send_next[...] = to_right[...]


def pack_own(views, own, send_pair, send_next, pack, to_left, to_right):
    column = lax.broadcasted_iota(jnp.int32, (COLS, LANES), 0)
    lane = lax.broadcasted_iota(jnp.int32, (COLS, LANES), 1)
    for t in range(-HALF, HALF + 1):
        hit = jnp.zeros((COLS, LANES), F32)
        if t >= 0:
            bound = D0 * t + D0
            hit = jnp.where((column < bound) & (lane - column == lane_first(t, 0)), 1.0, hit)
        if t <= 0:
            start = COLS - D0 * abs(t) - D0
            apart = lane_last(t, start) - start
            hit = jnp.where((column >= start) & (lane - column == apart), 1.0, hit)
        pack[t + HALF] = hit.astype(jnp.bfloat16)
    for p, pair in enumerate(PAIRS):
        both = []
        for s in pair:
            total = dot(views[(s + HALF) * ANG], pack[0])
            for ti in range(1, ANG):
                total = total + dot(views[(s + HALF) * ANG + ti], pack[ti])
            own[(s + HALF) * ROWS : (s + HALF + 1) * ROWS, :] = total.astype(jnp.bfloat16)
            both.append(total)
        share(both[0], both[1], to_left, to_right, p * ROWS)
    by_pair(to_left, to_right, send_pair, send_next)


def pack_edges(
    got_pair, got_next, pack, own_in, above, below, own, send_pair, send_next,
    to_left, to_right,
):
    even = is_even("row")

    @pl.when(even)
    def _():
        below[...] = got_pair[...]
        above[...] = got_next[...]

    @pl.when(jnp.logical_not(even))
    def _():
        below[...] = got_next[...]
        above[...] = got_pair[...]

    own[: ANG * ROWS, :] = own_in[...]
    for q in range(PIECES):
        both = []
        for side, ref in (("above", above), ("below", below)):
            total = dot(ref[q * ANG], pack[0])
            for ti in range(1, ANG):
                total = total + dot(ref[q * ANG + ti], pack[ti])
            own[pl.ds(packed_piece(side, q), EDGE), :] = total.astype(jnp.bfloat16)
            both.append(total)
        share(both[0], both[1], to_left, to_right, q * EDGE)
    by_pair(to_left, to_right, send_pair, send_next)


def unshare(blocks, pieces, high, out):
    def move(source, at, to, count, half):
        rows = source[pl.ds(at, count), :]
        if half != high:
            rows = pltpu.roll(rows.astype(F32), 64, 1).astype(jnp.bfloat16)
        out[pl.ds(to, count), :] = rows

    for p, pair in enumerate(PAIRS):
        for half, s in enumerate(pair):
            if s or not half:
                move(blocks, p * ROWS, (s + HALF) * ROWS, ROWS, half)
    for q in range(PIECES):
        for half, side in enumerate(("above", "below")):
            move(pieces, q * EDGE, packed_piece(side, q), EDGE, half)


def first_row(s):
    return D0 * s - 2 if s > 0 else EDGE - 2 + D0 * s


def own_row(s):
    return 0 if s > 0 else EDGE


def accumulate(s, warped, side, center, data, source):
    at = first_row(s)
    value = warped[pl.ds(at, OUT), :]
    slope = float(s) * (warped[pl.ds(at + 1, OUT), :] - warped[pl.ds(at - 1, OUT), :])
    if side is not None:
        side_part = side[pl.ds(at, OUT), :]
        slope = slope + side_part if s else side_part
    error = value - center
    robust = lax.rsqrt(1.0 + error * error)
    weighted = robust * slope
    return data + weighted * slope, source + weighted * error


def fill(slab, at, array):
    slab[pl.ds(at, array.shape[0]), :] = array


def zero_tails(slabs):
    for i in range(ANG):
        slabs[i, pl.ds(ROWS, SLAB - ROWS), :] = jnp.zeros((SLAB - ROWS, LANES), F32)


def fill_pieces(parts_of, outs):
    for (side, q), places in PLACES.items():
        parts = parts_of(side, q)
        for s, at in places:
            for out, part in zip(outs, parts):
                fill(out.at[s + HALF], at, part)


def halves(both):
    return both[:, :LANES], both[:, LANES:]


def shifted_views(matrix, own, piece, center, warped, side, data, source):
    fill_pieces(lambda name, q: halves(dot(piece(name, q), matrix)), (warped, side))
    for s in range(-HALF, HALF + 1):
        w, d = warped.at[s + HALF], side.at[s + HALF]
        both = dot(own(s), matrix)
        fill(w, own_row(s), both[:, :LANES])
        fill(d, own_row(s), both[:, LANES:])
        data, source = accumulate(s, w, d, center, data, source)
    return data, source


def inner_sums(views, above, below, inner, data_out, source_out, warped, side, center_ref):
    zero_tails(warped)
    zero_tails(side)
    zero = jnp.zeros((OUT, LANES), F32)
    edges = {"above": above, "below": below}
    for tile in (0, 1):
        lanes = slice(tile * LANES, (tile + 1) * LANES)
        fill_pieces(
            lambda name, q: (edges[name][q * ANG + HALF][:, lanes].astype(F32),), (warped,)
        )
        data = source = zero
        for s in (0, -4, -3, -2, -1, 1, 2, 3, 4):
            w = warped.at[s + HALF]
            fill(w, own_row(s), views[(s + HALF) * ANG + HALF][:, lanes].astype(F32))
            if s == 0:
                center_ref[...] = w[pl.ds(first_row(0), OUT), :]
            data, source = accumulate(s, w, None, center_ref[...], data, source)
        data_out[tile] = data
        source_out[tile] = source
        sign = 1 - tile

        def body(a, carry, tile=tile, sign=sign):
            ti = HALF + 1 + a if sign else HALF - 1 - a
            data, source = shifted_views(
                inner[sign, a],
                lambda s: views[(s + HALF) * ANG + ti],
                lambda name, q: edges[name][q * ANG + ti],
                center_ref[...],
                warped,
                side,
                zero,
                zero,
            )
            data_out[tile] += data
            source_out[tile] += source
            return carry

        lax.fori_loop(0, HALF, body, 0)


def outer_sums(
    total_rows,
    total_cols,
    views,
    above,
    below,
    own,
    got_pair,
    got_next,
    got_piece_pair,
    got_piece_next,
    data_in,
    source_in,
    outer,
    ghost,
    ghost_center,
    zed_out,
    near_out,
    next_out,
    precond_out,
    message,
    data_acc,
    source_acc,
    warped,
    side,
    center_ref,
    center_slab,
    left,
    right,
):
    even = is_even("col")

    @pl.when(even)
    def _():
        unshare(got_next, got_piece_next, 1, left)
        unshare(got_pair, got_piece_pair, 0, right)

    @pl.when(jnp.logical_not(even))
    def _():
        unshare(got_pair, got_piece_pair, 1, left)
        unshare(got_next, got_piece_next, 0, right)

    edges = {"above": above, "below": below}
    zero_tails(warped)
    zero_tails(side)
    zero = jnp.zeros((OUT, LANES), F32)

    def ghost_rows(row, count):
        return jnp.concatenate([x[pl.ds(row, count), :] for x in (left, own, right)], axis=1)

    def fill_center(at, ref, row, count):
        fill(center_slab.at[0], at, ref[:, :LANES].astype(F32))
        fill(center_slab.at[1], at, ref[:, LANES:].astype(F32))
        both = dot(ghost_rows(row, count), ghost_center[...])
        fill(warped.at[HALF], at, both[:, :LANES])
        fill(center_slab.at[2], at, both[:, LANES:])

    for name in ("above", "below"):
        fill_center(PLACES[name, 1][1][1], edges[name][ANG + HALF], packed_piece(name, 1), EDGE)
    fill_center(EDGE, views[HALF * ANG + HALF], HALF * ROWS, ROWS)
    for tile in (0, 1):
        data_acc[tile] = data_in[tile]
        source_acc[tile] = source_in[tile]
    center_ref[...] = warped[HALF, pl.ds(first_row(0), OUT), :]
    data, source = shifted_views(
        ghost[...],
        lambda s: ghost_rows((s + HALF) * ROWS, ROWS),
        lambda name, q: ghost_rows(packed_piece(name, q), EDGE),
        center_ref[...],
        warped,
        side,
        zero,
        zero,
    )
    for step in (4, 8, 16, 32):
        data = data + pltpu.roll(data, LANES - step, 1)
        source = source + pltpu.roll(source, LANES - step, 1)
    data_acc[2] = data
    source_acc[2] = source
    for tile in (0, 1):
        sign = tile
        center_ref[...] = center_slab[tile, pl.ds(first_row(0), OUT), :]

        def lhs(ref, row, sign=sign):
            count = ref.shape[0]
            if sign:
                return jnp.concatenate([ref[:, LANES:], right[pl.ds(row, count), :]], axis=1)
            return jnp.concatenate([left[pl.ds(row, count), :], ref[:, :LANES]], axis=1)

        def body(a, carry, tile=tile, sign=sign, lhs=lhs):
            ti = HALF + 1 + a if sign else HALF - 1 - a
            data, source = shifted_views(
                outer[sign, a],
                lambda s: lhs(views.at[(s + HALF) * ANG + ti], (s + HALF) * ROWS),
                lambda name, q: lhs(edges[name].at[q * ANG + ti], packed_piece(name, q)),
                center_ref[...],
                warped,
                side,
                zero,
                zero,
            )
            data_acc[tile] += data
            source_acc[tile] += source
            return carry

        lax.fori_loop(0, HALF, body, 0)

    def joined(ref):
        return jnp.concatenate([ref[0], ref[1], ref[2]], axis=1)

    wide = 3 * LANES

    def before(x):
        return pltpu.roll(x, 1, 1)

    def after(x):
        return pltpu.roll(x, wide - 1, 1)

    def over(x):
        return pltpu.roll(x, 1, 0)

    def under(x):
        return pltpu.roll(x, OUT - 1, 0)

    at = first_row(0)
    here = jnp.concatenate([center_slab[i, pl.ds(at, OUT), :] for i in range(3)], axis=1)
    higher = jnp.concatenate([center_slab[i, pl.ds(at - 1, OUT), :] for i in range(3)], axis=1)
    lane = lax.broadcasted_iota(jnp.int32, (OUT, wide), 1)
    local_row = lax.broadcasted_iota(jnp.int32, (OUT, wide), 0) - 2
    column = jnp.where(lane < wide - 64, lane, lane - wide) + lax.axis_index("col") * COLS
    row = local_row + lax.axis_index("row") * ROWS
    across = here - before(here)
    vertical = here - higher
    h_left = jnp.where((column >= 1) & (column <= total_cols - 1), jnp.exp(-across * across), 0.0)
    v_up = jnp.where((row >= 1) & (row <= total_rows - 1), jnp.exp(-vertical * vertical), 0.0)
    h_right = after(h_left)
    v_down = under(v_up)
    coeff = DAMPING + joined(data_acc) * (0.25 / VIEWS)
    source = joined(source_acc) * (-0.5 / VIEWS)
    precond = coeff + SMOOTH * (h_left + h_right + v_up + v_down)
    inverse = 1.0 / precond

    def neighbours(x):
        total = h_left * before(x) + h_right * after(x) + v_up * over(x) + v_down * under(x)
        return SMOOTH * inverse * total

    zed = source * inverse
    near = neighbours(zed)
    nxt = neighbours(near)

    def block(x):
        return x[:, :COLS]

    zed, near, nxt, precond = block(zed), block(near), block(nxt), block(precond)
    zed_out[...] = zed
    near_out[...] = near
    next_out[...] = nxt
    precond_out[...] = precond
    mine = (block(local_row) >= 0) & (block(local_row) < ROWS)

    def inner(x, y):
        return jnp.sum(jnp.where(mine, precond * x * y, 0.0), keepdims=True)

    zz = inner(zed, zed)
    zn = inner(zed, near)
    kappa = jnp.clip(zn / jnp.where(zz > 0, zz, 1.0), -1.0, 1.0)
    y = near - kappa * zed
    g = nxt - kappa * near
    numbers = (
        (0, inner(y, y)),
        (1, inner(y, g)),
        (32, 2.0 * inner(y, zed)),
        (33, inner(y, near) + inner(zed, g)),
        (64, zz),
        (65, zn),
        (96, kappa),
        (97, kappa),
    )
    place = lax.broadcasted_iota(jnp.int32, (1, LANES), 1)
    out = jnp.zeros((1, LANES), F32)
    for where, number in numbers:
        out = jnp.where(place == where, number, out)
    message[...] = out


def finish(messages, zed_ref, near_ref, next_ref, precond_ref, increment, residual):
    all_of = messages[...]
    total = jnp.sum(all_of, axis=0, keepdims=True)
    zz = total[:, 64:65]
    zn = total[:, 65:66]
    kappa = zn / zz
    delta = pltpu.roll(all_of, 32, 1) - kappa
    linear = pltpu.roll(all_of, 96, 1)
    quad = pltpu.roll(all_of, 64, 1)
    moved = jnp.sum(all_of + delta * (linear + delta * quad), axis=0, keepdims=True)
    yy = moved[:, 0:1]
    yny = moved[:, 1:2]
    step0 = zz / (zz - zn)
    beta = step0 * step0 * yy / zz
    step1 = yy / (yy - yny - step0 * yy * yy / zz)
    rows = pl.ds(2, ROWS)
    zed = zed_ref[rows, :]
    near = near_ref[rows, :]
    nxt = next_ref[rows, :]
    y = near - kappa * zed
    g = nxt - kappa * near
    increment[...] = step0 * zed + step1 * (step0 * y + beta * zed)
    residual[...] = precond_ref[rows, :] * (
        step0 * y - step1 * (step0 * (y - g) + beta * (zed - near))
    )


def call(kernel, outs, scratch=(), name=None):
    return pl.pallas_call(
        kernel,
        out_shape=outs,
        scratch_shapes=list(scratch),
        compiler_params=pltpu.CompilerParams(vmem_limit_bytes=24 * 1024 * 1024),
        name=name,
    )


def swap(array, axis, start):
    pairs = []
    for i in range(start, lax.axis_size(axis) - 1, 2):
        pairs += [(i, i + 1), (i + 1, i)]
    return lax.ppermute(array, axis, pairs)


def shards(views):
    rows, cols = lax.axis_size("row"), lax.axis_size("col")
    inner, outer, ghost, center = (jnp.asarray(x) for x in tables())
    bf16 = jnp.bfloat16
    struct = jax.ShapeDtypeStruct

    edge = struct((PIECES * ANG, EDGE, COLS), bf16)
    room = pltpu.VMEM(edge.shape, bf16)
    pair, after = call(pack_rows, (edge, edge), (room, room), name="pack_rows")(views)
    pair = swap(pair, "row", 0)
    after = swap(after, "row", 1)
    shared = struct((SHARED, LANES), bf16)
    room = pltpu.VMEM((SHARED, LANES), bf16)
    own, block_pair, block_next, pack = call(
        pack_own,
        (struct((ANG * ROWS, LANES), bf16), shared, shared, struct((ANG, COLS, LANES), bf16)),
        (room, room),
        name="pack_own",
    )(views)
    block_next = swap(block_next, "col", 1)
    block_pair = swap(block_pair, "col", 0)
    sent = struct((PIECES * EDGE, LANES), bf16)
    small = pltpu.VMEM((PIECES * EDGE, LANES), bf16)
    above, below, own, piece_pair, piece_next = call(
        pack_edges,
        (edge, edge, struct((PACKED, LANES), bf16), sent, sent),
        (small, small),
        name="pack_edges",
    )(pair, after, pack, own)
    piece_next = swap(piece_next, "col", 1)
    piece_pair = swap(piece_pair, "col", 0)
    slab = pltpu.VMEM((ANG, SLAB, LANES), F32)
    tile = pltpu.VMEM((OUT, LANES), F32)
    sums = struct((2, OUT, LANES), F32)
    data, source = call(inner_sums, (sums, sums), (slab, slab, tile), name="inner_sums")(
        views, above, below, inner
    )
    field = struct((OUT, COLS), F32)
    acc = pltpu.VMEM((3, OUT, LANES), F32)
    zed, near, nxt, precond, message = call(
        functools.partial(outer_sums, rows * ROWS, cols * COLS),
        (field, field, field, field, struct((1, LANES), F32)),
        (
            acc,
            acc,
            slab,
            slab,
            tile,
            pltpu.VMEM((3, SLAB, LANES), F32),
            pltpu.VMEM((PACKED, LANES), bf16),
            pltpu.VMEM((PACKED, LANES), bf16),
        ),
        name="outer_sums",
    )(
        views, above, below, own, block_pair, block_next, piece_pair, piece_next,
        data, source, outer, ghost, center,
    )
    n = rows * cols
    messages = lax.all_to_all(
        jnp.broadcast_to(message[None], (n, 1, LANES)), ALL, 0, 0, tiled=True
    ).reshape(n, LANES)
    block = struct((ROWS, COLS), F32)
    return call(finish, (block, block), name="finish")(messages, zed, near, nxt, precond)


def solution(mesh):
    return jax.shard_map(
        shards,
        mesh=mesh,
        in_specs=(P(None, "row", "col"),),
        out_specs=(P("row", "col"), P("row", "col")),
        check_vma=False,
    )
```

```python
import functools

import jax
import jax.numpy as jnp
import ml_dtypes
import numpy as np
from jax import lax
from jax.experimental import pallas as pl
from jax.experimental.pallas import tpu as pltpu
from jax.sharding import PartitionSpec as P

ANG = 9
VIEWS = 81
HALF = ANG // 2
D0 = 3
ROWS = 64
COLS = 256
EDGE = 16
OUT = 72
SLAB = 96
PIECES = 3
PACKED = ANG * ROWS + 2 * PIECES * EDGE
PAIRS = ((-4, -3), (-2, -1), (1, 2), (3, 4), (0, 0))
SENT = len(PAIRS) * ROWS + PIECES * EDGE
LANES = 128
SMOOTH = 2.0
DAMPING = 0.1
ALL = ("row", "col")
F32 = jnp.float32


def lane_first(t, c):
    return D0 * t * (t + 1) // 2 + c


def lane_last(t, c):
    a = abs(t)
    return 64 + D0 * a * (a + 1) // 2 + c - (COLS - D0 * a - D0)


def lane_here(t, c):
    return 45 + 2 * (-t - 1) + c if t < 0 else 109 + 2 * (t - 1) + c - (COLS - 2)


def edge_source(t, c):
    if c < 0:
        return lane_last(t, COLS + c)
    if c >= COLS:
        return 2 * LANES + lane_first(t, c - COLS)
    if t >= 0 and c <= D0 * t + D0 - 1:
        return LANES + lane_first(t, c)
    if t <= 0 and c >= COLS - D0 * abs(t) - D0:
        return LANES + lane_last(t, c)
    return LANES + lane_here(t, c)


def edge_pixels():
    for t in range(-HALF, HALF + 1):
        for column in range(-2, D0 * -t + 1 if t < 0 else 0):
            yield t, column
        for column in range(COLS - 1 - D0 * t if t > 0 else COLS, COLS + 2):
            yield t, column


def tables():
    inner = np.zeros((2, 2, HALF, COLS, 2 * LANES), np.float32)
    for tile in (0, 1):
        for a in range(1, HALF + 1):
            for sign in (0, 1):
                t = a if sign else -a
                for j in range(LANES):
                    c = tile * LANES + j + D0 * t
                    if 1 <= c < COLS - 1:
                        inner[tile, sign, a - 1, c, j] += 1
                        inner[tile, sign, a - 1, c + 1, LANES + j] += t
                        inner[tile, sign, a - 1, c - 1, LANES + j] -= t
    edge = np.zeros((3 * LANES, 2 * LANES), np.float32)
    center = np.zeros((LANES + COLS + LANES, 2 * LANES), np.float32)
    scatter = np.zeros((LANES, 3 * LANES), np.float32)

    def center_source(c):
        if c < 0:
            return lane_last(0, COLS + c)
        return LANES + c if c < COLS else LANES + COLS + lane_first(0, c - COLS)

    for lane, (t, col) in enumerate(edge_pixels()):
        c = col + D0 * t
        edge[edge_source(t, c), lane] += 1
        if t:
            edge[edge_source(t, c + 1), LANES + lane] += t
            edge[edge_source(t, c - 1), LANES + lane] -= t
        center[center_source(col), lane] = 1
        scatter[lane, col % (3 * LANES)] = 1
    for col in (-3, -2, -1, COLS, COLS + 1, COLS + 2):
        center[center_source(col), LANES + col % LANES] = 1
    return tuple(x.astype(ml_dtypes.bfloat16) for x in (inner, edge, center, scatter))


def dot(a, b):
    return jnp.dot(a, b, preferred_element_type=F32)


def is_even(axis):
    return lax.rem(lax.axis_index(axis), 2) == 0


def pack_rows(views, send_pair, send_next, tops, bottoms, ups, downs, sems):
    count = (HALF + 1) * ANG
    get_tops = pltpu.make_async_copy(
        views.at[pl.ds(HALF * ANG, count), pl.ds(0, EDGE)], tops, sems.at[0]
    )
    get_bottoms = pltpu.make_async_copy(
        views.at[pl.ds(0, count), pl.ds(ROWS - EDGE, EDGE)], bottoms, sems.at[1]
    )
    get_tops.start()
    get_bottoms.start()
    index = lax.broadcasted_iota(jnp.int32, (EDGE, COLS), 0)

    def put(out, q, ti, rows):
        out[q * ANG + ti] = rows.astype(jnp.bfloat16)

    get_tops.wait()
    for ti in range(ANG):

        def first(s, ti=ti):
            return tops[s * ANG + ti].astype(F32)

        put(ups, 0, ti, first(4))
        put(ups, 1, ti, jnp.where(index < 12, first(3), pltpu.roll(first(0), 12, 0)))
        put(ups, 2, ti, jnp.where(index < 9, first(2), pltpu.roll(first(1), 9, 0)))
    get_bottoms.wait()
    for ti in range(ANG):

        def last(s, ti=ti):
            return bottoms[(s + HALF) * ANG + ti].astype(F32)

        put(downs, 0, ti, last(-4))
        put(downs, 1, ti, jnp.where(index < 4, pltpu.roll(last(0), 4, 0), last(-3)))
        put(downs, 2, ti, jnp.where(index < 7, pltpu.roll(last(-1), 7, 0), last(-2)))
    even = is_even("row")

    @pl.when(even)
    def _():
        send_pair[...] = downs[...]
        send_next[...] = ups[...]

    @pl.when(jnp.logical_not(even))
    def _():
        send_pair[...] = ups[...]
        send_next[...] = downs[...]


PLACES = {
    ("above", 0): ((-4, 0),),
    ("above", 1): ((-3, 0), (0, 12)),
    ("above", 2): ((-2, 0), (-1, 9)),
    ("below", 0): ((4, ROWS),),
    ("below", 1): ((3, ROWS), (0, EDGE + ROWS - 12)),
    ("below", 2): ((2, ROWS), (1, ROWS - 9)),
}


def packed_piece(side, q):
    return ANG * ROWS + ((0 if side == "above" else PIECES) + q) * EDGE


def share(first_of, second_of, to_left, to_right, at):
    low = lax.broadcasted_iota(jnp.int32, first_of.shape, 1) < 64
    turned = pltpu.roll(second_of, 64, 1)
    to_left[pl.ds(at, first_of.shape[0]), :] = jnp.where(low, first_of, turned).astype(
        jnp.bfloat16
    )
    turned = pltpu.roll(first_of, 64, 1)
    to_right[pl.ds(at, first_of.shape[0]), :] = jnp.where(low, turned, second_of).astype(
        jnp.bfloat16
    )


def pack_own(views, own, to_left, to_right, pack):
    column = lax.broadcasted_iota(jnp.int32, (COLS, LANES), 0)
    lane = lax.broadcasted_iota(jnp.int32, (COLS, LANES), 1)
    for t in range(-HALF, HALF + 1):
        hit = jnp.zeros((COLS, LANES), F32)
        if t >= 0:
            bound = D0 * t + D0
            hit = jnp.where((column < bound) & (lane - column == lane_first(t, 0)), 1.0, hit)
        if t <= 0:
            start = COLS - D0 * abs(t) - D0
            apart = lane_last(t, start) - start
            hit = jnp.where((column >= start) & (lane - column == apart), 1.0, hit)
        if t:
            near = column < 2 if t < 0 else column >= COLS - 2
            apart = lane_here(t, 0)
            hit = jnp.where(near & (lane - column == apart), 1.0, hit)
        pack[t + HALF] = hit.astype(jnp.bfloat16)
    for p, pair in enumerate(PAIRS):
        both = []
        for s in pair:
            total = dot(views[(s + HALF) * ANG], pack[0])
            for ti in range(1, ANG):
                total = total + dot(views[(s + HALF) * ANG + ti], pack[ti])
            own[(s + HALF) * ROWS : (s + HALF + 1) * ROWS, :] = total.astype(jnp.bfloat16)
            both.append(total)
        share(both[0], both[1], to_left, to_right, p * ROWS)


def pack_edges(
    got_pair, got_next, pack, own_in, left_in, right_in,
    above, below, own, send_pair, send_next, to_left, to_right,
):
    even = is_even("row")

    @pl.when(even)
    def _():
        below[...] = got_pair[...]
        above[...] = got_next[...]

    @pl.when(jnp.logical_not(even))
    def _():
        below[...] = got_next[...]
        above[...] = got_pair[...]

    own[: ANG * ROWS, :] = own_in[...]
    for q in range(PIECES):
        both = []
        for side, ref in (("above", above), ("below", below)):
            total = dot(ref[q * ANG], pack[0])
            for ti in range(1, ANG):
                total = total + dot(ref[q * ANG + ti], pack[ti])
            own[pl.ds(packed_piece(side, q), EDGE), :] = total.astype(jnp.bfloat16)
            both.append(total)
        share(both[0], both[1], to_left, to_right, q * EDGE)
    rows = len(PAIRS) * ROWS
    even = is_even("col")

    def send(out, block, piece):
        out[:rows, :] = block[...]
        out[rows:, :] = piece[...]

    @pl.when(even)
    def _():
        send(send_pair, right_in, to_right)
        send(send_next, left_in, to_left)

    @pl.when(jnp.logical_not(even))
    def _():
        send(send_pair, left_in, to_left)
        send(send_next, right_in, to_right)


def unshare(source, high, out):
    def move(at, to, count, half):
        rows = source[pl.ds(at, count), :]
        if half != high:
            rows = pltpu.roll(rows.astype(F32), 64, 1).astype(jnp.bfloat16)
        out[pl.ds(to, count), :] = rows

    for p, pair in enumerate(PAIRS):
        for half, s in enumerate(pair):
            if s or not half:
                move(p * ROWS, (s + HALF) * ROWS, ROWS, half)
    for q in range(PIECES):
        for half, side in enumerate(("above", "below")):
            move(len(PAIRS) * ROWS + q * EDGE, packed_piece(side, q), EDGE, half)


def first_row(s):
    return D0 * s - 2 if s > 0 else EDGE - 2 + D0 * s


def own_row(s):
    return 0 if s > 0 else EDGE


def accumulate(s, warped, side, center, data, source):
    at = first_row(s)
    value = warped[pl.ds(at, OUT), :]
    slope = float(s) * (warped[pl.ds(at + 1, OUT), :] - warped[pl.ds(at - 1, OUT), :])
    if side is not None:
        side_part = side[pl.ds(at, OUT), :]
        slope = slope + side_part if s else side_part
    error = value - center
    robust = lax.rsqrt(1.0 + error * error)
    weighted = robust * slope
    return data + weighted * slope, source + weighted * error


def fill(slab, at, array):
    slab[pl.ds(at, array.shape[0]), :] = array


def zero_tails(slabs):
    for i in range(ANG):
        slabs[i, pl.ds(ROWS, SLAB - ROWS), :] = jnp.zeros((SLAB - ROWS, LANES), F32)


def fill_pieces(parts_of, outs):
    for (side, q), places in PLACES.items():
        parts = parts_of(side, q)
        for s, at in places:
            for out, part in zip(outs, parts):
                fill(out.at[s + HALF], at, part)


def halves(both):
    return both[:, :LANES], both[:, LANES:]


def shifted_views(matrix, own, piece, center, warped, side, data, source):
    fill_pieces(lambda name, q: halves(dot(piece(name, q), matrix)), (warped, side))
    for s in range(-HALF, HALF + 1):
        w, d = warped.at[s + HALF], side.at[s + HALF]
        both = dot(own(s), matrix)
        fill(w, own_row(s), both[:, :LANES])
        fill(d, own_row(s), both[:, LANES:])
        data, source = accumulate(s, w, d, center, data, source)
    return data, source


def inner_sums(views, above, below, inner, data_out, source_out, warped, side, center_ref):
    zero_tails(warped)
    zero_tails(side)
    zero = jnp.zeros((OUT, LANES), F32)
    edges = {"above": above, "below": below}
    for tile in (0, 1):
        lanes = slice(tile * LANES, (tile + 1) * LANES)
        fill_pieces(
            lambda name, q: (edges[name][q * ANG + HALF][:, lanes].astype(F32),), (warped,)
        )
        data = source = zero
        for s in (0, -4, -3, -2, -1, 1, 2, 3, 4):
            w = warped.at[s + HALF]
            fill(w, own_row(s), views[(s + HALF) * ANG + HALF][:, lanes].astype(F32))
            if s == 0:
                center_ref[...] = w[pl.ds(first_row(0), OUT), :]
            data, source = accumulate(s, w, None, center_ref[...], data, source)
        data_out[tile] = data
        source_out[tile] = source

        def body(a, carry, sign, tile=tile):
            ti = HALF + 1 + a if sign else HALF - 1 - a
            data, source = shifted_views(
                inner[tile, sign, a],
                lambda s: views[(s + HALF) * ANG + ti],
                lambda name, q: edges[name][q * ANG + ti],
                center_ref[...],
                warped,
                side,
                zero,
                zero,
            )
            data_out[tile] += data
            source_out[tile] += source
            return carry

        for sign in (0, 1):
            lax.fori_loop(0, HALF, functools.partial(body, sign=sign), 0)


def outer_sums(
    total_rows,
    total_cols,
    views,
    above,
    below,
    own,
    got_pair,
    got_next,
    data_in,
    source_in,
    edge,
    edge_center,
    scatter,
    zed_out,
    near_out,
    next_out,
    precond_out,
    message,
    warped,
    side,
    center_ref,
    center_slab,
    left,
    right,
):
    even = is_even("col")

    @pl.when(even)
    def _():
        unshare(got_next, 1, left)
        unshare(got_pair, 0, right)

    @pl.when(jnp.logical_not(even))
    def _():
        unshare(got_pair, 1, left)
        unshare(got_next, 0, right)

    edges = {"above": above, "below": below}
    zero_tails(warped)
    zero_tails(side)
    zero = jnp.zeros((OUT, LANES), F32)

    def edge_rows(row, count):
        return jnp.concatenate([x[pl.ds(row, count), :] for x in (left, own, right)], axis=1)

    def fill_center(at, ref, row, count):
        fill(center_slab.at[0], at, ref[:, :LANES].astype(F32))
        fill(center_slab.at[1], at, ref[:, LANES:].astype(F32))
        around = (left[pl.ds(row, count), :], ref[...], right[pl.ds(row, count), :])
        both = dot(jnp.concatenate(around, axis=1), edge_center[...])
        fill(warped.at[HALF], at, both[:, :LANES])
        fill(center_slab.at[2], at, both[:, LANES:])

    for name in ("above", "below"):
        at = PLACES[name, 1][1][1]
        fill_center(at, edges[name].at[ANG + HALF], packed_piece(name, 1), EDGE)
    fill_center(EDGE, views.at[HALF * ANG + HALF], HALF * ROWS, ROWS)
    center_ref[...] = warped[HALF, pl.ds(first_row(0), OUT), :]
    sums = shifted_views(
        edge[...],
        lambda s: edge_rows((s + HALF) * ROWS, ROWS),
        lambda name, q: edge_rows(packed_piece(name, q), EDGE),
        center_ref[...],
        warped,
        side,
        zero,
        zero,
    )

    def total(inside, x):
        high = x.astype(jnp.bfloat16)
        rest = x - high.astype(F32)
        middle = rest.astype(jnp.bfloat16)
        low = (rest - middle.astype(F32)).astype(jnp.bfloat16)
        spread = dot(low, scatter[...]) + dot(middle, scatter[...]) + dot(high, scatter[...])
        return jnp.concatenate([inside[0], inside[1], zero], axis=1) + spread

    data_sum = total(data_in, sums[0])
    source_sum = total(source_in, sums[1])

    wide = 3 * LANES

    def before(x):
        return pltpu.roll(x, 1, 1)

    def after(x):
        return pltpu.roll(x, wide - 1, 1)

    def over(x):
        return pltpu.roll(x, 1, 0)

    def under(x):
        return pltpu.roll(x, OUT - 1, 0)

    at = first_row(0)
    here = jnp.concatenate([center_slab[i, pl.ds(at, OUT), :] for i in range(3)], axis=1)
    higher = jnp.concatenate([center_slab[i, pl.ds(at - 1, OUT), :] for i in range(3)], axis=1)
    lane = lax.broadcasted_iota(jnp.int32, (OUT, wide), 1)
    local_row = lax.broadcasted_iota(jnp.int32, (OUT, wide), 0) - 2
    column = jnp.where(lane < wide - 64, lane, lane - wide) + lax.axis_index("col") * COLS
    row = local_row + lax.axis_index("row") * ROWS
    across = here - before(here)
    vertical = here - higher
    h_left = jnp.where((column >= 1) & (column <= total_cols - 1), jnp.exp(-across * across), 0.0)
    v_up = jnp.where((row >= 1) & (row <= total_rows - 1), jnp.exp(-vertical * vertical), 0.0)
    h_right = after(h_left)
    v_down = under(v_up)
    coeff = DAMPING + data_sum * (0.25 / VIEWS)
    source = source_sum * (-0.5 / VIEWS)
    precond = coeff + SMOOTH * (h_left + h_right + v_up + v_down)
    inverse = 1.0 / precond

    def neighbours(x):
        total = h_left * before(x) + h_right * after(x) + v_up * over(x) + v_down * under(x)
        return SMOOTH * inverse * total

    zed = source * inverse
    near = neighbours(zed)
    nxt = neighbours(near)

    def block(x):
        return x[:, :COLS]

    zed, near, nxt, precond = block(zed), block(near), block(nxt), block(precond)
    zed_out[...] = zed
    near_out[...] = near
    next_out[...] = nxt
    precond_out[...] = precond
    mine = (block(local_row) >= 0) & (block(local_row) < ROWS)

    def inner(x, y):
        return jnp.sum(jnp.where(mine, precond * x * y, 0.0), keepdims=True)

    zz = inner(zed, zed)
    zn = inner(zed, near)
    kappa = jnp.clip(zn / jnp.where(zz > 0, zz, 1.0), -1.0, 1.0)
    y = near - kappa * zed
    g = nxt - kappa * near
    numbers = (
        (0, inner(y, y)),
        (1, inner(y, g)),
        (32, 2.0 * inner(y, zed)),
        (33, inner(y, near) + inner(zed, g)),
        (64, zz),
        (65, zn),
        (96, kappa),
        (97, kappa),
    )
    place = lax.broadcasted_iota(jnp.int32, (1, LANES), 1)
    out = jnp.zeros((1, LANES), F32)
    for where, number in numbers:
        out = jnp.where(place == where, number, out)
    message[...] = out


def finish(messages, zed_ref, near_ref, next_ref, precond_ref, increment, residual):
    all_of = messages[...]
    total = jnp.sum(all_of, axis=0, keepdims=True)
    zz = total[:, 64:65]
    zn = total[:, 65:66]
    kappa = zn / zz
    delta = pltpu.roll(all_of, 32, 1) - kappa
    linear = pltpu.roll(all_of, 96, 1)
    quad = pltpu.roll(all_of, 64, 1)
    moved = jnp.sum(all_of + delta * (linear + delta * quad), axis=0, keepdims=True)
    yy = moved[:, 0:1]
    yny = moved[:, 1:2]
    step0 = zz / (zz - zn)
    beta = step0 * step0 * yy / zz
    step1 = yy / (yy - yny - step0 * yy * yy / zz)
    rows = pl.ds(2, ROWS)
    zed = zed_ref[rows, :]
    near = near_ref[rows, :]
    nxt = next_ref[rows, :]
    y = near - kappa * zed
    g = nxt - kappa * near
    increment[...] = step0 * zed + step1 * (step0 * y + beta * zed)
    residual[...] = precond_ref[rows, :] * (
        step0 * y - step1 * (step0 * (y - g) + beta * (zed - near))
    )


def call(kernel, outs, scratch=(), name=None, vmem=24, **more):
    return pl.pallas_call(
        kernel,
        out_shape=outs,
        scratch_shapes=list(scratch),
        compiler_params=pltpu.CompilerParams(vmem_limit_bytes=vmem * 1024 * 1024),
        name=name,
        **more,
    )


def swap(array, axis, start):
    pairs = []
    for i in range(start, lax.axis_size(axis) - 1, 2):
        pairs += [(i, i + 1), (i + 1, i)]
    return lax.ppermute(array, axis, pairs)


def shards(views):
    rows, cols = lax.axis_size("row"), lax.axis_size("col")
    inner, edge_matrix, center, scatter = (jnp.asarray(x) for x in tables())
    bf16 = jnp.bfloat16
    struct = jax.ShapeDtypeStruct

    edge = struct((PIECES * ANG, EDGE, COLS), bf16)
    room = pltpu.VMEM(edge.shape, bf16)
    taken = pltpu.VMEM(((HALF + 1) * ANG, EDGE, COLS), bf16)
    pair, after = call(
        pack_rows,
        (edge, edge),
        (taken, taken, room, room, pltpu.SemaphoreType.DMA((2,))),
        name="pack_rows",
        vmem=60,
        in_specs=[pl.BlockSpec(memory_space=pltpu.HBM)],
    )(views)
    pair = swap(pair, "row", 0)
    after = swap(after, "row", 1)
    shared = struct((len(PAIRS) * ROWS, LANES), bf16)
    own, to_left, to_right, pack = call(
        pack_own,
        (struct((ANG * ROWS, LANES), bf16), shared, shared, struct((ANG, COLS, LANES), bf16)),
        name="pack_own",
    )(views)
    sent = struct((SENT, LANES), bf16)
    small = pltpu.VMEM((PIECES * EDGE, LANES), bf16)
    above, below, own, pair, after = call(
        pack_edges,
        (edge, edge, struct((PACKED, LANES), bf16), sent, sent),
        (small, small),
        name="pack_edges",
    )(pair, after, pack, own, to_left, to_right)
    pair = swap(pair, "col", 0)
    after = swap(after, "col", 1)
    slab = pltpu.VMEM((ANG, SLAB, LANES), F32)
    tile = pltpu.VMEM((OUT, LANES), F32)
    sums = struct((2, OUT, LANES), F32)
    data, source = call(inner_sums, (sums, sums), (slab, slab, tile), name="inner_sums")(
        views, above, below, inner
    )
    field = struct((OUT, COLS), F32)
    zed, near, nxt, precond, message = call(
        functools.partial(outer_sums, rows * ROWS, cols * COLS),
        (field, field, field, field, struct((1, LANES), F32)),
        (
            slab,
            slab,
            tile,
            pltpu.VMEM((3, SLAB, LANES), F32),
            pltpu.VMEM((PACKED, LANES), bf16),
            pltpu.VMEM((PACKED, LANES), bf16),
        ),
        name="outer_sums",
    )(views, above, below, own, pair, after, data, source, edge_matrix, center, scatter)
    n = rows * cols
    messages = lax.all_to_all(
        jnp.broadcast_to(message[None], (n, 1, LANES)), ALL, 0, 0, tiled=True
    ).reshape(n, LANES)
    block = struct((ROWS, COLS), F32)
    return call(finish, (block, block), name="finish")(messages, zed, near, nxt, precond)


def solution(mesh):
    return jax.shard_map(
        shards,
        mesh=mesh,
        in_specs=(P(None, "row", "col"),),
        out_specs=(P("row", "col"), P("row", "col")),
        check_vma=False,
    )
```

```python
import functools

import jax
import jax.numpy as jnp
import ml_dtypes
import numpy as np
from jax import lax
from jax.experimental import pallas as pl
from jax.experimental.pallas import tpu as pltpu
from jax.sharding import PartitionSpec as P

ANG = 9
VIEWS = 81
HALF = ANG // 2
D0 = 3
ROWS = 64
COLS = 256
EDGE = 16
OUT = 72
SLAB = 96
PIECES = 3
PACKED = ANG * ROWS + 2 * PIECES * EDGE
PAIRS = ((-4, -3), (-2, -1), (1, 2), (3, 4), (0, 0))
SHARED = len(PAIRS) * ROWS
LANES = 128
SMOOTH = 2.0
DAMPING = 0.1
ALL = ("row", "col")
F32 = jnp.float32


def lane_first(t, c):
    return D0 * t * (t + 1) // 2 + c


def lane_last(t, c):
    a = abs(t)
    return 64 + D0 * a * (a + 1) // 2 + c - (COLS - D0 * a - D0)


def lane_here(t, c):
    return 45 + 2 * (-t - 1) + c if t < 0 else 109 + 2 * (t - 1) + c - (COLS - 2)


def edge_source(t, c):
    if c < 0:
        return lane_last(t, COLS + c)
    if c >= COLS:
        return 2 * LANES + lane_first(t, c - COLS)
    if t >= 0 and c <= D0 * t + D0 - 1:
        return LANES + lane_first(t, c)
    if t <= 0 and c >= COLS - D0 * abs(t) - D0:
        return LANES + lane_last(t, c)
    return LANES + lane_here(t, c)


def edge_pixels():
    for t in range(-HALF, HALF + 1):
        for column in range(-2, D0 * -t + 1 if t < 0 else 0):
            yield t, column
        for column in range(COLS - 1 - D0 * t if t > 0 else COLS, COLS + 2):
            yield t, column


def tables():
    inner = np.zeros((2, 2, HALF, COLS, 2 * LANES), np.float32)
    for tile in (0, 1):
        for a in range(1, HALF + 1):
            for sign in (0, 1):
                t = a if sign else -a
                for j in range(LANES):
                    c = tile * LANES + j + D0 * t
                    if 1 <= c < COLS - 1:
                        inner[tile, sign, a - 1, c, j] += 1
                        inner[tile, sign, a - 1, c + 1, LANES + j] += t
                        inner[tile, sign, a - 1, c - 1, LANES + j] -= t
    edge = np.zeros((3 * LANES, 2 * LANES), np.float32)
    center = np.zeros((LANES + COLS + LANES, 2 * LANES), np.float32)
    scatter = np.zeros((LANES, 3 * LANES), np.float32)

    def center_source(c):
        if c < 0:
            return lane_last(0, COLS + c)
        return LANES + c if c < COLS else LANES + COLS + lane_first(0, c - COLS)

    for lane, (t, col) in enumerate(edge_pixels()):
        c = col + D0 * t
        edge[edge_source(t, c), lane] += 1
        if t:
            edge[edge_source(t, c + 1), LANES + lane] += t
            edge[edge_source(t, c - 1), LANES + lane] -= t
        center[center_source(col), lane] = 1
        scatter[lane, col % (3 * LANES)] = 1
    for col in (-3, -2, -1, COLS, COLS + 1, COLS + 2):
        center[center_source(col), LANES + col % LANES] = 1
    return tuple(x.astype(ml_dtypes.bfloat16) for x in (*inner, edge, center, scatter))


def dot(a, b):
    return jnp.dot(a, b, preferred_element_type=F32)


def is_even(axis):
    return lax.rem(lax.axis_index(axis), 2) == 0


def pack_rows(views, send_pair, send_next, ups_out, downs_out):
    even = is_even("row")
    index = lax.broadcasted_iota(jnp.int32, (EDGE, COLS), 0)

    def put(ups, q, ti, rows):
        (ups_out if ups else downs_out)[q * ANG + ti] = rows.astype(jnp.bfloat16)

    for ti in range(ANG):

        def rows_of(s, start, ti=ti):
            return views[(s + HALF) * ANG + ti, pl.ds(start, EDGE), :].astype(F32)

        first = functools.partial(rows_of, start=0)
        last = functools.partial(rows_of, start=ROWS - EDGE)
        put(True, 0, ti, first(4))
        put(True, 1, ti, jnp.where(index < 12, first(3), pltpu.roll(first(0), 12, 0)))
        put(True, 2, ti, jnp.where(index < 9, first(2), pltpu.roll(first(1), 9, 0)))
        put(False, 0, ti, last(-4))
        put(False, 1, ti, jnp.where(index < 4, pltpu.roll(last(0), 4, 0), last(-3)))
        put(False, 2, ti, jnp.where(index < 7, pltpu.roll(last(-1), 7, 0), last(-2)))

    @pl.when(even)
    def _():
        send_pair[...] = downs_out[...]
        send_next[...] = ups_out[...]

    @pl.when(jnp.logical_not(even))
    def _():
        send_pair[...] = ups_out[...]
        send_next[...] = downs_out[...]


PLACES = {
    ("above", 0): ((-4, 0),),
    ("above", 1): ((-3, 0), (0, 12)),
    ("above", 2): ((-2, 0), (-1, 9)),
    ("below", 0): ((4, ROWS),),
    ("below", 1): ((3, ROWS), (0, EDGE + ROWS - 12)),
    ("below", 2): ((2, ROWS), (1, ROWS - 9)),
}


def packed_piece(side, q):
    return ANG * ROWS + ((0 if side == "above" else PIECES) + q) * EDGE


def share(first_of, second_of, to_left, to_right, at):
    low = lax.broadcasted_iota(jnp.int32, first_of.shape, 1) < 64
    turned = pltpu.roll(second_of, 64, 1)
    to_left[pl.ds(at, first_of.shape[0]), :] = jnp.where(low, first_of, turned).astype(
        jnp.bfloat16
    )
    turned = pltpu.roll(first_of, 64, 1)
    to_right[pl.ds(at, first_of.shape[0]), :] = jnp.where(low, turned, second_of).astype(
        jnp.bfloat16
    )


def by_pair(to_left, to_right, send_pair, send_next):
    even = is_even("col")

    @pl.when(even)
    def _():
        send_pair[...] = to_right[...]
        send_next[...] = to_left[...]

    @pl.when(jnp.logical_not(even))
    def _():
        send_pair[...] = to_left[...]
        send_next[...] = to_right[...]


def pack_own(views, own, send_pair, send_next, pack, to_left, to_right):
    column = lax.broadcasted_iota(jnp.int32, (COLS, LANES), 0)
    lane = lax.broadcasted_iota(jnp.int32, (COLS, LANES), 1)
    for t in range(-HALF, HALF + 1):
        hit = jnp.zeros((COLS, LANES), F32)
        if t >= 0:
            bound = D0 * t + D0
            hit = jnp.where((column < bound) & (lane - column == lane_first(t, 0)), 1.0, hit)
        if t <= 0:
            start = COLS - D0 * abs(t) - D0
            apart = lane_last(t, start) - start
            hit = jnp.where((column >= start) & (lane - column == apart), 1.0, hit)
        if t:
            near = column < 2 if t < 0 else column >= COLS - 2
            apart = lane_here(t, 0)
            hit = jnp.where(near & (lane - column == apart), 1.0, hit)
        pack[t + HALF] = hit.astype(jnp.bfloat16)
    for p, pair in enumerate(PAIRS):
        both = []
        for s in pair:
            total = dot(views[(s + HALF) * ANG], pack[0])
            for ti in range(1, ANG):
                total = total + dot(views[(s + HALF) * ANG + ti], pack[ti])
            own[(s + HALF) * ROWS : (s + HALF + 1) * ROWS, :] = total.astype(jnp.bfloat16)
            both.append(total)
        share(both[0], both[1], to_left, to_right, p * ROWS)
    by_pair(to_left, to_right, send_pair, send_next)


def pack_edges_and_left_sums(
    views, inner, got_pair, got_next, pack, own_in,
    data_out, source_out, above, below, own, send_pair, send_next,
    to_left, to_right, *scratch,
):
    even = is_even("row")

    @pl.when(even)
    def _():
        below[...] = got_pair[...]
        above[...] = got_next[...]

    @pl.when(jnp.logical_not(even))
    def _():
        below[...] = got_next[...]
        above[...] = got_pair[...]

    own[: ANG * ROWS, :] = own_in[...]
    for q in range(PIECES):
        both = []
        for side, ref in (("above", above), ("below", below)):
            total = dot(ref[q * ANG], pack[0])
            for ti in range(1, ANG):
                total = total + dot(ref[q * ANG + ti], pack[ti])
            own[pl.ds(packed_piece(side, q), EDGE), :] = total.astype(jnp.bfloat16)
            both.append(total)
        share(both[0], both[1], to_left, to_right, q * EDGE)
    by_pair(to_left, to_right, send_pair, send_next)
    edges = {"above": above, "below": below}
    inner_sums(0, views, edges, inner, data_out, source_out, *scratch)


def unshare(blocks, pieces, high, out):
    def move(source, at, to, count, half):
        rows = source[pl.ds(at, count), :]
        if half != high:
            rows = pltpu.roll(rows.astype(F32), 64, 1).astype(jnp.bfloat16)
        out[pl.ds(to, count), :] = rows

    for p, pair in enumerate(PAIRS):
        for half, s in enumerate(pair):
            if s or not half:
                move(blocks, p * ROWS, (s + HALF) * ROWS, ROWS, half)
    for q in range(PIECES):
        for half, side in enumerate(("above", "below")):
            move(pieces, q * EDGE, packed_piece(side, q), EDGE, half)


def first_row(s):
    return D0 * s - 2 if s > 0 else EDGE - 2 + D0 * s


def own_row(s):
    return 0 if s > 0 else EDGE


def accumulate(s, warped, side, center, data, source):
    at = first_row(s)
    value = warped[pl.ds(at, OUT), :]
    slope = float(s) * (warped[pl.ds(at + 1, OUT), :] - warped[pl.ds(at - 1, OUT), :])
    if side is not None:
        side_part = side[pl.ds(at, OUT), :]
        slope = slope + side_part if s else side_part
    error = value - center
    robust = lax.rsqrt(1.0 + error * error)
    weighted = robust * slope
    return data + weighted * slope, source + weighted * error


def fill(slab, at, array):
    slab[pl.ds(at, array.shape[0]), :] = array


def zero_tails(slabs):
    for i in range(ANG):
        slabs[i, pl.ds(ROWS, SLAB - ROWS), :] = jnp.zeros((SLAB - ROWS, LANES), F32)


def fill_pieces(parts_of, outs):
    for (side, q), places in PLACES.items():
        parts = parts_of(side, q)
        for s, at in places:
            for out, part in zip(outs, parts):
                fill(out.at[s + HALF], at, part)


def halves(both):
    return both[:, :LANES], both[:, LANES:]


def shifted_views(matrix, own, piece, center, warped, side):
    span = range(-HALF, HALF + 1)
    rows = [own(s) for s in span] + [piece(name, q) for name, q in PLACES]
    both = dot(jnp.concatenate(rows, axis=0), matrix)
    first = {key: ANG * ROWS + i * EDGE for i, key in enumerate(PLACES)}

    def part(at, count):
        return both[at : at + count, :LANES], both[at : at + count, LANES:]

    fill_pieces(lambda name, q: part(first[name, q], EDGE), (warped, side))
    data = source = jnp.zeros((OUT, LANES), F32)
    for s in span:
        w, d = warped.at[s + HALF], side.at[s + HALF]
        shifted, slope = part((s + HALF) * ROWS, ROWS)
        fill(w, own_row(s), shifted)
        fill(d, own_row(s), slope)
        data, source = accumulate(s, w, d, center, data, source)
    return data, source


def inner_sums(tile, views, edges, inner, data_out, source_out, warped, side, center_ref):
    zero_tails(warped)
    zero_tails(side)
    lanes = slice(tile * LANES, (tile + 1) * LANES)
    fill_pieces(
        lambda name, q: (edges[name][q * ANG + HALF][:, lanes].astype(F32),), (warped,)
    )
    data = source = jnp.zeros((OUT, LANES), F32)
    for s in (0, -4, -3, -2, -1, 1, 2, 3, 4):
        w = warped.at[s + HALF]
        fill(w, own_row(s), views[(s + HALF) * ANG + HALF][:, lanes].astype(F32))
        if s == 0:
            center_ref[...] = w[pl.ds(first_row(0), OUT), :]
        data, source = accumulate(s, w, None, center_ref[...], data, source)
    data_out[...] = data
    source_out[...] = source

    def body(a, carry, sign):
        ti = HALF + 1 + a if sign else HALF - 1 - a
        data, source = shifted_views(
            inner[sign, a],
            lambda s: views[(s + HALF) * ANG + ti],
            lambda name, q: edges[name][q * ANG + ti],
            center_ref[...],
            warped,
            side,
        )
        data_out[...] += data
        source_out[...] += source
        return carry

    for sign in (0, 1):
        lax.fori_loop(0, HALF, functools.partial(body, sign=sign), 0)


def right_sums(views, above, below, inner, data_out, source_out, *scratch):
    edges = {"above": above, "below": below}
    inner_sums(1, views, edges, inner, data_out, source_out, *scratch)


def outer_sums(
    total_rows,
    total_cols,
    views,
    above,
    below,
    own,
    got_pair,
    got_next,
    got_piece_pair,
    got_piece_next,
    data_left,
    source_left,
    data_right,
    source_right,
    edge,
    edge_center,
    scatter,
    zed_out,
    near_out,
    next_out,
    precond_out,
    message,
    warped,
    side,
    center_ref,
    center_slab,
    left,
    right,
):
    even = is_even("col")

    @pl.when(even)
    def _():
        unshare(got_next, got_piece_next, 1, left)
        unshare(got_pair, got_piece_pair, 0, right)

    @pl.when(jnp.logical_not(even))
    def _():
        unshare(got_pair, got_piece_pair, 1, left)
        unshare(got_next, got_piece_next, 0, right)

    edges = {"above": above, "below": below}
    zero_tails(warped)
    zero_tails(side)
    zero = jnp.zeros((OUT, LANES), F32)

    def edge_rows(row, count):
        return jnp.concatenate([x[pl.ds(row, count), :] for x in (left, own, right)], axis=1)

    def fill_center(at, ref, row, count):
        fill(center_slab.at[0], at, ref[:, :LANES].astype(F32))
        fill(center_slab.at[1], at, ref[:, LANES:].astype(F32))
        around = (left[pl.ds(row, count), :], ref[...], right[pl.ds(row, count), :])
        both = dot(jnp.concatenate(around, axis=1), edge_center[...])
        fill(warped.at[HALF], at, both[:, :LANES])
        fill(center_slab.at[2], at, both[:, LANES:])

    for name in ("above", "below"):
        at = PLACES[name, 1][1][1]
        fill_center(at, edges[name].at[ANG + HALF], packed_piece(name, 1), EDGE)
    fill_center(EDGE, views.at[HALF * ANG + HALF], HALF * ROWS, ROWS)
    center_ref[...] = warped[HALF, pl.ds(first_row(0), OUT), :]
    sums = shifted_views(
        edge[...],
        lambda s: edge_rows((s + HALF) * ROWS, ROWS),
        lambda name, q: edge_rows(packed_piece(name, q), EDGE),
        center_ref[...],
        warped,
        side,
    )

    def total(inside, x):
        high = x.astype(jnp.bfloat16)
        rest = x - high.astype(F32)
        middle = rest.astype(jnp.bfloat16)
        low = (rest - middle.astype(F32)).astype(jnp.bfloat16)
        spread = dot(low, scatter[...]) + dot(middle, scatter[...]) + dot(high, scatter[...])
        return jnp.concatenate([inside[0][...], inside[1][...], zero], axis=1) + spread

    data_sum = total((data_left, data_right), sums[0])
    source_sum = total((source_left, source_right), sums[1])

    wide = 3 * LANES

    def before(x):
        return pltpu.roll(x, 1, 1)

    def after(x):
        return pltpu.roll(x, wide - 1, 1)

    def over(x):
        return pltpu.roll(x, 1, 0)

    def under(x):
        return pltpu.roll(x, OUT - 1, 0)

    at = first_row(0)
    here = jnp.concatenate([center_slab[i, pl.ds(at, OUT), :] for i in range(3)], axis=1)
    higher = jnp.concatenate([center_slab[i, pl.ds(at - 1, OUT), :] for i in range(3)], axis=1)
    lane = lax.broadcasted_iota(jnp.int32, (OUT, wide), 1)
    local_row = lax.broadcasted_iota(jnp.int32, (OUT, wide), 0) - 2
    column = jnp.where(lane < wide - 64, lane, lane - wide) + lax.axis_index("col") * COLS
    row = local_row + lax.axis_index("row") * ROWS
    across = here - before(here)
    vertical = here - higher
    h_left = jnp.where((column >= 1) & (column <= total_cols - 1), jnp.exp(-across * across), 0.0)
    v_up = jnp.where((row >= 1) & (row <= total_rows - 1), jnp.exp(-vertical * vertical), 0.0)
    h_right = after(h_left)
    v_down = under(v_up)
    coeff = DAMPING + data_sum * (0.25 / VIEWS)
    source = source_sum * (-0.5 / VIEWS)
    precond = coeff + SMOOTH * (h_left + h_right + v_up + v_down)
    inverse = 1.0 / precond

    def neighbours(x):
        total = h_left * before(x) + h_right * after(x) + v_up * over(x) + v_down * under(x)
        return SMOOTH * inverse * total

    zed = source * inverse
    near = neighbours(zed)
    nxt = neighbours(near)

    def block(x):
        return x[:, :COLS]

    zed, near, nxt, precond = block(zed), block(near), block(nxt), block(precond)
    zed_out[...] = zed
    near_out[...] = near
    next_out[...] = nxt
    precond_out[...] = precond
    mine = (block(local_row) >= 0) & (block(local_row) < ROWS)

    def inner(x, y):
        return jnp.sum(jnp.where(mine, precond * x * y, 0.0), keepdims=True)

    zz = inner(zed, zed)
    zn = inner(zed, near)
    kappa = jnp.clip(zn / jnp.where(zz > 0, zz, 1.0), -1.0, 1.0)
    y = near - kappa * zed
    g = nxt - kappa * near
    numbers = (
        (0, inner(y, y)),
        (1, inner(y, g)),
        (32, 2.0 * inner(y, zed)),
        (33, inner(y, near) + inner(zed, g)),
        (64, zz),
        (65, zn),
        (96, kappa),
        (97, kappa),
    )
    place = lax.broadcasted_iota(jnp.int32, (1, LANES), 1)
    out = jnp.zeros((1, LANES), F32)
    for where, number in numbers:
        out = jnp.where(place == where, number, out)
    message[...] = out


def finish(messages, zed_ref, near_ref, next_ref, precond_ref, increment, residual):
    all_of = messages[...]
    total = jnp.sum(all_of, axis=0, keepdims=True)
    zz = total[:, 64:65]
    zn = total[:, 65:66]
    kappa = zn / zz
    delta = pltpu.roll(all_of, 32, 1) - kappa
    linear = pltpu.roll(all_of, 96, 1)
    quad = pltpu.roll(all_of, 64, 1)
    moved = jnp.sum(all_of + delta * (linear + delta * quad), axis=0, keepdims=True)
    yy = moved[:, 0:1]
    yny = moved[:, 1:2]
    step0 = zz / (zz - zn)
    beta = step0 * step0 * yy / zz
    step1 = yy / (yy - yny - step0 * yy * yy / zz)
    rows = pl.ds(2, ROWS)
    zed = zed_ref[rows, :]
    near = near_ref[rows, :]
    nxt = next_ref[rows, :]
    y = near - kappa * zed
    g = nxt - kappa * near
    increment[...] = step0 * zed + step1 * (step0 * y + beta * zed)
    residual[...] = precond_ref[rows, :] * (
        step0 * y - step1 * (step0 * (y - g) + beta * (zed - near))
    )


def call(kernel, outs, scratch=(), name=None):
    return pl.pallas_call(
        kernel,
        out_shape=outs,
        scratch_shapes=list(scratch),
        compiler_params=pltpu.CompilerParams(vmem_limit_bytes=24 * 1024 * 1024),
        name=name,
    )


def swap(array, axis, start):
    pairs = []
    for i in range(start, lax.axis_size(axis) - 1, 2):
        pairs += [(i, i + 1), (i + 1, i)]
    return lax.ppermute(array, axis, pairs)


def shards(views):
    rows, cols = lax.axis_size("row"), lax.axis_size("col")
    left_inner, right_inner, edge_matrix, center, scatter = (jnp.asarray(x) for x in tables())
    bf16 = jnp.bfloat16
    struct = jax.ShapeDtypeStruct

    edge = struct((PIECES * ANG, EDGE, COLS), bf16)
    room = pltpu.VMEM(edge.shape, bf16)
    pair, after = call(pack_rows, (edge, edge), (room, room), name="pack_rows")(views)
    pair = swap(pair, "row", 0)
    after = swap(after, "row", 1)
    shared = struct((SHARED, LANES), bf16)
    room = pltpu.VMEM((SHARED, LANES), bf16)
    own, block_pair, block_next, pack = call(
        pack_own,
        (struct((ANG * ROWS, LANES), bf16), shared, shared, struct((ANG, COLS, LANES), bf16)),
        (room, room),
        name="pack_own",
    )(views)
    block_next = swap(block_next, "col", 1)
    block_pair = swap(block_pair, "col", 0)
    slab = pltpu.VMEM((ANG, SLAB, LANES), F32)
    tile = pltpu.VMEM((OUT, LANES), F32)
    sums = struct((OUT, LANES), F32)
    sent = struct((PIECES * EDGE, LANES), bf16)
    small = pltpu.VMEM((PIECES * EDGE, LANES), bf16)
    data_left, source_left, above, below, own, piece_pair, piece_next = call(
        pack_edges_and_left_sums,
        (sums, sums, edge, edge, struct((PACKED, LANES), bf16), sent, sent),
        (small, small, slab, slab, tile),
        name="left_sums",
    )(views, left_inner, pair, after, pack, own)
    piece_next = swap(piece_next, "col", 1)
    piece_pair = swap(piece_pair, "col", 0)
    data_right, source_right = call(
        right_sums, (sums, sums), (slab, slab, tile), name="right_sums"
    )(views, above, below, right_inner)
    field = struct((OUT, COLS), F32)
    zed, near, nxt, precond, message = call(
        functools.partial(outer_sums, rows * ROWS, cols * COLS),
        (field, field, field, field, struct((1, LANES), F32)),
        (
            slab,
            slab,
            tile,
            pltpu.VMEM((3, SLAB, LANES), F32),
            pltpu.VMEM((PACKED, LANES), bf16),
            pltpu.VMEM((PACKED, LANES), bf16),
        ),
        name="outer_sums",
    )(
        views, above, below, own, block_pair, block_next, piece_pair, piece_next,
        data_left, source_left, data_right, source_right, edge_matrix, center, scatter,
    )
    n = rows * cols
    messages = lax.all_to_all(
        jnp.broadcast_to(message[None], (n, 1, LANES)), ALL, 0, 0, tiled=True
    ).reshape(n, LANES)
    block = struct((ROWS, COLS), F32)
    return call(finish, (block, block), name="finish")(messages, zed, near, nxt, precond)


def solution(mesh):
    return jax.shard_map(
        shards,
        mesh=mesh,
        in_specs=(P(None, "row", "col"),),
        out_specs=(P("row", "col"), P("row", "col")),
        check_vma=False,
    )
```

```python
import functools

import jax
import jax.numpy as jnp
import ml_dtypes
import numpy as np
from jax import lax
from jax.experimental import pallas as pl
from jax.experimental.pallas import tpu as pltpu
from jax.sharding import PartitionSpec as P

ANG = 9
VIEWS = 81
HALF = ANG // 2
D0 = 3
ROWS = 64
COLS = 256
EDGE = 16
OUT = 72
SLAB = 96
PIECES = 3
PACKED = ANG * ROWS + 2 * PIECES * EDGE
PAIRS = ((-4, -3), (-2, -1), (1, 2), (3, 4))
SHARED = len(PAIRS) * ROWS
SENT = SHARED + PIECES * EDGE
SPARE = ((0, 0, 18, 45), (0, 18, 12, 109), (1, 30, 15, 45))
LANES = 128
SMOOTH = 2.0
DAMPING = 0.1
ALL = ("row", "col")
F32 = jnp.float32


def lane_first(t, c):
    return D0 * t * (t + 1) // 2 + c


def lane_last(t, c):
    a = abs(t)
    return 64 + D0 * a * (a + 1) // 2 + c - (COLS - D0 * a - D0)


def lane_here(t, c):
    return 45 + 2 * (-t - 1) + c if t < 0 else 109 + 2 * (t - 1) + c - (COLS - 2)


def edge_source(t, c):
    if c < 0:
        return lane_last(t, COLS + c)
    if c >= COLS:
        return 2 * LANES + lane_first(t, c - COLS)
    if t >= 0 and c <= D0 * t + D0 - 1:
        return LANES + lane_first(t, c)
    if t <= 0 and c >= COLS - D0 * abs(t) - D0:
        return LANES + lane_last(t, c)
    return LANES + lane_here(t, c)


def edge_pixels():
    for t in range(-HALF, HALF + 1):
        for column in range(-2, D0 * -t + 1 if t < 0 else 0):
            yield t, column
        for column in range(COLS - 1 - D0 * t if t > 0 else COLS, COLS + 2):
            yield t, column


def tables():
    inner = np.zeros((2, 2, HALF, COLS, 2 * LANES), np.float32)
    for tile in (0, 1):
        for a in range(1, HALF + 1):
            for sign in (0, 1):
                t = a if sign else -a
                for j in range(LANES):
                    c = tile * LANES + j + D0 * t
                    if 1 <= c < COLS - 1:
                        inner[tile, sign, a - 1, c, j] += 1
                        inner[tile, sign, a - 1, c + 1, LANES + j] += t
                        inner[tile, sign, a - 1, c - 1, LANES + j] -= t
    edge = np.zeros((3 * LANES, 2 * LANES), np.float32)
    center = np.zeros((LANES + COLS + LANES, 2 * LANES), np.float32)
    scatter = np.zeros((LANES, 3 * LANES), np.float32)

    def center_source(c):
        if c < 0:
            return lane_last(0, COLS + c)
        return LANES + c if c < COLS else LANES + COLS + lane_first(0, c - COLS)

    for lane, (t, col) in enumerate(edge_pixels()):
        c = col + D0 * t
        edge[edge_source(t, c), lane] += 1
        if t:
            edge[edge_source(t, c + 1), LANES + lane] += t
            edge[edge_source(t, c - 1), LANES + lane] -= t
        center[center_source(col), lane] = 1
        scatter[lane, col % (3 * LANES)] = 1
    for col in (-3, -2, -1, COLS, COLS + 1, COLS + 2):
        center[center_source(col), LANES + col % LANES] = 1
    return tuple(x.astype(ml_dtypes.bfloat16) for x in (*inner, edge, center, scatter))


def dot(a, b):
    return jnp.dot(a, b, preferred_element_type=F32)


def is_even(axis):
    return lax.rem(lax.axis_index(axis), 2) == 0


def pack_rows(views, send_pair, send_next, ups_out, downs_out):
    even = is_even("row")
    index = lax.broadcasted_iota(jnp.int32, (EDGE, COLS), 0)

    def put(ups, q, ti, rows):
        (ups_out if ups else downs_out)[q * ANG + ti] = rows.astype(jnp.bfloat16)

    for ti in range(ANG):

        def rows_of(s, start, ti=ti):
            return views[(s + HALF) * ANG + ti, pl.ds(start, EDGE), :].astype(F32)

        first = functools.partial(rows_of, start=0)
        last = functools.partial(rows_of, start=ROWS - EDGE)
        put(True, 0, ti, first(4))
        put(True, 1, ti, jnp.where(index < 12, first(3), pltpu.roll(first(0), 12, 0)))
        put(True, 2, ti, jnp.where(index < 9, first(2), pltpu.roll(first(1), 9, 0)))
        put(False, 0, ti, last(-4))
        put(False, 1, ti, jnp.where(index < 4, pltpu.roll(last(0), 4, 0), last(-3)))
        put(False, 2, ti, jnp.where(index < 7, pltpu.roll(last(-1), 7, 0), last(-2)))

    @pl.when(even)
    def _():
        send_pair[...] = downs_out[...]
        send_next[...] = ups_out[...]

    @pl.when(jnp.logical_not(even))
    def _():
        send_pair[...] = ups_out[...]
        send_next[...] = downs_out[...]


PLACES = {
    ("above", 0): ((-4, 0),),
    ("above", 1): ((-3, 0), (0, 12)),
    ("above", 2): ((-2, 0), (-1, 9)),
    ("below", 0): ((4, ROWS),),
    ("below", 1): ((3, ROWS), (0, EDGE + ROWS - 12)),
    ("below", 2): ((2, ROWS), (1, ROWS - 9)),
}


def packed_piece(side, q):
    return ANG * ROWS + ((0 if side == "above" else PIECES) + q) * EDGE


def share(first_of, second_of, to_left, to_right, at, spare=()):
    lane = lax.broadcasted_iota(jnp.int32, first_of.shape, 1)
    rows = pl.ds(at, first_of.shape[0])
    for out, turn in ((to_left, 0), (to_right, 64)):
        low = pltpu.roll(first_of, 64, 1) if turn else first_of
        high = second_of if turn else pltpu.roll(second_of, 64, 1)
        both = jnp.where(lane < 64, low, high)
        for pack, start, count, there in spare:
            moved = pltpu.roll(pack, (there - start - turn) % LANES, 1)
            both = jnp.where((lane >= there) & (lane < there + count), moved, both)
        out[rows, :] = both.astype(jnp.bfloat16)


def pack_own(views, own, to_left, to_right, pack):
    column = lax.broadcasted_iota(jnp.int32, (COLS, LANES), 0)
    lane = lax.broadcasted_iota(jnp.int32, (COLS, LANES), 1)
    for t in range(-HALF, HALF + 1):
        hit = jnp.zeros((COLS, LANES), F32)
        if t >= 0:
            bound = D0 * t + D0
            hit = jnp.where((column < bound) & (lane - column == lane_first(t, 0)), 1.0, hit)
        if t <= 0:
            start = COLS - D0 * abs(t) - D0
            apart = lane_last(t, start) - start
            hit = jnp.where((column >= start) & (lane - column == apart), 1.0, hit)
        if t:
            near = column < 2 if t < 0 else column >= COLS - 2
            apart = lane_here(t, 0)
            hit = jnp.where(near & (lane - column == apart), 1.0, hit)
        pack[t + HALF] = hit.astype(jnp.bfloat16)

    def packed(s):
        total = dot(views[(s + HALF) * ANG], pack[0])
        for ti in range(1, ANG):
            total = total + dot(views[(s + HALF) * ANG + ti], pack[ti])
        own[(s + HALF) * ROWS : (s + HALF + 1) * ROWS, :] = total.astype(jnp.bfloat16)
        return total

    middle = packed(0)
    for p, (low, high) in enumerate(PAIRS):
        spare = [(middle, *lanes) for q, *lanes in SPARE if q == p]
        share(packed(low), packed(high), to_left, to_right, p * ROWS, spare)


def pack_edges(
    got_pair, got_next, pack, own_in, left_in, right_in,
    above, below, own, send_pair, send_next, to_left, to_right,
):
    even = is_even("row")

    @pl.when(even)
    def _():
        below[...] = got_pair[...]
        above[...] = got_next[...]

    @pl.when(jnp.logical_not(even))
    def _():
        below[...] = got_next[...]
        above[...] = got_pair[...]

    own[: ANG * ROWS, :] = own_in[...]
    for q in range(PIECES):
        both = []
        for side, ref in (("above", above), ("below", below)):
            total = dot(ref[q * ANG], pack[0])
            for ti in range(1, ANG):
                total = total + dot(ref[q * ANG + ti], pack[ti])
            own[pl.ds(packed_piece(side, q), EDGE), :] = total.astype(jnp.bfloat16)
            both.append(total)
        share(both[0], both[1], to_left, to_right, q * EDGE)
    even = is_even("col")

    def send(out, block, piece):
        out[:SHARED, :] = block[...]
        out[SHARED:, :] = piece[...]

    @pl.when(even)
    def _():
        send(send_pair, right_in, to_right)
        send(send_next, left_in, to_left)

    @pl.when(jnp.logical_not(even))
    def _():
        send(send_pair, left_in, to_left)
        send(send_next, right_in, to_right)


def unshare(source, high, out):
    def rows_at(at, count):
        return source[pl.ds(at, count), :].astype(F32)

    def move(at, to, count, half):
        rows = rows_at(at, count)
        if half != high:
            rows = pltpu.roll(rows, 64, 1)
        out[pl.ds(to, count), :] = rows.astype(jnp.bfloat16)

    for p, pair in enumerate(PAIRS):
        for half, s in enumerate(pair):
            move(p * ROWS, (s + HALF) * ROWS, ROWS, half)
    for q in range(PIECES):
        for half, side in enumerate(("above", "below")):
            move(SHARED + q * EDGE, packed_piece(side, q), EDGE, half)
    lane = lax.broadcasted_iota(jnp.int32, (ROWS, LANES), 1)
    middle = jnp.zeros((ROWS, LANES), F32)
    for p, start, count, there in SPARE:
        at = start + 64 * high
        rows = pltpu.roll(rows_at(p * ROWS, ROWS), (at - there) % LANES, 1)
        middle = jnp.where((lane >= at) & (lane < at + count), rows, middle)
    out[pl.ds(HALF * ROWS, ROWS), :] = middle.astype(jnp.bfloat16)


def first_row(s):
    return D0 * s - 2 if s > 0 else EDGE - 2 + D0 * s


def own_row(s):
    return 0 if s > 0 else EDGE


def accumulate(s, warped, side, center, data, source):
    at = first_row(s)
    value = warped[pl.ds(at, OUT), :]
    slope = float(s) * (warped[pl.ds(at + 1, OUT), :] - warped[pl.ds(at - 1, OUT), :])
    if side is not None:
        side_part = side[pl.ds(at, OUT), :]
        slope = slope + side_part if s else side_part
    error = value - center
    robust = lax.rsqrt(1.0 + error * error)
    weighted = robust * slope
    return data + weighted * slope, source + weighted * error


def fill(slab, at, array):
    slab[pl.ds(at, array.shape[0]), :] = array


def zero_tails(slabs):
    for i in range(ANG):
        slabs[i, pl.ds(ROWS, SLAB - ROWS), :] = jnp.zeros((SLAB - ROWS, LANES), F32)


def fill_pieces(parts_of, outs):
    for (side, q), places in PLACES.items():
        parts = parts_of(side, q)
        for s, at in places:
            for out, part in zip(outs, parts):
                fill(out.at[s + HALF], at, part)


def halves(both):
    return both[:, :LANES], both[:, LANES:]


def shifted_views(matrix, own, piece, center, warped, side):
    span = range(-HALF, HALF + 1)
    rows = [own(s) for s in span] + [piece(name, q) for name, q in PLACES]
    both = dot(jnp.concatenate(rows, axis=0), matrix)
    first = {key: ANG * ROWS + i * EDGE for i, key in enumerate(PLACES)}

    def part(at, count):
        return both[at : at + count, :LANES], both[at : at + count, LANES:]

    fill_pieces(lambda name, q: part(first[name, q], EDGE), (warped, side))
    data = source = jnp.zeros((OUT, LANES), F32)
    for s in span:
        w, d = warped.at[s + HALF], side.at[s + HALF]
        shifted, slope = part((s + HALF) * ROWS, ROWS)
        fill(w, own_row(s), shifted)
        fill(d, own_row(s), slope)
        data, source = accumulate(s, w, d, center, data, source)
    return data, source


def inner_sums(tile, views, edges, inner, data_out, source_out, warped, side, center_ref):
    zero_tails(warped)
    zero_tails(side)
    lanes = slice(tile * LANES, (tile + 1) * LANES)
    fill_pieces(
        lambda name, q: (edges[name][q * ANG + HALF][:, lanes].astype(F32),), (warped,)
    )
    data = source = jnp.zeros((OUT, LANES), F32)
    for s in (0, -4, -3, -2, -1, 1, 2, 3, 4):
        w = warped.at[s + HALF]
        fill(w, own_row(s), views[(s + HALF) * ANG + HALF][:, lanes].astype(F32))
        if s == 0:
            center_ref[...] = w[pl.ds(first_row(0), OUT), :]
        data, source = accumulate(s, w, None, center_ref[...], data, source)
    data_out[...] = data
    source_out[...] = source

    def body(a, carry, sign):
        ti = HALF + 1 + a if sign else HALF - 1 - a
        data, source = shifted_views(
            inner[sign, a],
            lambda s: views[(s + HALF) * ANG + ti],
            lambda name, q: edges[name][q * ANG + ti],
            center_ref[...],
            warped,
            side,
        )
        data_out[...] += data
        source_out[...] += source
        return carry

    for sign in (0, 1):
        lax.fori_loop(0, HALF, functools.partial(body, sign=sign), 0)


def both_sums(views, above, below, left, right, data_out, source_out, *scratch):
    edges = {"above": above, "below": below}
    for tile, inner in enumerate((left, right)):
        inner_sums(tile, views, edges, inner, data_out.at[tile], source_out.at[tile], *scratch)


def outer_sums(
    total_rows,
    total_cols,
    views,
    above,
    below,
    own,
    got_next,
    got_pair,
    data_in,
    source_in,
    edge,
    edge_center,
    scatter,
    zed_out,
    near_out,
    next_out,
    precond_out,
    message,
    warped,
    side,
    center_ref,
    center_slab,
    left,
    right,
):
    even = is_even("col")

    @pl.when(even)
    def _():
        unshare(got_next, 1, left)
        unshare(got_pair, 0, right)

    @pl.when(jnp.logical_not(even))
    def _():
        unshare(got_pair, 1, left)
        unshare(got_next, 0, right)

    edges = {"above": above, "below": below}
    zero_tails(warped)
    zero_tails(side)
    zero = jnp.zeros((OUT, LANES), F32)

    def edge_rows(row, count):
        return jnp.concatenate([x[pl.ds(row, count), :] for x in (left, own, right)], axis=1)

    def fill_center(at, ref, row, count):
        fill(center_slab.at[0], at, ref[:, :LANES].astype(F32))
        fill(center_slab.at[1], at, ref[:, LANES:].astype(F32))
        around = (left[pl.ds(row, count), :], ref[...], right[pl.ds(row, count), :])
        both = dot(jnp.concatenate(around, axis=1), edge_center[...])
        fill(warped.at[HALF], at, both[:, :LANES])
        fill(center_slab.at[2], at, both[:, LANES:])

    for name in ("above", "below"):
        at = PLACES[name, 1][1][1]
        fill_center(at, edges[name].at[ANG + HALF], packed_piece(name, 1), EDGE)
    fill_center(EDGE, views.at[HALF * ANG + HALF], HALF * ROWS, ROWS)
    center_ref[...] = warped[HALF, pl.ds(first_row(0), OUT), :]
    sums = shifted_views(
        edge[...],
        lambda s: edge_rows((s + HALF) * ROWS, ROWS),
        lambda name, q: edge_rows(packed_piece(name, q), EDGE),
        center_ref[...],
        warped,
        side,
    )

    def total(inside, x):
        high = x.astype(jnp.bfloat16)
        rest = x - high.astype(F32)
        middle = rest.astype(jnp.bfloat16)
        low = (rest - middle.astype(F32)).astype(jnp.bfloat16)
        spread = dot(low, scatter[...]) + dot(middle, scatter[...]) + dot(high, scatter[...])
        return jnp.concatenate([inside[0], inside[1], zero], axis=1) + spread

    data_sum = total(data_in, sums[0])
    source_sum = total(source_in, sums[1])

    wide = 3 * LANES

    def before(x):
        return pltpu.roll(x, 1, 1)

    def after(x):
        return pltpu.roll(x, wide - 1, 1)

    def over(x):
        return pltpu.roll(x, 1, 0)

    def under(x):
        return pltpu.roll(x, OUT - 1, 0)

    at = first_row(0)
    here = jnp.concatenate([center_slab[i, pl.ds(at, OUT), :] for i in range(3)], axis=1)
    higher = jnp.concatenate([center_slab[i, pl.ds(at - 1, OUT), :] for i in range(3)], axis=1)
    lane = lax.broadcasted_iota(jnp.int32, (OUT, wide), 1)
    local_row = lax.broadcasted_iota(jnp.int32, (OUT, wide), 0) - 2
    column = jnp.where(lane < wide - 64, lane, lane - wide) + lax.axis_index("col") * COLS
    row = local_row + lax.axis_index("row") * ROWS
    across = here - before(here)
    vertical = here - higher
    h_left = jnp.where((column >= 1) & (column <= total_cols - 1), jnp.exp(-across * across), 0.0)
    v_up = jnp.where((row >= 1) & (row <= total_rows - 1), jnp.exp(-vertical * vertical), 0.0)
    h_right = after(h_left)
    v_down = under(v_up)
    coeff = DAMPING + data_sum * (0.25 / VIEWS)
    source = source_sum * (-0.5 / VIEWS)
    precond = coeff + SMOOTH * (h_left + h_right + v_up + v_down)
    inverse = 1.0 / precond

    def neighbours(x):
        total = h_left * before(x) + h_right * after(x) + v_up * over(x) + v_down * under(x)
        return SMOOTH * inverse * total

    zed = source * inverse
    near = neighbours(zed)
    nxt = neighbours(near)

    def block(x):
        return x[:, :COLS]

    zed, near, nxt, precond = block(zed), block(near), block(nxt), block(precond)
    zed_out[...] = zed
    near_out[...] = near
    next_out[...] = nxt
    precond_out[...] = precond
    mine = (block(local_row) >= 0) & (block(local_row) < ROWS)

    def inner(x, y):
        return jnp.sum(jnp.where(mine, precond * x * y, 0.0), keepdims=True)

    zz = inner(zed, zed)
    zn = inner(zed, near)
    kappa = jnp.clip(zn / jnp.where(zz > 0, zz, 1.0), -1.0, 1.0)
    y = near - kappa * zed
    g = nxt - kappa * near
    numbers = (
        (0, inner(y, y)),
        (1, inner(y, g)),
        (32, 2.0 * inner(y, zed)),
        (33, inner(y, near) + inner(zed, g)),
        (64, zz),
        (65, zn),
        (96, kappa),
        (97, kappa),
    )
    place = lax.broadcasted_iota(jnp.int32, (1, LANES), 1)
    out = jnp.zeros((1, LANES), F32)
    for where, number in numbers:
        out = jnp.where(place == where, number, out)
    message[...] = out


def finish(messages, zed_ref, near_ref, next_ref, precond_ref, increment, residual):
    all_of = messages[...]
    total = jnp.sum(all_of, axis=0, keepdims=True)
    zz = total[:, 64:65]
    zn = total[:, 65:66]
    kappa = zn / zz
    delta = pltpu.roll(all_of, 32, 1) - kappa
    linear = pltpu.roll(all_of, 96, 1)
    quad = pltpu.roll(all_of, 64, 1)
    moved = jnp.sum(all_of + delta * (linear + delta * quad), axis=0, keepdims=True)
    yy = moved[:, 0:1]
    yny = moved[:, 1:2]
    step0 = zz / (zz - zn)
    beta = step0 * step0 * yy / zz
    step1 = yy / (yy - yny - step0 * yy * yy / zz)
    rows = pl.ds(2, ROWS)
    zed = zed_ref[rows, :]
    near = near_ref[rows, :]
    nxt = next_ref[rows, :]
    y = near - kappa * zed
    g = nxt - kappa * near
    increment[...] = step0 * zed + step1 * (step0 * y + beta * zed)
    residual[...] = precond_ref[rows, :] * (
        step0 * y - step1 * (step0 * (y - g) + beta * (zed - near))
    )


def call(kernel, outs, scratch=(), name=None):
    return pl.pallas_call(
        kernel,
        out_shape=outs,
        scratch_shapes=list(scratch),
        compiler_params=pltpu.CompilerParams(vmem_limit_bytes=24 * 1024 * 1024),
        name=name,
    )


def swap(array, axis, start):
    pairs = []
    for i in range(start, lax.axis_size(axis) - 1, 2):
        pairs += [(i, i + 1), (i + 1, i)]
    return lax.ppermute(array, axis, pairs)


def shards(views):
    rows, cols = lax.axis_size("row"), lax.axis_size("col")
    left_inner, right_inner, edge_matrix, center, scatter = (jnp.asarray(x) for x in tables())
    bf16 = jnp.bfloat16
    struct = jax.ShapeDtypeStruct

    edge = struct((PIECES * ANG, EDGE, COLS), bf16)
    room = pltpu.VMEM(edge.shape, bf16)
    pair, after = call(pack_rows, (edge, edge), (room, room), name="pack_rows")(views)
    pair = swap(pair, "row", 0)
    after = swap(after, "row", 1)
    shared = struct((SHARED, LANES), bf16)
    own, to_left, to_right, pack = call(
        pack_own,
        (struct((ANG * ROWS, LANES), bf16), shared, shared, struct((ANG, COLS, LANES), bf16)),
        name="pack_own",
    )(views)
    sent = struct((SENT, LANES), bf16)
    small = pltpu.VMEM((PIECES * EDGE, LANES), bf16)
    above, below, own, pair, after = call(
        pack_edges,
        (edge, edge, struct((PACKED, LANES), bf16), sent, sent),
        (small, small),
        name="pack_edges",
    )(pair, after, pack, own, to_left, to_right)
    after = swap(after, "col", 1)
    pair = swap(pair, "col", 0)
    slab = pltpu.VMEM((ANG, SLAB, LANES), F32)
    tile = pltpu.VMEM((OUT, LANES), F32)
    sums = struct((2, OUT, LANES), F32)
    data, source = call(both_sums, (sums, sums), (slab, slab, tile), name="inner_sums")(
        views, above, below, left_inner, right_inner
    )
    field = struct((OUT, COLS), F32)
    zed, near, nxt, precond, message = call(
        functools.partial(outer_sums, rows * ROWS, cols * COLS),
        (field, field, field, field, struct((1, LANES), F32)),
        (
            slab,
            slab,
            tile,
            pltpu.VMEM((3, SLAB, LANES), F32),
            pltpu.VMEM((PACKED, LANES), bf16),
            pltpu.VMEM((PACKED, LANES), bf16),
        ),
        name="outer_sums",
    )(views, above, below, own, after, pair, data, source, edge_matrix, center, scatter)
    n = rows * cols
    messages = lax.all_to_all(
        jnp.broadcast_to(message[None], (n, 1, LANES)), ALL, 0, 0, tiled=True
    ).reshape(n, LANES)
    block = struct((ROWS, COLS), F32)
    return call(finish, (block, block), name="finish")(messages, zed, near, nxt, precond)


def solution(mesh):
    return jax.shard_map(
        shards,
        mesh=mesh,
        in_specs=(P(None, "row", "col"),),
        out_specs=(P("row", "col"), P("row", "col")),
        check_vma=False,
    )
```

```python
import functools

import jax
import jax.numpy as jnp
import ml_dtypes
import numpy as np
from jax import lax
from jax.experimental import pallas as pl
from jax.experimental.pallas import tpu as pltpu
from jax.sharding import PartitionSpec as P

ANG = 9
VIEWS = 81
HALF = ANG // 2
D0 = 3
ROWS = 64
COLS = 256
EDGE = 16
OUT = 72
SLAB = 96
PIECES = 3
PACKED = ANG * ROWS + 2 * PIECES * EDGE
PAIRS = ((-4, -3), (-2, -1), (1, 2), (3, 4))
SHARED = len(PAIRS) * ROWS
CUTS = ((0, 18), (18, 12), (30, 15))
SPARE = tuple((p, *cut, there) for cut, (p, there) in zip(CUTS, ((0, 45), (0, 109), (1, 45))))
LANES = 128
SMOOTH = 2.0
DAMPING = 0.1
ALL = ("row", "col")
F32 = jnp.float32


def lane_first(t, c):
    return D0 * t * (t + 1) // 2 + c


def lane_last(t, c):
    a = abs(t)
    return 64 + D0 * a * (a + 1) // 2 + c - (COLS - D0 * a - D0)


def lane_here(t, c):
    return 45 + 2 * (-t - 1) + c if t < 0 else 109 + 2 * (t - 1) + c - (COLS - 2)


def edge_source(t, c):
    if c < 0:
        return lane_last(t, COLS + c)
    if c >= COLS:
        return 2 * LANES + lane_first(t, c - COLS)
    if t >= 0 and c <= D0 * t + D0 - 1:
        return LANES + lane_first(t, c)
    if t <= 0 and c >= COLS - D0 * abs(t) - D0:
        return LANES + lane_last(t, c)
    return LANES + lane_here(t, c)


def edge_pixels():
    for t in range(-HALF, HALF + 1):
        for column in range(-2, D0 * -t + 1 if t < 0 else 0):
            yield t, column
        for column in range(COLS - 1 - D0 * t if t > 0 else COLS, COLS + 2):
            yield t, column


def tables():
    inner = np.zeros((2, 2, HALF, COLS, 2 * LANES), np.float32)
    for tile in (0, 1):
        for a in range(1, HALF + 1):
            for sign in (0, 1):
                t = a if sign else -a
                for j in range(LANES):
                    c = tile * LANES + j + D0 * t
                    if 1 <= c < COLS - 1:
                        inner[tile, sign, a - 1, c, j] += 1
                        inner[tile, sign, a - 1, c + 1, LANES + j] += t
                        inner[tile, sign, a - 1, c - 1, LANES + j] -= t
    edge = np.zeros((3 * LANES, 2 * LANES), np.float32)
    center = np.zeros((LANES + COLS + LANES, 2 * LANES), np.float32)
    scatter = np.zeros((LANES, 3 * LANES), np.float32)

    def center_source(c):
        if c < 0:
            return lane_last(0, COLS + c)
        return LANES + c if c < COLS else LANES + COLS + lane_first(0, c - COLS)

    for lane, (t, col) in enumerate(edge_pixels()):
        c = col + D0 * t
        edge[edge_source(t, c), lane] += 1
        if t:
            edge[edge_source(t, c + 1), LANES + lane] += t
            edge[edge_source(t, c - 1), LANES + lane] -= t
        center[center_source(col), lane] = 1
        scatter[lane, col % (3 * LANES)] = 1
    for col in (-3, -2, -1, COLS, COLS + 1, COLS + 2):
        center[center_source(col), LANES + col % LANES] = 1
    return tuple(x.astype(ml_dtypes.bfloat16) for x in (*inner, edge, center, scatter))


def dot(a, b):
    return jnp.dot(a, b, preferred_element_type=F32)


def is_even(axis):
    return lax.rem(lax.axis_index(axis), 2) == 0


def pack_rows(views, send_pair, send_next, ups_out, downs_out):
    even = is_even("row")
    index = lax.broadcasted_iota(jnp.int32, (EDGE, COLS), 0)

    def put(ups, q, ti, rows):
        (ups_out if ups else downs_out)[q * ANG + ti] = rows.astype(jnp.bfloat16)

    for ti in range(ANG):

        def rows_of(s, start, ti=ti):
            return views[(s + HALF) * ANG + ti, pl.ds(start, EDGE), :].astype(F32)

        first = functools.partial(rows_of, start=0)
        last = functools.partial(rows_of, start=ROWS - EDGE)
        put(True, 0, ti, first(4))
        put(True, 1, ti, jnp.where(index < 12, first(3), pltpu.roll(first(0), 12, 0)))
        put(True, 2, ti, jnp.where(index < 9, first(2), pltpu.roll(first(1), 9, 0)))
        put(False, 0, ti, last(-4))
        put(False, 1, ti, jnp.where(index < 4, pltpu.roll(last(0), 4, 0), last(-3)))
        put(False, 2, ti, jnp.where(index < 7, pltpu.roll(last(-1), 7, 0), last(-2)))

    @pl.when(even)
    def _():
        send_pair[...] = downs_out[...]
        send_next[...] = ups_out[...]

    @pl.when(jnp.logical_not(even))
    def _():
        send_pair[...] = ups_out[...]
        send_next[...] = downs_out[...]


PLACES = {
    ("above", 0): ((-4, 0),),
    ("above", 1): ((-3, 0), (0, 12)),
    ("above", 2): ((-2, 0), (-1, 9)),
    ("below", 0): ((4, ROWS),),
    ("below", 1): ((3, ROWS), (0, EDGE + ROWS - 12)),
    ("below", 2): ((2, ROWS), (1, ROWS - 9)),
}


def packed_piece(side, q):
    return ANG * ROWS + ((0 if side == "above" else PIECES) + q) * EDGE


def piece_places():
    slots = ((1, 109), (2, 45), (2, 109), (3, 45), (3, 109))
    places = {}
    for n, (name, cut) in enumerate((name, cut) for name in PLACES for cut in CUTS):
        p, there = slots[n % len(slots)]
        row = p * ROWS + n // len(slots) * EDGE
        places.setdefault(name, []).append((row, *cut, there))
    return places


def share(first_of, second_of, to_left, to_right, at, spare=()):
    lane = lax.broadcasted_iota(jnp.int32, first_of.shape, 1)
    rows = pl.ds(at, first_of.shape[0])
    for out, turn in ((to_left, 0), (to_right, 64)):
        low = pltpu.roll(first_of, 64, 1) if turn else first_of
        high = second_of if turn else pltpu.roll(second_of, 64, 1)
        both = jnp.where(lane < 64, low, high)
        for pack, start, count, there in spare:
            moved = pltpu.roll(pack, (there - start - turn) % LANES, 1)
            both = jnp.where((lane >= there) & (lane < there + count), moved, both)
        out[rows, :] = both.astype(jnp.bfloat16)


def pack_own(views, own, to_left, to_right, pack):
    column = lax.broadcasted_iota(jnp.int32, (COLS, LANES), 0)
    lane = lax.broadcasted_iota(jnp.int32, (COLS, LANES), 1)
    for t in range(-HALF, HALF + 1):
        hit = jnp.zeros((COLS, LANES), F32)
        if t >= 0:
            bound = D0 * t + D0
            hit = jnp.where((column < bound) & (lane - column == lane_first(t, 0)), 1.0, hit)
        if t <= 0:
            start = COLS - D0 * abs(t) - D0
            apart = lane_last(t, start) - start
            hit = jnp.where((column >= start) & (lane - column == apart), 1.0, hit)
        if t:
            near = column < 2 if t < 0 else column >= COLS - 2
            apart = lane_here(t, 0)
            hit = jnp.where(near & (lane - column == apart), 1.0, hit)
        pack[t + HALF] = hit.astype(jnp.bfloat16)

    def packed(s):
        total = dot(views[(s + HALF) * ANG], pack[0])
        for ti in range(1, ANG):
            total = total + dot(views[(s + HALF) * ANG + ti], pack[ti])
        own[(s + HALF) * ROWS : (s + HALF + 1) * ROWS, :] = total.astype(jnp.bfloat16)
        return total

    middle = packed(0)
    for p, (low, high) in enumerate(PAIRS):
        spare = [(middle, *lanes) for q, *lanes in SPARE if q == p]
        share(packed(low), packed(high), to_left, to_right, p * ROWS, spare)


def pack_edges(
    got_pair, got_next, pack, own_in, left_in, right_in,
    above, below, own, send_pair, send_next, to_left, to_right,
):
    even = is_even("row")

    @pl.when(even)
    def _():
        below[...] = got_pair[...]
        above[...] = got_next[...]

    @pl.when(jnp.logical_not(even))
    def _():
        below[...] = got_next[...]
        above[...] = got_pair[...]

    own[: ANG * ROWS, :] = own_in[...]
    edges = {"above": above, "below": below}
    total = jnp.zeros((len(PLACES) * EDGE, LANES), F32)
    for ti in range(ANG):
        rows = [edges[side][q * ANG + ti] for side, q in PLACES]
        total = total + dot(jnp.concatenate(rows, axis=0), pack[ti])
    parts = {}
    places = piece_places()
    for i, (side, q) in enumerate(PLACES):
        piece = total[i * EDGE : (i + 1) * EDGE]
        own[pl.ds(packed_piece(side, q), EDGE), :] = piece.astype(jnp.bfloat16)
        for row, *lanes in places[side, q]:
            parts.setdefault(row, []).append((piece, *lanes))
    lane = lax.broadcasted_iota(jnp.int32, (EDGE, LANES), 1)
    for out, block, turn in ((to_left, left_in, 0), (to_right, right_in, 64)):
        out[...] = block[...]
        for row, group in parts.items():
            both = block[row : row + EDGE, :].astype(F32)
            for piece, start, count, there in group:
                moved = pltpu.roll(piece, (there - start - turn) % LANES, 1)
                both = jnp.where((lane >= there) & (lane < there + count), moved, both)
            out[row : row + EDGE, :] = both.astype(jnp.bfloat16)
    even = is_even("col")

    @pl.when(even)
    def _():
        send_pair[...] = to_right[...]
        send_next[...] = to_left[...]

    @pl.when(jnp.logical_not(even))
    def _():
        send_pair[...] = to_left[...]
        send_next[...] = to_right[...]


def unshare(source, high, out):
    def rows_at(at, count):
        return source[pl.ds(at, count), :].astype(F32)

    for p, pair in enumerate(PAIRS):
        for half, s in enumerate(pair):
            rows = rows_at(p * ROWS, ROWS)
            if half != high:
                rows = pltpu.roll(rows, 64, 1)
            out[pl.ds((s + HALF) * ROWS, ROWS), :] = rows.astype(jnp.bfloat16)

    def join(parts, to, count):
        lane = lax.broadcasted_iota(jnp.int32, (count, LANES), 1)
        whole = jnp.zeros((count, LANES), F32)
        for row, start, lanes, there in parts:
            at = start + 64 * high
            rows = pltpu.roll(rows_at(row, count), (at - there) % LANES, 1)
            whole = jnp.where((lane >= at) & (lane < at + lanes), rows, whole)
        out[pl.ds(to, count), :] = whole.astype(jnp.bfloat16)

    join([(p * ROWS, *lanes) for p, *lanes in SPARE], HALF * ROWS, ROWS)
    for (side, q), parts in piece_places().items():
        join(parts, packed_piece(side, q), EDGE)


def first_row(s):
    return D0 * s - 2 if s > 0 else EDGE - 2 + D0 * s


def own_row(s):
    return 0 if s > 0 else EDGE


def accumulate(s, warped, side, center, data, source):
    at = first_row(s)
    value = warped[pl.ds(at, OUT), :]
    slope = float(s) * (warped[pl.ds(at + 1, OUT), :] - warped[pl.ds(at - 1, OUT), :])
    if side is not None:
        side_part = side[pl.ds(at, OUT), :]
        slope = slope + side_part if s else side_part
    error = value - center
    robust = lax.rsqrt(1.0 + error * error)
    weighted = robust * slope
    return data + weighted * slope, source + weighted * error


def fill(slab, at, array):
    slab[pl.ds(at, array.shape[0]), :] = array


def zero_tails(slabs):
    for i in range(ANG):
        slabs[i, pl.ds(ROWS, SLAB - ROWS), :] = jnp.zeros((SLAB - ROWS, LANES), F32)


def fill_pieces(parts_of, outs):
    for (side, q), places in PLACES.items():
        parts = parts_of(side, q)
        for s, at in places:
            for out, part in zip(outs, parts):
                fill(out.at[s + HALF], at, part)


def halves(both):
    return both[:, :LANES], both[:, LANES:]


def shifted_views(matrix, own, piece, center, warped, side):
    span = range(-HALF, HALF + 1)
    rows = [own(s) for s in span] + [piece(name, q) for name, q in PLACES]
    both = dot(jnp.concatenate(rows, axis=0), matrix)
    first = {key: ANG * ROWS + i * EDGE for i, key in enumerate(PLACES)}

    def part(at, count):
        return both[at : at + count, :LANES], both[at : at + count, LANES:]

    fill_pieces(lambda name, q: part(first[name, q], EDGE), (warped, side))
    data = source = jnp.zeros((OUT, LANES), F32)
    for s in span:
        w, d = warped.at[s + HALF], side.at[s + HALF]
        shifted, slope = part((s + HALF) * ROWS, ROWS)
        fill(w, own_row(s), shifted)
        fill(d, own_row(s), slope)
        data, source = accumulate(s, w, d, center, data, source)
    return data, source


def inner_sums(tile, views, edges, inner, data_out, source_out, warped, side, center_ref):
    zero_tails(warped)
    zero_tails(side)
    lanes = slice(tile * LANES, (tile + 1) * LANES)
    fill_pieces(
        lambda name, q: (edges[name][q * ANG + HALF][:, lanes].astype(F32),), (warped,)
    )
    data = source = jnp.zeros((OUT, LANES), F32)
    for s in (0, -4, -3, -2, -1, 1, 2, 3, 4):
        w = warped.at[s + HALF]
        fill(w, own_row(s), views[(s + HALF) * ANG + HALF][:, lanes].astype(F32))
        if s == 0:
            center_ref[...] = w[pl.ds(first_row(0), OUT), :]
        data, source = accumulate(s, w, None, center_ref[...], data, source)
    data_out[...] = data
    source_out[...] = source

    def body(a, carry, sign):
        ti = HALF + 1 + a if sign else HALF - 1 - a
        data, source = shifted_views(
            inner[sign, a],
            lambda s: views[(s + HALF) * ANG + ti],
            lambda name, q: edges[name][q * ANG + ti],
            center_ref[...],
            warped,
            side,
        )
        data_out[...] += data
        source_out[...] += source
        return carry

    for sign in (0, 1):
        lax.fori_loop(0, HALF, functools.partial(body, sign=sign), 0)


def both_sums(views, above, below, left, right, data_out, source_out, *scratch):
    edges = {"above": above, "below": below}
    for tile, inner in enumerate((left, right)):
        inner_sums(tile, views, edges, inner, data_out.at[tile], source_out.at[tile], *scratch)


def outer_sums(
    total_rows,
    total_cols,
    views,
    above,
    below,
    own,
    got_next,
    got_pair,
    data_in,
    source_in,
    edge,
    edge_center,
    scatter,
    zed_out,
    near_out,
    next_out,
    precond_out,
    message,
    warped,
    side,
    center_ref,
    center_slab,
    left,
    right,
):
    even = is_even("col")

    @pl.when(even)
    def _():
        unshare(got_next, 1, left)
        unshare(got_pair, 0, right)

    @pl.when(jnp.logical_not(even))
    def _():
        unshare(got_pair, 1, left)
        unshare(got_next, 0, right)

    edges = {"above": above, "below": below}
    zero_tails(warped)
    zero_tails(side)
    zero = jnp.zeros((OUT, LANES), F32)

    def edge_rows(row, count):
        return jnp.concatenate([x[pl.ds(row, count), :] for x in (left, own, right)], axis=1)

    def fill_center(at, ref, row, count):
        fill(center_slab.at[0], at, ref[:, :LANES].astype(F32))
        fill(center_slab.at[1], at, ref[:, LANES:].astype(F32))
        around = (left[pl.ds(row, count), :], ref[...], right[pl.ds(row, count), :])
        both = dot(jnp.concatenate(around, axis=1), edge_center[...])
        fill(warped.at[HALF], at, both[:, :LANES])
        fill(center_slab.at[2], at, both[:, LANES:])

    for name in ("above", "below"):
        at = PLACES[name, 1][1][1]
        fill_center(at, edges[name].at[ANG + HALF], packed_piece(name, 1), EDGE)
    fill_center(EDGE, views.at[HALF * ANG + HALF], HALF * ROWS, ROWS)
    center_ref[...] = warped[HALF, pl.ds(first_row(0), OUT), :]
    sums = shifted_views(
        edge[...],
        lambda s: edge_rows((s + HALF) * ROWS, ROWS),
        lambda name, q: edge_rows(packed_piece(name, q), EDGE),
        center_ref[...],
        warped,
        side,
    )

    def total(inside, x):
        high = x.astype(jnp.bfloat16)
        rest = x - high.astype(F32)
        middle = rest.astype(jnp.bfloat16)
        low = (rest - middle.astype(F32)).astype(jnp.bfloat16)
        spread = dot(low, scatter[...]) + dot(middle, scatter[...]) + dot(high, scatter[...])
        return jnp.concatenate([inside[0], inside[1], zero], axis=1) + spread

    data_sum = total(data_in, sums[0])
    source_sum = total(source_in, sums[1])

    wide = 3 * LANES

    def before(x):
        return pltpu.roll(x, 1, 1)

    def after(x):
        return pltpu.roll(x, wide - 1, 1)

    def over(x):
        return pltpu.roll(x, 1, 0)

    def under(x):
        return pltpu.roll(x, OUT - 1, 0)

    at = first_row(0)
    here = jnp.concatenate([center_slab[i, pl.ds(at, OUT), :] for i in range(3)], axis=1)
    higher = jnp.concatenate([center_slab[i, pl.ds(at - 1, OUT), :] for i in range(3)], axis=1)
    lane = lax.broadcasted_iota(jnp.int32, (OUT, wide), 1)
    local_row = lax.broadcasted_iota(jnp.int32, (OUT, wide), 0) - 2
    column = jnp.where(lane < wide - 64, lane, lane - wide) + lax.axis_index("col") * COLS
    row = local_row + lax.axis_index("row") * ROWS
    across = here - before(here)
    vertical = here - higher
    h_left = jnp.where((column >= 1) & (column <= total_cols - 1), jnp.exp(-across * across), 0.0)
    v_up = jnp.where((row >= 1) & (row <= total_rows - 1), jnp.exp(-vertical * vertical), 0.0)
    h_right = after(h_left)
    v_down = under(v_up)
    coeff = DAMPING + data_sum * (0.25 / VIEWS)
    source = source_sum * (-0.5 / VIEWS)
    precond = coeff + SMOOTH * (h_left + h_right + v_up + v_down)
    inverse = 1.0 / precond

    def neighbours(x):
        total = h_left * before(x) + h_right * after(x) + v_up * over(x) + v_down * under(x)
        return SMOOTH * inverse * total

    zed = source * inverse
    near = neighbours(zed)
    nxt = neighbours(near)

    def block(x):
        return x[:, :COLS]

    zed, near, nxt, precond = block(zed), block(near), block(nxt), block(precond)
    zed_out[...] = zed
    near_out[...] = near
    next_out[...] = nxt
    precond_out[...] = precond
    mine = (block(local_row) >= 0) & (block(local_row) < ROWS)

    def inner(x, y):
        return jnp.sum(jnp.where(mine, precond * x * y, 0.0), keepdims=True)

    zz = inner(zed, zed)
    zn = inner(zed, near)
    kappa = jnp.clip(zn / jnp.where(zz > 0, zz, 1.0), -1.0, 1.0)
    y = near - kappa * zed
    g = nxt - kappa * near
    numbers = (
        (0, inner(y, y)),
        (1, inner(y, g)),
        (32, 2.0 * inner(y, zed)),
        (33, inner(y, near) + inner(zed, g)),
        (64, zz),
        (65, zn),
        (96, kappa),
        (97, kappa),
    )
    place = lax.broadcasted_iota(jnp.int32, (1, LANES), 1)
    out = jnp.zeros((1, LANES), F32)
    for where, number in numbers:
        out = jnp.where(place == where, number, out)
    message[...] = out


def finish(messages, zed_ref, near_ref, next_ref, precond_ref, increment, residual):
    all_of = messages[...]
    total = jnp.sum(all_of, axis=0, keepdims=True)
    zz = total[:, 64:65]
    zn = total[:, 65:66]
    kappa = zn / zz
    delta = pltpu.roll(all_of, 32, 1) - kappa
    linear = pltpu.roll(all_of, 96, 1)
    quad = pltpu.roll(all_of, 64, 1)
    moved = jnp.sum(all_of + delta * (linear + delta * quad), axis=0, keepdims=True)
    yy = moved[:, 0:1]
    yny = moved[:, 1:2]
    step0 = zz / (zz - zn)
    beta = step0 * step0 * yy / zz
    step1 = yy / (yy - yny - step0 * yy * yy / zz)
    rows = pl.ds(2, ROWS)
    zed = zed_ref[rows, :]
    near = near_ref[rows, :]
    nxt = next_ref[rows, :]
    y = near - kappa * zed
    g = nxt - kappa * near
    increment[...] = step0 * zed + step1 * (step0 * y + beta * zed)
    residual[...] = precond_ref[rows, :] * (
        step0 * y - step1 * (step0 * (y - g) + beta * (zed - near))
    )


def call(kernel, outs, scratch=(), name=None):
    return pl.pallas_call(
        kernel,
        out_shape=outs,
        scratch_shapes=list(scratch),
        compiler_params=pltpu.CompilerParams(vmem_limit_bytes=24 * 1024 * 1024),
        name=name,
    )


def swap(array, axis, start):
    pairs = []
    for i in range(start, lax.axis_size(axis) - 1, 2):
        pairs += [(i, i + 1), (i + 1, i)]
    return lax.ppermute(array, axis, pairs)


def shards(views):
    rows, cols = lax.axis_size("row"), lax.axis_size("col")
    left_inner, right_inner, edge_matrix, center, scatter = (jnp.asarray(x) for x in tables())
    bf16 = jnp.bfloat16
    struct = jax.ShapeDtypeStruct

    edge = struct((PIECES * ANG, EDGE, COLS), bf16)
    room = pltpu.VMEM(edge.shape, bf16)
    pair, after = call(pack_rows, (edge, edge), (room, room), name="pack_rows")(views)
    pair = swap(pair, "row", 0)
    after = swap(after, "row", 1)
    shared = struct((SHARED, LANES), bf16)
    own, to_left, to_right, pack = call(
        pack_own,
        (struct((ANG * ROWS, LANES), bf16), shared, shared, struct((ANG, COLS, LANES), bf16)),
        name="pack_own",
    )(views)
    room = pltpu.VMEM(shared.shape, bf16)
    above, below, own, pair, after = call(
        pack_edges,
        (edge, edge, struct((PACKED, LANES), bf16), shared, shared),
        (room, room),
        name="pack_edges",
    )(pair, after, pack, own, to_left, to_right)
    after = swap(after, "col", 1)
    pair = swap(pair, "col", 0)
    slab = pltpu.VMEM((ANG, SLAB, LANES), F32)
    tile = pltpu.VMEM((OUT, LANES), F32)
    sums = struct((2, OUT, LANES), F32)
    data, source = call(both_sums, (sums, sums), (slab, slab, tile), name="inner_sums")(
        views, above, below, left_inner, right_inner
    )
    field = struct((OUT, COLS), F32)
    zed, near, nxt, precond, message = call(
        functools.partial(outer_sums, rows * ROWS, cols * COLS),
        (field, field, field, field, struct((1, LANES), F32)),
        (
            slab,
            slab,
            tile,
            pltpu.VMEM((3, SLAB, LANES), F32),
            pltpu.VMEM((PACKED, LANES), bf16),
            pltpu.VMEM((PACKED, LANES), bf16),
        ),
        name="outer_sums",
    )(views, above, below, own, after, pair, data, source, edge_matrix, center, scatter)
    n = rows * cols
    messages = lax.all_to_all(
        jnp.broadcast_to(message[None], (n, 1, LANES)), ALL, 0, 0, tiled=True
    ).reshape(n, LANES)
    block = struct((ROWS, COLS), F32)
    return call(finish, (block, block), name="finish")(messages, zed, near, nxt, precond)


def solution(mesh):
    return jax.shard_map(
        shards,
        mesh=mesh,
        in_specs=(P(None, "row", "col"),),
        out_specs=(P("row", "col"), P("row", "col")),
        check_vma=False,
    )
```

```python
import functools

import jax
import jax.numpy as jnp
import ml_dtypes
import numpy as np
from jax import lax
from jax.experimental import pallas as pl
from jax.experimental.pallas import tpu as pltpu
from jax.sharding import PartitionSpec as P

ANG = 9
VIEWS = 81
HALF = ANG // 2
D0 = 3
ROWS = 64
COLS = 256
EDGE = 16
OUT = 72
SLAB = 96
PIECES = 3
PACKED = ANG * ROWS + 2 * PIECES * EDGE
PAIRS = ((-4, -3), (-2, -1), (1, 2), (3, 4))
SHARED = len(PAIRS) * ROWS
CUTS = ((0, 18), (18, 12), (30, 15))
SPARE = tuple((p, *cut, there) for cut, (p, there) in zip(CUTS, ((0, 45), (0, 109), (1, 45))))
LANES = 128
SMOOTH = 2.0
DAMPING = 0.1
ALL = ("row", "col")
F32 = jnp.float32


def lane_first(t, c):
    return D0 * t * (t + 1) // 2 + c


def lane_last(t, c):
    a = abs(t)
    return 64 + D0 * a * (a + 1) // 2 + c - (COLS - D0 * a - D0)


def lane_here(t, c):
    return 45 + 2 * (-t - 1) + c if t < 0 else 109 + 2 * (t - 1) + c - (COLS - 2)


def edge_source(t, c):
    if c < 0:
        return lane_last(t, COLS + c)
    if c >= COLS:
        return 2 * LANES + lane_first(t, c - COLS)
    if t >= 0 and c <= D0 * t + D0 - 1:
        return LANES + lane_first(t, c)
    if t <= 0 and c >= COLS - D0 * abs(t) - D0:
        return LANES + lane_last(t, c)
    return LANES + lane_here(t, c)


def edge_pixels():
    for t in range(-HALF, HALF + 1):
        for column in range(-2, D0 * -t + 1 if t < 0 else 0):
            yield t, column
        for column in range(COLS - 1 - D0 * t if t > 0 else COLS, COLS + 2):
            yield t, column


def tables():
    inner = np.zeros((2, 2, HALF, COLS, 2 * LANES), np.float32)
    for tile in (0, 1):
        for a in range(1, HALF + 1):
            for sign in (0, 1):
                t = a if sign else -a
                for j in range(LANES):
                    c = tile * LANES + j + D0 * t
                    if 1 <= c < COLS - 1:
                        inner[tile, sign, a - 1, c, j] += 1
                        inner[tile, sign, a - 1, c + 1, LANES + j] += t
                        inner[tile, sign, a - 1, c - 1, LANES + j] -= t
    edge = np.zeros((3 * LANES, 2 * LANES), np.float32)
    center = np.zeros((LANES + COLS + LANES, 2 * LANES), np.float32)
    scatter = np.zeros((LANES, 3 * LANES), np.float32)

    def center_source(c):
        if c < 0:
            return lane_last(0, COLS + c)
        return LANES + c if c < COLS else LANES + COLS + lane_first(0, c - COLS)

    for lane, (t, col) in enumerate(edge_pixels()):
        c = col + D0 * t
        edge[edge_source(t, c), lane] += 1
        if t:
            edge[edge_source(t, c + 1), LANES + lane] += t
            edge[edge_source(t, c - 1), LANES + lane] -= t
        center[center_source(col), lane] = 1
        scatter[lane, col % (3 * LANES)] = 1
    for col in (-3, -2, -1, COLS, COLS + 1, COLS + 2):
        center[center_source(col), LANES + col % LANES] = 1
    return tuple(x.astype(ml_dtypes.bfloat16) for x in (*inner, edge, center, scatter))


def dot(a, b):
    return jnp.dot(a, b, preferred_element_type=F32)


def is_even(axis):
    return lax.rem(lax.axis_index(axis), 2) == 0


def pack_rows(views, send_pair, send_next, tops, bottoms, ups, downs, sems):
    count = (HALF + 1) * ANG
    get_tops = pltpu.make_async_copy(
        views.at[pl.ds(HALF * ANG, count), pl.ds(0, EDGE)], tops, sems.at[0]
    )
    get_bottoms = pltpu.make_async_copy(
        views.at[pl.ds(0, count), pl.ds(ROWS - EDGE, EDGE)], bottoms, sems.at[1]
    )
    get_tops.start()
    get_bottoms.start()
    index = lax.broadcasted_iota(jnp.int32, (EDGE, COLS), 0)

    def put(out, q, ti, rows):
        out[q * ANG + ti] = rows.astype(jnp.bfloat16)

    get_tops.wait()
    for ti in range(ANG):

        def first(s, ti=ti):
            return tops[s * ANG + ti].astype(F32)

        put(ups, 0, ti, first(4))
        put(ups, 1, ti, jnp.where(index < 12, first(3), pltpu.roll(first(0), 12, 0)))
        put(ups, 2, ti, jnp.where(index < 9, first(2), pltpu.roll(first(1), 9, 0)))
    get_bottoms.wait()
    for ti in range(ANG):

        def last(s, ti=ti):
            return bottoms[(s + HALF) * ANG + ti].astype(F32)

        put(downs, 0, ti, last(-4))
        put(downs, 1, ti, jnp.where(index < 4, pltpu.roll(last(0), 4, 0), last(-3)))
        put(downs, 2, ti, jnp.where(index < 7, pltpu.roll(last(-1), 7, 0), last(-2)))
    even = is_even("row")

    @pl.when(even)
    def _():
        send_pair[...] = downs[...]
        send_next[...] = ups[...]

    @pl.when(jnp.logical_not(even))
    def _():
        send_pair[...] = ups[...]
        send_next[...] = downs[...]


PLACES = {
    ("above", 0): ((-4, 0),),
    ("above", 1): ((-3, 0), (0, 12)),
    ("above", 2): ((-2, 0), (-1, 9)),
    ("below", 0): ((4, ROWS),),
    ("below", 1): ((3, ROWS), (0, EDGE + ROWS - 12)),
    ("below", 2): ((2, ROWS), (1, ROWS - 9)),
}


def packed_piece(side, q):
    return ANG * ROWS + ((0 if side == "above" else PIECES) + q) * EDGE


def piece_places():
    slots = ((1, 109), (2, 45), (2, 109), (3, 45), (3, 109))
    places = {}
    for n, (name, cut) in enumerate((name, cut) for name in PLACES for cut in CUTS):
        p, there = slots[n % len(slots)]
        row = p * ROWS + n // len(slots) * EDGE
        places.setdefault(name, []).append((row, *cut, there))
    return places


def share(first_of, second_of, to_left, to_right, at, spare=()):
    lane = lax.broadcasted_iota(jnp.int32, first_of.shape, 1)
    rows = pl.ds(at, first_of.shape[0])
    for out, turn in ((to_left, 0), (to_right, 64)):
        low = pltpu.roll(first_of, 64, 1) if turn else first_of
        high = second_of if turn else pltpu.roll(second_of, 64, 1)
        both = jnp.where(lane < 64, low, high)
        for pack, start, count, there in spare:
            moved = pltpu.roll(pack, (there - start - turn) % LANES, 1)
            both = jnp.where((lane >= there) & (lane < there + count), moved, both)
        out[rows, :] = both.astype(jnp.bfloat16)


def pack_own(views, own, to_left, to_right, pack):
    column = lax.broadcasted_iota(jnp.int32, (COLS, LANES), 0)
    lane = lax.broadcasted_iota(jnp.int32, (COLS, LANES), 1)
    for t in range(-HALF, HALF + 1):
        hit = jnp.zeros((COLS, LANES), F32)
        if t >= 0:
            bound = D0 * t + D0
            hit = jnp.where((column < bound) & (lane - column == lane_first(t, 0)), 1.0, hit)
        if t <= 0:
            start = COLS - D0 * abs(t) - D0
            apart = lane_last(t, start) - start
            hit = jnp.where((column >= start) & (lane - column == apart), 1.0, hit)
        if t:
            near = column < 2 if t < 0 else column >= COLS - 2
            apart = lane_here(t, 0)
            hit = jnp.where(near & (lane - column == apart), 1.0, hit)
        pack[t + HALF] = hit.astype(jnp.bfloat16)

    def packed(s):
        total = dot(views[(s + HALF) * ANG], pack[0])
        for ti in range(1, ANG):
            total = total + dot(views[(s + HALF) * ANG + ti], pack[ti])
        own[(s + HALF) * ROWS : (s + HALF + 1) * ROWS, :] = total.astype(jnp.bfloat16)
        return total

    middle = packed(0)
    for p, (low, high) in enumerate(PAIRS):
        spare = [(middle, *lanes) for q, *lanes in SPARE if q == p]
        share(packed(low), packed(high), to_left, to_right, p * ROWS, spare)


def pack_edges(
    got_pair, got_next, pack, own_in, left_in, right_in,
    above, below, own, send_pair, send_next, to_left, to_right,
):
    even = is_even("row")

    @pl.when(even)
    def _():
        below[...] = got_pair[...]
        above[...] = got_next[...]

    @pl.when(jnp.logical_not(even))
    def _():
        below[...] = got_next[...]
        above[...] = got_pair[...]

    own[: ANG * ROWS, :] = own_in[...]
    edges = {"above": above, "below": below}
    total = jnp.zeros((len(PLACES) * EDGE, LANES), F32)
    for ti in range(ANG):
        rows = [edges[side][q * ANG + ti] for side, q in PLACES]
        total = total + dot(jnp.concatenate(rows, axis=0), pack[ti])
    parts = {}
    places = piece_places()
    for i, (side, q) in enumerate(PLACES):
        piece = total[i * EDGE : (i + 1) * EDGE]
        own[pl.ds(packed_piece(side, q), EDGE), :] = piece.astype(jnp.bfloat16)
        for row, *lanes in places[side, q]:
            parts.setdefault(row, []).append((piece, *lanes))
    lane = lax.broadcasted_iota(jnp.int32, (EDGE, LANES), 1)
    for out, block, turn in ((to_left, left_in, 0), (to_right, right_in, 64)):
        out[...] = block[...]
        for row, group in parts.items():
            both = block[row : row + EDGE, :].astype(F32)
            for piece, start, count, there in group:
                moved = pltpu.roll(piece, (there - start - turn) % LANES, 1)
                both = jnp.where((lane >= there) & (lane < there + count), moved, both)
            out[row : row + EDGE, :] = both.astype(jnp.bfloat16)
    even = is_even("col")

    @pl.when(even)
    def _():
        send_pair[...] = to_right[...]
        send_next[...] = to_left[...]

    @pl.when(jnp.logical_not(even))
    def _():
        send_pair[...] = to_left[...]
        send_next[...] = to_right[...]


def unshare(source, high, out):
    def rows_at(at, count):
        return source[pl.ds(at, count), :].astype(F32)

    for p, pair in enumerate(PAIRS):
        for half, s in enumerate(pair):
            rows = rows_at(p * ROWS, ROWS)
            if half != high:
                rows = pltpu.roll(rows, 64, 1)
            out[pl.ds((s + HALF) * ROWS, ROWS), :] = rows.astype(jnp.bfloat16)

    def join(parts, to, count):
        lane = lax.broadcasted_iota(jnp.int32, (count, LANES), 1)
        whole = jnp.zeros((count, LANES), F32)
        for row, start, lanes, there in parts:
            at = start + 64 * high
            rows = pltpu.roll(rows_at(row, count), (at - there) % LANES, 1)
            whole = jnp.where((lane >= at) & (lane < at + lanes), rows, whole)
        out[pl.ds(to, count), :] = whole.astype(jnp.bfloat16)

    join([(p * ROWS, *lanes) for p, *lanes in SPARE], HALF * ROWS, ROWS)
    for (side, q), parts in piece_places().items():
        join(parts, packed_piece(side, q), EDGE)


def first_row(s):
    return D0 * s - 2 if s > 0 else EDGE - 2 + D0 * s


def own_row(s):
    return 0 if s > 0 else EDGE


def accumulate(s, warped, side, center, data, source):
    at = first_row(s)
    value = warped[pl.ds(at, OUT), :]
    slope = float(s) * (warped[pl.ds(at + 1, OUT), :] - warped[pl.ds(at - 1, OUT), :])
    if side is not None:
        side_part = side[pl.ds(at, OUT), :]
        slope = slope + side_part if s else side_part
    error = value - center
    robust = lax.rsqrt(1.0 + error * error)
    weighted = robust * slope
    return data + weighted * slope, source + weighted * error


def fill(slab, at, array):
    slab[pl.ds(at, array.shape[0]), :] = array


def zero_tails(slabs):
    for i in range(ANG):
        slabs[i, pl.ds(ROWS, SLAB - ROWS), :] = jnp.zeros((SLAB - ROWS, LANES), F32)


def fill_pieces(parts_of, outs):
    for (side, q), places in PLACES.items():
        parts = parts_of(side, q)
        for s, at in places:
            for out, part in zip(outs, parts):
                fill(out.at[s + HALF], at, part)


def halves(both):
    return both[:, :LANES], both[:, LANES:]


def shifted_views(matrix, own, piece, center, warped, side):
    span = range(-HALF, HALF + 1)
    rows = [own(s) for s in span] + [piece(name, q) for name, q in PLACES]
    both = dot(jnp.concatenate(rows, axis=0), matrix)
    first = {key: ANG * ROWS + i * EDGE for i, key in enumerate(PLACES)}

    def part(at, count):
        return both[at : at + count, :LANES], both[at : at + count, LANES:]

    fill_pieces(lambda name, q: part(first[name, q], EDGE), (warped, side))
    data = source = jnp.zeros((OUT, LANES), F32)
    for s in span:
        w, d = warped.at[s + HALF], side.at[s + HALF]
        shifted, slope = part((s + HALF) * ROWS, ROWS)
        fill(w, own_row(s), shifted)
        fill(d, own_row(s), slope)
        data, source = accumulate(s, w, d, center, data, source)
    return data, source


def inner_sums(tile, views, edges, inner, data_out, source_out, warped, side, center_ref):
    zero_tails(warped)
    zero_tails(side)
    lanes = slice(tile * LANES, (tile + 1) * LANES)
    fill_pieces(
        lambda name, q: (edges[name][q * ANG + HALF][:, lanes].astype(F32),), (warped,)
    )
    data = source = jnp.zeros((OUT, LANES), F32)
    for s in (0, -4, -3, -2, -1, 1, 2, 3, 4):
        w = warped.at[s + HALF]
        fill(w, own_row(s), views[(s + HALF) * ANG + HALF][:, lanes].astype(F32))
        if s == 0:
            center_ref[...] = w[pl.ds(first_row(0), OUT), :]
        data, source = accumulate(s, w, None, center_ref[...], data, source)
    data_out[...] = data
    source_out[...] = source

    def body(a, carry, sign):
        ti = HALF + 1 + a if sign else HALF - 1 - a
        data, source = shifted_views(
            inner[sign, a],
            lambda s: views[(s + HALF) * ANG + ti],
            lambda name, q: edges[name][q * ANG + ti],
            center_ref[...],
            warped,
            side,
        )
        data_out[...] += data
        source_out[...] += source
        return carry

    for sign in (0, 1):
        lax.fori_loop(0, HALF, functools.partial(body, sign=sign), 0)


def both_sums(views, above, below, left, right, data_out, source_out, *scratch):
    edges = {"above": above, "below": below}
    for tile, inner in enumerate((left, right)):
        inner_sums(tile, views, edges, inner, data_out.at[tile], source_out.at[tile], *scratch)


def outer_sums(
    total_rows,
    total_cols,
    views,
    above,
    below,
    own,
    got_next,
    got_pair,
    data_in,
    source_in,
    edge,
    edge_center,
    scatter,
    zed_out,
    near_out,
    next_out,
    precond_out,
    message,
    warped,
    side,
    center_ref,
    center_slab,
    left,
    right,
):
    even = is_even("col")

    @pl.when(even)
    def _():
        unshare(got_next, 1, left)
        unshare(got_pair, 0, right)

    @pl.when(jnp.logical_not(even))
    def _():
        unshare(got_pair, 1, left)
        unshare(got_next, 0, right)

    edges = {"above": above, "below": below}
    zero_tails(warped)
    zero_tails(side)
    zero = jnp.zeros((OUT, LANES), F32)

    def edge_rows(row, count):
        return jnp.concatenate([x[pl.ds(row, count), :] for x in (left, own, right)], axis=1)

    def fill_center(at, ref, row, count):
        fill(center_slab.at[0], at, ref[:, :LANES].astype(F32))
        fill(center_slab.at[1], at, ref[:, LANES:].astype(F32))
        around = (left[pl.ds(row, count), :], ref[...], right[pl.ds(row, count), :])
        both = dot(jnp.concatenate(around, axis=1), edge_center[...])
        fill(warped.at[HALF], at, both[:, :LANES])
        fill(center_slab.at[2], at, both[:, LANES:])

    for name in ("above", "below"):
        at = PLACES[name, 1][1][1]
        fill_center(at, edges[name].at[ANG + HALF], packed_piece(name, 1), EDGE)
    fill_center(EDGE, views.at[HALF * ANG + HALF], HALF * ROWS, ROWS)
    center_ref[...] = warped[HALF, pl.ds(first_row(0), OUT), :]
    sums = shifted_views(
        edge[...],
        lambda s: edge_rows((s + HALF) * ROWS, ROWS),
        lambda name, q: edge_rows(packed_piece(name, q), EDGE),
        center_ref[...],
        warped,
        side,
    )

    parts = []
    for x in sums:
        for _ in range(3):
            part = x.astype(jnp.bfloat16)
            parts.append(part)
            x = x - part.astype(F32)
    spread = dot(jnp.concatenate(parts, axis=0), scatter[...])

    def total(inside, at):
        high, middle, low = (spread[(at + i) * OUT : (at + i + 1) * OUT] for i in range(3))
        return jnp.concatenate([inside[0], inside[1], zero], axis=1) + ((low + middle) + high)

    data_sum = total(data_in, 0)
    source_sum = total(source_in, 3)

    wide = 3 * LANES

    def before(x):
        return pltpu.roll(x, 1, 1)

    def after(x):
        return pltpu.roll(x, wide - 1, 1)

    def over(x):
        return pltpu.roll(x, 1, 0)

    def under(x):
        return pltpu.roll(x, OUT - 1, 0)

    at = first_row(0)
    here = jnp.concatenate([center_slab[i, pl.ds(at, OUT), :] for i in range(3)], axis=1)
    higher = jnp.concatenate([center_slab[i, pl.ds(at - 1, OUT), :] for i in range(3)], axis=1)
    lane = lax.broadcasted_iota(jnp.int32, (OUT, wide), 1)
    local_row = lax.broadcasted_iota(jnp.int32, (OUT, wide), 0) - 2
    column = jnp.where(lane < wide - 64, lane, lane - wide) + lax.axis_index("col") * COLS
    row = local_row + lax.axis_index("row") * ROWS
    across = here - before(here)
    vertical = here - higher
    h_left = jnp.where((column >= 1) & (column <= total_cols - 1), jnp.exp(-across * across), 0.0)
    v_up = jnp.where((row >= 1) & (row <= total_rows - 1), jnp.exp(-vertical * vertical), 0.0)
    h_right = after(h_left)
    v_down = under(v_up)
    coeff = DAMPING + data_sum * (0.25 / VIEWS)
    source = source_sum * (-0.5 / VIEWS)
    precond = coeff + SMOOTH * (h_left + h_right + v_up + v_down)
    inverse = 1.0 / precond

    def neighbours(x):
        total = h_left * before(x) + h_right * after(x) + v_up * over(x) + v_down * under(x)
        return SMOOTH * inverse * total

    zed = source * inverse
    near = neighbours(zed)
    nxt = neighbours(near)

    def block(x):
        return x[:, :COLS]

    zed, near, nxt, precond = block(zed), block(near), block(nxt), block(precond)
    zed_out[...] = zed
    near_out[...] = near
    next_out[...] = nxt
    precond_out[...] = precond
    mine = (block(local_row) >= 0) & (block(local_row) < ROWS)

    def inner(x, y):
        return jnp.sum(jnp.where(mine, precond * x * y, 0.0), keepdims=True)

    zz = inner(zed, zed)
    zn = inner(zed, near)
    kappa = jnp.clip(zn / jnp.where(zz > 0, zz, 1.0), -1.0, 1.0)
    y = near - kappa * zed
    g = nxt - kappa * near
    numbers = (
        (0, inner(y, y)),
        (1, inner(y, g)),
        (32, 2.0 * inner(y, zed)),
        (33, inner(y, near) + inner(zed, g)),
        (64, zz),
        (65, zn),
        (96, kappa),
        (97, kappa),
    )
    place = lax.broadcasted_iota(jnp.int32, (1, LANES), 1)
    out = jnp.zeros((1, LANES), F32)
    for where, number in numbers:
        out = jnp.where(place == where, number, out)
    message[...] = out


def finish(messages, zed_ref, near_ref, next_ref, precond_ref, increment, residual):
    all_of = messages[...]
    total = jnp.sum(all_of, axis=0, keepdims=True)
    zz = total[:, 64:65]
    zn = total[:, 65:66]
    kappa = zn / zz
    delta = pltpu.roll(all_of, 32, 1) - kappa
    linear = pltpu.roll(all_of, 96, 1)
    quad = pltpu.roll(all_of, 64, 1)
    moved = jnp.sum(all_of + delta * (linear + delta * quad), axis=0, keepdims=True)
    yy = moved[:, 0:1]
    yny = moved[:, 1:2]
    step0 = zz / (zz - zn)
    beta = step0 * step0 * yy / zz
    step1 = yy / (yy - yny - step0 * yy * yy / zz)
    rows = pl.ds(2, ROWS)
    zed = zed_ref[rows, :]
    near = near_ref[rows, :]
    nxt = next_ref[rows, :]
    y = near - kappa * zed
    g = nxt - kappa * near
    increment[...] = step0 * zed + step1 * (step0 * y + beta * zed)
    residual[...] = precond_ref[rows, :] * (
        step0 * y - step1 * (step0 * (y - g) + beta * (zed - near))
    )


def call(kernel, outs, scratch=(), name=None, vmem=24, **more):
    return pl.pallas_call(
        kernel,
        out_shape=outs,
        scratch_shapes=list(scratch),
        compiler_params=pltpu.CompilerParams(vmem_limit_bytes=vmem * 1024 * 1024),
        name=name,
        **more,
    )


def swap(array, axis, start):
    pairs = []
    for i in range(start, lax.axis_size(axis) - 1, 2):
        pairs += [(i, i + 1), (i + 1, i)]
    return lax.ppermute(array, axis, pairs)


def shards(views):
    rows, cols = lax.axis_size("row"), lax.axis_size("col")
    left_inner, right_inner, edge_matrix, center, scatter = (jnp.asarray(x) for x in tables())
    bf16 = jnp.bfloat16
    struct = jax.ShapeDtypeStruct

    edge = struct((PIECES * ANG, EDGE, COLS), bf16)
    room = pltpu.VMEM(edge.shape, bf16)
    taken = pltpu.VMEM(((HALF + 1) * ANG, EDGE, COLS), bf16)
    pair, after = call(
        pack_rows,
        (edge, edge),
        (taken, taken, room, room, pltpu.SemaphoreType.DMA((2,))),
        name="pack_rows",
        vmem=62,
        in_specs=[pl.BlockSpec(memory_space=pltpu.HBM)],
    )(views)
    pair = swap(pair, "row", 0)
    after = swap(after, "row", 1)
    shared = struct((SHARED, LANES), bf16)
    own, to_left, to_right, pack = call(
        pack_own,
        (struct((ANG * ROWS, LANES), bf16), shared, shared, struct((ANG, COLS, LANES), bf16)),
        name="pack_own",
    )(views)
    room = pltpu.VMEM(shared.shape, bf16)
    above, below, own, pair, after = call(
        pack_edges,
        (edge, edge, struct((PACKED, LANES), bf16), shared, shared),
        (room, room),
        name="pack_edges",
    )(pair, after, pack, own, to_left, to_right)
    after = swap(after, "col", 1)
    pair = swap(pair, "col", 0)
    slab = pltpu.VMEM((ANG, SLAB, LANES), F32)
    tile = pltpu.VMEM((OUT, LANES), F32)
    sums = struct((2, OUT, LANES), F32)
    data, source = call(both_sums, (sums, sums), (slab, slab, tile), name="inner_sums")(
        views, above, below, left_inner, right_inner
    )
    field = struct((OUT, COLS), F32)
    zed, near, nxt, precond, message = call(
        functools.partial(outer_sums, rows * ROWS, cols * COLS),
        (field, field, field, field, struct((1, LANES), F32)),
        (
            slab,
            slab,
            tile,
            pltpu.VMEM((3, SLAB, LANES), F32),
            pltpu.VMEM((PACKED, LANES), bf16),
            pltpu.VMEM((PACKED, LANES), bf16),
        ),
        name="outer_sums",
    )(views, above, below, own, after, pair, data, source, edge_matrix, center, scatter)
    n = rows * cols
    messages = lax.all_to_all(
        jnp.broadcast_to(message[None], (n, 1, LANES)), ALL, 0, 0, tiled=True
    ).reshape(n, LANES)
    block = struct((ROWS, COLS), F32)
    return call(finish, (block, block), name="finish")(messages, zed, near, nxt, precond)


def solution(mesh):
    return jax.shard_map(
        shards,
        mesh=mesh,
        in_specs=(P(None, "row", "col"),),
        out_specs=(P("row", "col"), P("row", "col")),
        check_vma=False,
    )
```

```python
import functools

import jax
import jax.numpy as jnp
import ml_dtypes
import numpy as np
from jax import lax
from jax.experimental import pallas as pl
from jax.experimental.pallas import tpu as pltpu
from jax.sharding import Mesh
from jax.sharding import PartitionSpec as P

ANG = 9
VIEWS = 81
HALF = ANG // 2
D0 = 3
ROWS = 64
COLS = 256
EDGE = 16
OUT = 72
SLAB = 96
PIECES = 3
PACKED = ANG * ROWS + 2 * PIECES * EDGE
PAIRS = ((-4, -3), (-2, -1), (1, 2), (3, 4))
SHARED = len(PAIRS) * ROWS
CUTS = ((0, 18), (18, 12), (30, 15))
SPARE = tuple((p, *cut, there) for cut, (p, there) in zip(CUTS, ((0, 45), (0, 109), (1, 45))))
LANES = 128
SMOOTH = 2.0
DAMPING = 0.1
ROW = ("chip", "core")
COL = "col"
F32 = jnp.float32


def lane_first(t, c):
    return D0 * t * (t + 1) // 2 + c


def lane_last(t, c):
    a = abs(t)
    return 64 + D0 * a * (a + 1) // 2 + c - (COLS - D0 * a - D0)


def lane_here(t, c):
    return 45 + 2 * (-t - 1) + c if t < 0 else 109 + 2 * (t - 1) + c - (COLS - 2)


def edge_source(t, c):
    if c < 0:
        return lane_last(t, COLS + c)
    if c >= COLS:
        return 2 * LANES + lane_first(t, c - COLS)
    if t >= 0 and c <= D0 * t + D0 - 1:
        return LANES + lane_first(t, c)
    if t <= 0 and c >= COLS - D0 * abs(t) - D0:
        return LANES + lane_last(t, c)
    return LANES + lane_here(t, c)


def edge_pixels():
    for t in range(-HALF, HALF + 1):
        for column in range(-2, D0 * -t + 1 if t < 0 else 0):
            yield t, column
        for column in range(COLS - 1 - D0 * t if t > 0 else COLS, COLS + 2):
            yield t, column


def tables():
    inner = np.zeros((2, 2, HALF, COLS, 2 * LANES), np.float32)
    for tile in (0, 1):
        for a in range(1, HALF + 1):
            for sign in (0, 1):
                t = a if sign else -a
                for j in range(LANES):
                    c = tile * LANES + j + D0 * t
                    if 1 <= c < COLS - 1:
                        inner[tile, sign, a - 1, c, j] += 1
                        inner[tile, sign, a - 1, c + 1, LANES + j] += t
                        inner[tile, sign, a - 1, c - 1, LANES + j] -= t
    edge = np.zeros((3 * LANES, 2 * LANES), np.float32)
    center = np.zeros((LANES + COLS + LANES, 2 * LANES), np.float32)
    scatter = np.zeros((LANES, 3 * LANES), np.float32)

    def center_source(c):
        if c < 0:
            return lane_last(0, COLS + c)
        return LANES + c if c < COLS else LANES + COLS + lane_first(0, c - COLS)

    for lane, (t, col) in enumerate(edge_pixels()):
        c = col + D0 * t
        edge[edge_source(t, c), lane] += 1
        if t:
            edge[edge_source(t, c + 1), LANES + lane] += t
            edge[edge_source(t, c - 1), LANES + lane] -= t
        center[center_source(col), lane] = 1
        scatter[lane, col % (3 * LANES)] = 1
    for col in (-3, -2, -1, COLS, COLS + 1, COLS + 2):
        center[center_source(col), LANES + col % LANES] = 1
    return tuple(x.astype(ml_dtypes.bfloat16) for x in (*inner, edge, center, scatter))


def dot(a, b):
    return jnp.dot(a, b, preferred_element_type=F32)


def is_even(axis):
    return lax.rem(lax.axis_index(axis), 2) == 0


def pack_rows(views, send_pair, send_next, ups_out, downs_out):
    even = is_even(ROW)
    index = lax.broadcasted_iota(jnp.int32, (EDGE, COLS), 0)

    def put(ups, q, ti, rows):
        (ups_out if ups else downs_out)[q * ANG + ti] = rows.astype(jnp.bfloat16)

    for ti in range(ANG):

        def rows_of(s, start, ti=ti):
            return views[(s + HALF) * ANG + ti, pl.ds(start, EDGE), :].astype(F32)

        first = functools.partial(rows_of, start=0)
        last = functools.partial(rows_of, start=ROWS - EDGE)
        put(True, 0, ti, first(4))
        put(True, 1, ti, jnp.where(index < 12, first(3), pltpu.roll(first(0), 12, 0)))
        put(True, 2, ti, jnp.where(index < 9, first(2), pltpu.roll(first(1), 9, 0)))
        put(False, 0, ti, last(-4))
        put(False, 1, ti, jnp.where(index < 4, pltpu.roll(last(0), 4, 0), last(-3)))
        put(False, 2, ti, jnp.where(index < 7, pltpu.roll(last(-1), 7, 0), last(-2)))

    @pl.when(even)
    def _():
        send_pair[...] = downs_out[...]
        send_next[...] = ups_out[...]

    @pl.when(jnp.logical_not(even))
    def _():
        send_pair[...] = ups_out[...]
        send_next[...] = downs_out[...]


PLACES = {
    ("above", 0): ((-4, 0),),
    ("above", 1): ((-3, 0), (0, 12)),
    ("above", 2): ((-2, 0), (-1, 9)),
    ("below", 0): ((4, ROWS),),
    ("below", 1): ((3, ROWS), (0, EDGE + ROWS - 12)),
    ("below", 2): ((2, ROWS), (1, ROWS - 9)),
}


def packed_piece(side, q):
    return ANG * ROWS + ((0 if side == "above" else PIECES) + q) * EDGE


def piece_places():
    slots = ((1, 109), (2, 45), (2, 109), (3, 45), (3, 109))
    places = {}
    for n, (name, cut) in enumerate((name, cut) for name in PLACES for cut in CUTS):
        p, there = slots[n % len(slots)]
        row = p * ROWS + n // len(slots) * EDGE
        places.setdefault(name, []).append((row, *cut, there))
    return places


def share(first_of, second_of, to_left, to_right, at, spare=()):
    lane = lax.broadcasted_iota(jnp.int32, first_of.shape, 1)
    rows = pl.ds(at, first_of.shape[0])
    for out, turn in ((to_left, 0), (to_right, 64)):
        low = pltpu.roll(first_of, 64, 1) if turn else first_of
        high = second_of if turn else pltpu.roll(second_of, 64, 1)
        both = jnp.where(lane < 64, low, high)
        for pack, start, count, there in spare:
            moved = pltpu.roll(pack, (there - start - turn) % LANES, 1)
            both = jnp.where((lane >= there) & (lane < there + count), moved, both)
        out[rows, :] = both.astype(jnp.bfloat16)


def pack_own(views, own, to_left, to_right, pack):
    column = lax.broadcasted_iota(jnp.int32, (COLS, LANES), 0)
    lane = lax.broadcasted_iota(jnp.int32, (COLS, LANES), 1)
    for t in range(-HALF, HALF + 1):
        hit = jnp.zeros((COLS, LANES), F32)
        if t >= 0:
            bound = D0 * t + D0
            hit = jnp.where((column < bound) & (lane - column == lane_first(t, 0)), 1.0, hit)
        if t <= 0:
            start = COLS - D0 * abs(t) - D0
            apart = lane_last(t, start) - start
            hit = jnp.where((column >= start) & (lane - column == apart), 1.0, hit)
        if t:
            near = column < 2 if t < 0 else column >= COLS - 2
            apart = lane_here(t, 0)
            hit = jnp.where(near & (lane - column == apart), 1.0, hit)
        pack[t + HALF] = hit.astype(jnp.bfloat16)

    def packed(s):
        total = dot(views[(s + HALF) * ANG], pack[0])
        for ti in range(1, ANG):
            total = total + dot(views[(s + HALF) * ANG + ti], pack[ti])
        own[(s + HALF) * ROWS : (s + HALF + 1) * ROWS, :] = total.astype(jnp.bfloat16)
        return total

    middle = packed(0)
    for p, (low, high) in enumerate(PAIRS):
        spare = [(middle, *lanes) for q, *lanes in SPARE if q == p]
        share(packed(low), packed(high), to_left, to_right, p * ROWS, spare)


def pack_edges(
    got_pair, got_next, pack, own_in, left_in, right_in,
    above, below, own, send_pair, send_next, to_left, to_right,
):
    even = is_even(ROW)

    @pl.when(even)
    def _():
        below[...] = got_pair[...]
        above[...] = got_next[...]

    @pl.when(jnp.logical_not(even))
    def _():
        below[...] = got_next[...]
        above[...] = got_pair[...]

    own[: ANG * ROWS, :] = own_in[...]
    edges = {"above": above, "below": below}
    total = jnp.zeros((len(PLACES) * EDGE, LANES), F32)
    for ti in range(ANG):
        rows = [edges[side][q * ANG + ti] for side, q in PLACES]
        total = total + dot(jnp.concatenate(rows, axis=0), pack[ti])
    parts = {}
    places = piece_places()
    for i, (side, q) in enumerate(PLACES):
        piece = total[i * EDGE : (i + 1) * EDGE]
        own[pl.ds(packed_piece(side, q), EDGE), :] = piece.astype(jnp.bfloat16)
        for row, *lanes in places[side, q]:
            parts.setdefault(row, []).append((piece, *lanes))
    lane = lax.broadcasted_iota(jnp.int32, (EDGE, LANES), 1)
    for out, block, turn in ((to_left, left_in, 0), (to_right, right_in, 64)):
        out[...] = block[...]
        for row, group in parts.items():
            both = block[row : row + EDGE, :].astype(F32)
            for piece, start, count, there in group:
                moved = pltpu.roll(piece, (there - start - turn) % LANES, 1)
                both = jnp.where((lane >= there) & (lane < there + count), moved, both)
            out[row : row + EDGE, :] = both.astype(jnp.bfloat16)
    even = is_even(COL)

    @pl.when(even)
    def _():
        send_pair[...] = to_right[...]
        send_next[...] = to_left[...]

    @pl.when(jnp.logical_not(even))
    def _():
        send_pair[...] = to_left[...]
        send_next[...] = to_right[...]


def unshare(source, high, out):
    def rows_at(at, count):
        return source[pl.ds(at, count), :].astype(F32)

    for p, pair in enumerate(PAIRS):
        for half, s in enumerate(pair):
            rows = rows_at(p * ROWS, ROWS)
            if half != high:
                rows = pltpu.roll(rows, 64, 1)
            out[pl.ds((s + HALF) * ROWS, ROWS), :] = rows.astype(jnp.bfloat16)

    def join(parts, to, count):
        lane = lax.broadcasted_iota(jnp.int32, (count, LANES), 1)
        whole = jnp.zeros((count, LANES), F32)
        for row, start, lanes, there in parts:
            at = start + 64 * high
            rows = pltpu.roll(rows_at(row, count), (at - there) % LANES, 1)
            whole = jnp.where((lane >= at) & (lane < at + lanes), rows, whole)
        out[pl.ds(to, count), :] = whole.astype(jnp.bfloat16)

    join([(p * ROWS, *lanes) for p, *lanes in SPARE], HALF * ROWS, ROWS)
    for (side, q), parts in piece_places().items():
        join(parts, packed_piece(side, q), EDGE)


def first_row(s):
    return D0 * s - 2 if s > 0 else EDGE - 2 + D0 * s


def own_row(s):
    return 0 if s > 0 else EDGE


def accumulate(s, warped, side, center, data, source):
    at = first_row(s)
    value = warped[pl.ds(at, OUT), :]
    slope = float(s) * (warped[pl.ds(at + 1, OUT), :] - warped[pl.ds(at - 1, OUT), :])
    if side is not None:
        side_part = side[pl.ds(at, OUT), :]
        slope = slope + side_part if s else side_part
    error = value - center
    robust = lax.rsqrt(1.0 + error * error)
    weighted = robust * slope
    return data + weighted * slope, source + weighted * error


def fill(slab, at, array):
    slab[pl.ds(at, array.shape[0]), :] = array


def zero_tails(slabs):
    for i in range(ANG):
        slabs[i, pl.ds(ROWS, SLAB - ROWS), :] = jnp.zeros((SLAB - ROWS, LANES), F32)


def fill_pieces(parts_of, outs):
    for (side, q), places in PLACES.items():
        parts = parts_of(side, q)
        for s, at in places:
            for out, part in zip(outs, parts):
                fill(out.at[s + HALF], at, part)


def halves(both):
    return both[:, :LANES], both[:, LANES:]


def shifted_views(matrix, own, piece, center, warped, side):
    span = range(-HALF, HALF + 1)
    rows = [own(s) for s in span] + [piece(name, q) for name, q in PLACES]
    both = dot(jnp.concatenate(rows, axis=0), matrix)
    first = {key: ANG * ROWS + i * EDGE for i, key in enumerate(PLACES)}

    def part(at, count):
        return both[at : at + count, :LANES], both[at : at + count, LANES:]

    fill_pieces(lambda name, q: part(first[name, q], EDGE), (warped, side))
    data = source = jnp.zeros((OUT, LANES), F32)
    for s in span:
        w, d = warped.at[s + HALF], side.at[s + HALF]
        shifted, slope = part((s + HALF) * ROWS, ROWS)
        fill(w, own_row(s), shifted)
        fill(d, own_row(s), slope)
        data, source = accumulate(s, w, d, center, data, source)
    return data, source


def inner_sums(tile, views, edges, inner, data_out, source_out, warped, side, center_ref):
    zero_tails(warped)
    zero_tails(side)
    lanes = slice(tile * LANES, (tile + 1) * LANES)
    fill_pieces(
        lambda name, q: (edges[name][q * ANG + HALF][:, lanes].astype(F32),), (warped,)
    )
    data = source = jnp.zeros((OUT, LANES), F32)
    for s in (0, -4, -3, -2, -1, 1, 2, 3, 4):
        w = warped.at[s + HALF]
        fill(w, own_row(s), views[(s + HALF) * ANG + HALF][:, lanes].astype(F32))
        if s == 0:
            center_ref[...] = w[pl.ds(first_row(0), OUT), :]
        data, source = accumulate(s, w, None, center_ref[...], data, source)
    data_out[...] = data
    source_out[...] = source

    def body(a, carry, sign):
        ti = HALF + 1 + a if sign else HALF - 1 - a
        data, source = shifted_views(
            inner[sign, a],
            lambda s: views[(s + HALF) * ANG + ti],
            lambda name, q: edges[name][q * ANG + ti],
            center_ref[...],
            warped,
            side,
        )
        data_out[...] += data
        source_out[...] += source
        return carry

    for sign in (0, 1):
        lax.fori_loop(0, HALF, functools.partial(body, sign=sign), 0)


def both_sums(views, above, below, left, right, data_out, source_out, *scratch):
    edges = {"above": above, "below": below}
    for tile, inner in enumerate((left, right)):
        inner_sums(tile, views, edges, inner, data_out.at[tile], source_out.at[tile], *scratch)


def outer_sums(
    total_rows,
    total_cols,
    views,
    above,
    below,
    own,
    got_next,
    got_pair,
    data_in,
    source_in,
    edge,
    edge_center,
    scatter,
    zed_out,
    near_out,
    next_out,
    precond_out,
    message,
    warped,
    side,
    center_ref,
    center_slab,
    left,
    right,
):
    even = is_even(COL)

    @pl.when(even)
    def _():
        unshare(got_next, 1, left)
        unshare(got_pair, 0, right)

    @pl.when(jnp.logical_not(even))
    def _():
        unshare(got_pair, 1, left)
        unshare(got_next, 0, right)

    edges = {"above": above, "below": below}
    zero_tails(warped)
    zero_tails(side)
    zero = jnp.zeros((OUT, LANES), F32)

    def edge_rows(row, count):
        return jnp.concatenate([x[pl.ds(row, count), :] for x in (left, own, right)], axis=1)

    def fill_center(at, ref, row, count):
        fill(center_slab.at[0], at, ref[:, :LANES].astype(F32))
        fill(center_slab.at[1], at, ref[:, LANES:].astype(F32))
        around = (left[pl.ds(row, count), :], ref[...], right[pl.ds(row, count), :])
        both = dot(jnp.concatenate(around, axis=1), edge_center[...])
        fill(warped.at[HALF], at, both[:, :LANES])
        fill(center_slab.at[2], at, both[:, LANES:])

    for name in ("above", "below"):
        at = PLACES[name, 1][1][1]
        fill_center(at, edges[name].at[ANG + HALF], packed_piece(name, 1), EDGE)
    fill_center(EDGE, views.at[HALF * ANG + HALF], HALF * ROWS, ROWS)
    center_ref[...] = warped[HALF, pl.ds(first_row(0), OUT), :]
    sums = shifted_views(
        edge[...],
        lambda s: edge_rows((s + HALF) * ROWS, ROWS),
        lambda name, q: edge_rows(packed_piece(name, q), EDGE),
        center_ref[...],
        warped,
        side,
    )

    parts = []
    for x in sums:
        for _ in range(3):
            part = x.astype(jnp.bfloat16)
            parts.append(part)
            x = x - part.astype(F32)
    spread = dot(jnp.concatenate(parts, axis=0), scatter[...])

    def total(inside, at):
        high, middle, low = (spread[(at + i) * OUT : (at + i + 1) * OUT] for i in range(3))
        return jnp.concatenate([inside[0], inside[1], zero], axis=1) + ((low + middle) + high)

    data_sum = total(data_in, 0)
    source_sum = total(source_in, 3)

    wide = 3 * LANES

    def before(x):
        return pltpu.roll(x, 1, 1)

    def after(x):
        return pltpu.roll(x, wide - 1, 1)

    def over(x):
        return pltpu.roll(x, 1, 0)

    def under(x):
        return pltpu.roll(x, OUT - 1, 0)

    at = first_row(0)
    here = jnp.concatenate([center_slab[i, pl.ds(at, OUT), :] for i in range(3)], axis=1)
    higher = jnp.concatenate([center_slab[i, pl.ds(at - 1, OUT), :] for i in range(3)], axis=1)
    lane = lax.broadcasted_iota(jnp.int32, (OUT, wide), 1)
    local_row = lax.broadcasted_iota(jnp.int32, (OUT, wide), 0) - 2
    column = jnp.where(lane < wide - 64, lane, lane - wide) + lax.axis_index(COL) * COLS
    row = local_row + lax.axis_index(ROW) * ROWS
    across = here - before(here)
    vertical = here - higher
    h_left = jnp.where((column >= 1) & (column <= total_cols - 1), jnp.exp(-across * across), 0.0)
    v_up = jnp.where((row >= 1) & (row <= total_rows - 1), jnp.exp(-vertical * vertical), 0.0)
    h_right = after(h_left)
    v_down = under(v_up)
    coeff = DAMPING + data_sum * (0.25 / VIEWS)
    source = source_sum * (-0.5 / VIEWS)
    precond = coeff + SMOOTH * (h_left + h_right + v_up + v_down)
    inverse = 1.0 / precond

    def neighbours(x):
        total = h_left * before(x) + h_right * after(x) + v_up * over(x) + v_down * under(x)
        return SMOOTH * inverse * total

    zed = source * inverse
    near = neighbours(zed)
    nxt = neighbours(near)

    def block(x):
        return x[:, :COLS]

    zed, near, nxt, precond = block(zed), block(near), block(nxt), block(precond)
    zed_out[...] = zed
    near_out[...] = near
    next_out[...] = nxt
    precond_out[...] = precond
    mine = (block(local_row) >= 0) & (block(local_row) < ROWS)

    def inner(x, y):
        return jnp.sum(jnp.where(mine, precond * x * y, 0.0), keepdims=True)

    zz = inner(zed, zed)
    zn = inner(zed, near)
    kappa = jnp.clip(zn / jnp.where(zz > 0, zz, 1.0), -1.0, 1.0)
    y = near - kappa * zed
    g = nxt - kappa * near
    numbers = (
        (0, inner(y, y)),
        (1, inner(y, g)),
        (32, 2.0 * inner(y, zed)),
        (33, inner(y, near) + inner(zed, g)),
        (64, zz),
        (65, zn),
        (96, kappa),
        (97, kappa),
    )
    place = lax.broadcasted_iota(jnp.int32, (1, LANES), 1)
    out = jnp.zeros((1, LANES), F32)
    for where, number in numbers:
        out = jnp.where(place == where, number, out)
    message[...] = out


def finish(messages, zed_ref, near_ref, next_ref, precond_ref, increment, residual):
    all_of = messages[...]
    total = jnp.sum(all_of, axis=0, keepdims=True)
    zz = total[:, 64:65] + total[:, 66:67]
    zn = total[:, 65:66] + total[:, 67:68]
    kappa = zn / zz
    delta = pltpu.roll(all_of, 32, 1) - kappa
    linear = pltpu.roll(all_of, 96, 1)
    quad = pltpu.roll(all_of, 64, 1)
    moved = jnp.sum(all_of + delta * (linear + delta * quad), axis=0, keepdims=True)
    yy = moved[:, 0:1] + moved[:, 2:3]
    yny = moved[:, 1:2] + moved[:, 3:4]
    step0 = zz / (zz - zn)
    beta = step0 * step0 * yy / zz
    step1 = yy / (yy - yny - step0 * yy * yy / zz)
    rows = pl.ds(2, ROWS)
    zed = zed_ref[rows, :]
    near = near_ref[rows, :]
    nxt = next_ref[rows, :]
    y = near - kappa * zed
    g = nxt - kappa * near
    increment[...] = step0 * zed + step1 * (step0 * y + beta * zed)
    residual[...] = precond_ref[rows, :] * (
        step0 * y - step1 * (step0 * (y - g) + beta * (zed - near))
    )


def call(kernel, outs, scratch=(), name=None):
    return pl.pallas_call(
        kernel,
        out_shape=outs,
        scratch_shapes=list(scratch),
        compiler_params=pltpu.CompilerParams(vmem_limit_bytes=24 * 1024 * 1024),
        name=name,
    )


def swap(array, axis, start):
    pairs = []
    for i in range(start, lax.axis_size(axis) - 1, 2):
        pairs += [(i, i + 1), (i + 1, i)]
    return lax.ppermute(array, axis, pairs)


def shards(views):
    rows, cols = lax.axis_size(ROW), lax.axis_size(COL)
    left_inner, right_inner, edge_matrix, center, scatter = (jnp.asarray(x) for x in tables())
    bf16 = jnp.bfloat16
    struct = jax.ShapeDtypeStruct

    edge = struct((PIECES * ANG, EDGE, COLS), bf16)
    room = pltpu.VMEM(edge.shape, bf16)
    pair, after = call(pack_rows, (edge, edge), (room, room), name="pack_rows")(views)
    pair = swap(pair, ROW, 0)
    after = swap(after, ROW, 1)
    shared = struct((SHARED, LANES), bf16)
    own, to_left, to_right, pack = call(
        pack_own,
        (struct((ANG * ROWS, LANES), bf16), shared, shared, struct((ANG, COLS, LANES), bf16)),
        name="pack_own",
    )(views)
    room = pltpu.VMEM(shared.shape, bf16)
    above, below, own, pair, after = call(
        pack_edges,
        (edge, edge, struct((PACKED, LANES), bf16), shared, shared),
        (room, room),
        name="pack_edges",
    )(pair, after, pack, own, to_left, to_right)
    after = swap(after, COL, 1)
    pair = swap(pair, COL, 0)
    slab = pltpu.VMEM((ANG, SLAB, LANES), F32)
    tile = pltpu.VMEM((OUT, LANES), F32)
    sums = struct((2, OUT, LANES), F32)
    data, source = call(both_sums, (sums, sums), (slab, slab, tile), name="inner_sums")(
        views, above, below, left_inner, right_inner
    )
    field = struct((OUT, COLS), F32)
    zed, near, nxt, precond, message = call(
        functools.partial(outer_sums, rows * ROWS, cols * COLS),
        (field, field, field, field, struct((1, LANES), F32)),
        (
            slab,
            slab,
            tile,
            pltpu.VMEM((3, SLAB, LANES), F32),
            pltpu.VMEM((PACKED, LANES), bf16),
            pltpu.VMEM((PACKED, LANES), bf16),
        ),
        name="outer_sums",
    )(views, above, below, own, after, pair, data, source, edge_matrix, center, scatter)
    message = message + jnp.roll(swap(message, ROW, 0), 2, axis=1)
    n = rows * cols // 2
    messages = lax.all_to_all(
        jnp.broadcast_to(message[None], (n, 1, LANES)), ("chip", COL), 0, 0, tiled=True
    ).reshape(n, LANES)
    block = struct((ROWS, COLS), F32)
    return call(finish, (block, block), name="finish")(messages, zed, near, nxt, precond)


def solution(mesh):
    rows, cols = mesh.devices.shape
    finer = Mesh(mesh.devices.reshape(rows // 2, 2, cols), (*ROW, COL))
    return jax.shard_map(
        shards,
        mesh=finer,
        in_specs=(P(None, ROW, COL),),
        out_specs=(P(ROW, COL), P(ROW, COL)),
        check_vma=False,
    )
```

```python
import functools

import jax
import jax.numpy as jnp
import ml_dtypes
import numpy as np
from jax import lax
from jax.experimental import pallas as pl
from jax.experimental.pallas import tpu as pltpu
from jax.sharding import Mesh
from jax.sharding import PartitionSpec as P

ANG = 9
VIEWS = 81
HALF = ANG // 2
D0 = 3
ROWS = 64
COLS = 256
EDGE = 16
OUT = 72
SLAB = 96
PIECES = 3
PACKED = ANG * ROWS + 2 * PIECES * EDGE
PAIRS = ((-4, -3), (-2, -1), (1, 2), (3, 4))
SHARED = len(PAIRS) * ROWS
CUTS = ((0, 18), (18, 12), (30, 15))
SPARE = tuple((p, *cut, there) for cut, (p, there) in zip(CUTS, ((0, 45), (0, 109), (1, 45))))
LANES = 128
SMOOTH = 2.0
DAMPING = 0.1
ROW = ("chip", "core")
COL = "col"
F32 = jnp.float32


def lane_first(t, c):
    return D0 * t * (t + 1) // 2 + c


def lane_last(t, c):
    a = abs(t)
    return 64 + D0 * a * (a + 1) // 2 + c - (COLS - D0 * a - D0)


def lane_here(t, c):
    return 45 + 2 * (-t - 1) + c if t < 0 else 109 + 2 * (t - 1) + c - (COLS - 2)


def edge_source(t, c):
    if c < 0:
        return lane_last(t, COLS + c)
    if c >= COLS:
        return 2 * LANES + lane_first(t, c - COLS)
    if t >= 0 and c <= D0 * t + D0 - 1:
        return LANES + lane_first(t, c)
    if t <= 0 and c >= COLS - D0 * abs(t) - D0:
        return LANES + lane_last(t, c)
    return LANES + lane_here(t, c)


def edge_pixels():
    for t in range(-HALF, HALF + 1):
        for column in range(-2, D0 * -t + 1 if t < 0 else 0):
            yield t, column
        for column in range(COLS - 1 - D0 * t if t > 0 else COLS, COLS + 2):
            yield t, column


def tables():
    inner = np.zeros((2, 2, HALF, COLS, 2 * LANES), np.float32)
    for tile in (0, 1):
        for a in range(1, HALF + 1):
            for sign in (0, 1):
                t = a if sign else -a
                for j in range(LANES):
                    c = tile * LANES + j + D0 * t
                    if 1 <= c < COLS - 1:
                        inner[tile, sign, a - 1, c, j] += 1
                        inner[tile, sign, a - 1, c + 1, LANES + j] += t
                        inner[tile, sign, a - 1, c - 1, LANES + j] -= t
    edge = np.zeros((3 * LANES, 2 * LANES), np.float32)
    center = np.zeros((LANES + COLS + LANES, 2 * LANES), np.float32)
    scatter = np.zeros((LANES, 3 * LANES), np.float32)

    def center_source(c):
        if c < 0:
            return lane_last(0, COLS + c)
        return LANES + c if c < COLS else LANES + COLS + lane_first(0, c - COLS)

    for lane, (t, col) in enumerate(edge_pixels()):
        c = col + D0 * t
        edge[edge_source(t, c), lane] += 1
        if t:
            edge[edge_source(t, c + 1), LANES + lane] += t
            edge[edge_source(t, c - 1), LANES + lane] -= t
        center[center_source(col), lane] = 1
        scatter[lane, col % (3 * LANES)] = 1
    for col in (-3, -2, -1, COLS, COLS + 1, COLS + 2):
        center[center_source(col), LANES + col % LANES] = 1
    return tuple(x.astype(ml_dtypes.bfloat16) for x in (*inner, edge, center, scatter))


def dot(a, b):
    return jnp.dot(a, b, preferred_element_type=F32)


def is_even(axis):
    return lax.rem(lax.axis_index(axis), 2) == 0


def pack_rows(tops, bottoms, send_pair, send_next, ups_out, downs_out):
    even = is_even(ROW)
    index = lax.broadcasted_iota(jnp.int32, (EDGE, COLS), 0)

    def put(ups, q, ti, rows):
        (ups_out if ups else downs_out)[q * ANG + ti] = rows.astype(jnp.bfloat16)

    for ti in range(ANG):

        def first(s, ti=ti):
            return tops[s * ANG + ti].astype(F32)

        def last(s, ti=ti):
            return bottoms[(s + HALF) * ANG + ti].astype(F32)

        put(True, 0, ti, first(4))
        put(True, 1, ti, jnp.where(index < 12, first(3), pltpu.roll(first(0), 12, 0)))
        put(True, 2, ti, jnp.where(index < 9, first(2), pltpu.roll(first(1), 9, 0)))
        put(False, 0, ti, last(-4))
        put(False, 1, ti, jnp.where(index < 4, pltpu.roll(last(0), 4, 0), last(-3)))
        put(False, 2, ti, jnp.where(index < 7, pltpu.roll(last(-1), 7, 0), last(-2)))

    @pl.when(even)
    def _():
        send_pair[...] = downs_out[...]
        send_next[...] = ups_out[...]

    @pl.when(jnp.logical_not(even))
    def _():
        send_pair[...] = ups_out[...]
        send_next[...] = downs_out[...]


PLACES = {
    ("above", 0): ((-4, 0),),
    ("above", 1): ((-3, 0), (0, 12)),
    ("above", 2): ((-2, 0), (-1, 9)),
    ("below", 0): ((4, ROWS),),
    ("below", 1): ((3, ROWS), (0, EDGE + ROWS - 12)),
    ("below", 2): ((2, ROWS), (1, ROWS - 9)),
}


def packed_piece(side, q):
    return ANG * ROWS + ((0 if side == "above" else PIECES) + q) * EDGE


def piece_places():
    slots = ((1, 109), (2, 45), (2, 109), (3, 45), (3, 109))
    places = {}
    for n, (name, cut) in enumerate((name, cut) for name in PLACES for cut in CUTS):
        p, there = slots[n % len(slots)]
        row = p * ROWS + n // len(slots) * EDGE
        places.setdefault(name, []).append((row, *cut, there))
    return places


def share(first_of, second_of, to_left, to_right, at, spare=()):
    lane = lax.broadcasted_iota(jnp.int32, first_of.shape, 1)
    rows = pl.ds(at, first_of.shape[0])
    for out, turn in ((to_left, 0), (to_right, 64)):
        low = pltpu.roll(first_of, 64, 1) if turn else first_of
        high = second_of if turn else pltpu.roll(second_of, 64, 1)
        both = jnp.where(lane < 64, low, high)
        for pack, start, count, there in spare:
            moved = pltpu.roll(pack, (there - start - turn) % LANES, 1)
            both = jnp.where((lane >= there) & (lane < there + count), moved, both)
        out[rows, :] = both.astype(jnp.bfloat16)


def pack_own(views, own, to_left, to_right, pack):
    column = lax.broadcasted_iota(jnp.int32, (COLS, LANES), 0)
    lane = lax.broadcasted_iota(jnp.int32, (COLS, LANES), 1)
    for t in range(-HALF, HALF + 1):
        hit = jnp.zeros((COLS, LANES), F32)
        if t >= 0:
            bound = D0 * t + D0
            hit = jnp.where((column < bound) & (lane - column == lane_first(t, 0)), 1.0, hit)
        if t <= 0:
            start = COLS - D0 * abs(t) - D0
            apart = lane_last(t, start) - start
            hit = jnp.where((column >= start) & (lane - column == apart), 1.0, hit)
        if t:
            near = column < 2 if t < 0 else column >= COLS - 2
            apart = lane_here(t, 0)
            hit = jnp.where(near & (lane - column == apart), 1.0, hit)
        pack[t + HALF] = hit.astype(jnp.bfloat16)

    def packed(s):
        total = dot(views[(s + HALF) * ANG], pack[0])
        for ti in range(1, ANG):
            total = total + dot(views[(s + HALF) * ANG + ti], pack[ti])
        own[(s + HALF) * ROWS : (s + HALF + 1) * ROWS, :] = total.astype(jnp.bfloat16)
        return total

    middle = packed(0)
    for p, (low, high) in enumerate(PAIRS):
        spare = [(middle, *lanes) for q, *lanes in SPARE if q == p]
        share(packed(low), packed(high), to_left, to_right, p * ROWS, spare)


def pack_edges(
    got_pair, got_next, pack, own_in, left_in, right_in,
    above, below, own, send_pair, send_next, to_left, to_right,
):
    even = is_even(ROW)

    @pl.when(even)
    def _():
        below[...] = got_pair[...]
        above[...] = got_next[...]

    @pl.when(jnp.logical_not(even))
    def _():
        below[...] = got_next[...]
        above[...] = got_pair[...]

    own[: ANG * ROWS, :] = own_in[...]
    edges = {"above": above, "below": below}
    total = jnp.zeros((len(PLACES) * EDGE, LANES), F32)
    for ti in range(ANG):
        rows = [edges[side][q * ANG + ti] for side, q in PLACES]
        total = total + dot(jnp.concatenate(rows, axis=0), pack[ti])
    parts = {}
    places = piece_places()
    for i, (side, q) in enumerate(PLACES):
        piece = total[i * EDGE : (i + 1) * EDGE]
        own[pl.ds(packed_piece(side, q), EDGE), :] = piece.astype(jnp.bfloat16)
        for row, *lanes in places[side, q]:
            parts.setdefault(row, []).append((piece, *lanes))
    lane = lax.broadcasted_iota(jnp.int32, (EDGE, LANES), 1)
    for out, block, turn in ((to_left, left_in, 0), (to_right, right_in, 64)):
        out[...] = block[...]
        for row, group in parts.items():
            both = block[row : row + EDGE, :].astype(F32)
            for piece, start, count, there in group:
                moved = pltpu.roll(piece, (there - start - turn) % LANES, 1)
                both = jnp.where((lane >= there) & (lane < there + count), moved, both)
            out[row : row + EDGE, :] = both.astype(jnp.bfloat16)
    even = is_even(COL)

    @pl.when(even)
    def _():
        send_pair[...] = to_right[...]
        send_next[...] = to_left[...]

    @pl.when(jnp.logical_not(even))
    def _():
        send_pair[...] = to_left[...]
        send_next[...] = to_right[...]


def unshare(source, high, out):
    def rows_at(at, count):
        return source[pl.ds(at, count), :].astype(F32)

    for p, pair in enumerate(PAIRS):
        for half, s in enumerate(pair):
            rows = rows_at(p * ROWS, ROWS)
            if half != high:
                rows = pltpu.roll(rows, 64, 1)
            out[pl.ds((s + HALF) * ROWS, ROWS), :] = rows.astype(jnp.bfloat16)

    def join(parts, to, count):
        lane = lax.broadcasted_iota(jnp.int32, (count, LANES), 1)
        whole = jnp.zeros((count, LANES), F32)
        for row, start, lanes, there in parts:
            at = start + 64 * high
            rows = pltpu.roll(rows_at(row, count), (at - there) % LANES, 1)
            whole = jnp.where((lane >= at) & (lane < at + lanes), rows, whole)
        out[pl.ds(to, count), :] = whole.astype(jnp.bfloat16)

    join([(p * ROWS, *lanes) for p, *lanes in SPARE], HALF * ROWS, ROWS)
    for (side, q), parts in piece_places().items():
        join(parts, packed_piece(side, q), EDGE)


def first_row(s):
    return D0 * s - 2 if s > 0 else EDGE - 2 + D0 * s


def own_row(s):
    return 0 if s > 0 else EDGE


def accumulate(s, warped, side, center, data, source):
    at = first_row(s)
    value = warped[pl.ds(at, OUT), :]
    slope = float(s) * (warped[pl.ds(at + 1, OUT), :] - warped[pl.ds(at - 1, OUT), :])
    if side is not None:
        side_part = side[pl.ds(at, OUT), :]
        slope = slope + side_part if s else side_part
    error = value - center
    robust = lax.rsqrt(1.0 + error * error)
    weighted = robust * slope
    return data + weighted * slope, source + weighted * error


def fill(slab, at, array):
    slab[pl.ds(at, array.shape[0]), :] = array


def zero_tails(slabs):
    for i in range(ANG):
        slabs[i, pl.ds(ROWS, SLAB - ROWS), :] = jnp.zeros((SLAB - ROWS, LANES), F32)


def fill_pieces(parts_of, outs):
    for (side, q), places in PLACES.items():
        parts = parts_of(side, q)
        for s, at in places:
            for out, part in zip(outs, parts):
                fill(out.at[s + HALF], at, part)


def halves(both):
    return both[:, :LANES], both[:, LANES:]


def shifted_views(matrix, own, piece, center, warped, side):
    span = range(-HALF, HALF + 1)
    rows = [own(s) for s in span] + [piece(name, q) for name, q in PLACES]
    both = dot(jnp.concatenate(rows, axis=0), matrix)
    first = {key: ANG * ROWS + i * EDGE for i, key in enumerate(PLACES)}

    def part(at, count):
        return both[at : at + count, :LANES], both[at : at + count, LANES:]

    fill_pieces(lambda name, q: part(first[name, q], EDGE), (warped, side))
    data = source = jnp.zeros((OUT, LANES), F32)
    for s in span:
        w, d = warped.at[s + HALF], side.at[s + HALF]
        shifted, slope = part((s + HALF) * ROWS, ROWS)
        fill(w, own_row(s), shifted)
        fill(d, own_row(s), slope)
        data, source = accumulate(s, w, d, center, data, source)
    return data, source


def inner_sums(tile, views, edges, inner, data_out, source_out, warped, side, center_ref):
    zero_tails(warped)
    zero_tails(side)
    lanes = slice(tile * LANES, (tile + 1) * LANES)
    fill_pieces(
        lambda name, q: (edges[name][q * ANG + HALF][:, lanes].astype(F32),), (warped,)
    )
    data = source = jnp.zeros((OUT, LANES), F32)
    for s in (0, -4, -3, -2, -1, 1, 2, 3, 4):
        w = warped.at[s + HALF]
        fill(w, own_row(s), views[(s + HALF) * ANG + HALF][:, lanes].astype(F32))
        if s == 0:
            center_ref[...] = w[pl.ds(first_row(0), OUT), :]
        data, source = accumulate(s, w, None, center_ref[...], data, source)
    data_out[...] = data
    source_out[...] = source

    def body(a, carry, sign):
        ti = HALF + 1 + a if sign else HALF - 1 - a
        data, source = shifted_views(
            inner[sign, a],
            lambda s: views[(s + HALF) * ANG + ti],
            lambda name, q: edges[name][q * ANG + ti],
            center_ref[...],
            warped,
            side,
        )
        data_out[...] += data
        source_out[...] += source
        return carry

    for sign in (0, 1):
        lax.fori_loop(0, HALF, functools.partial(body, sign=sign), 0)


def both_sums(views, above, below, left, right, data_out, source_out, *scratch):
    edges = {"above": above, "below": below}
    for tile, inner in enumerate((left, right)):
        inner_sums(tile, views, edges, inner, data_out.at[tile], source_out.at[tile], *scratch)


def outer_sums(
    total_rows,
    total_cols,
    views,
    above,
    below,
    own,
    got_next,
    got_pair,
    data_in,
    source_in,
    edge,
    edge_center,
    scatter,
    zed_out,
    near_out,
    next_out,
    precond_out,
    message,
    turned,
    warped,
    side,
    center_ref,
    center_slab,
    left,
    right,
):
    even = is_even(COL)

    @pl.when(even)
    def _():
        unshare(got_next, 1, left)
        unshare(got_pair, 0, right)

    @pl.when(jnp.logical_not(even))
    def _():
        unshare(got_pair, 1, left)
        unshare(got_next, 0, right)

    edges = {"above": above, "below": below}
    zero_tails(warped)
    zero_tails(side)
    zero = jnp.zeros((OUT, LANES), F32)

    def edge_rows(row, count):
        return jnp.concatenate([x[pl.ds(row, count), :] for x in (left, own, right)], axis=1)

    def fill_center(at, ref, row, count):
        fill(center_slab.at[0], at, ref[:, :LANES].astype(F32))
        fill(center_slab.at[1], at, ref[:, LANES:].astype(F32))
        around = (left[pl.ds(row, count), :], ref[...], right[pl.ds(row, count), :])
        both = dot(jnp.concatenate(around, axis=1), edge_center[...])
        fill(warped.at[HALF], at, both[:, :LANES])
        fill(center_slab.at[2], at, both[:, LANES:])

    for name in ("above", "below"):
        at = PLACES[name, 1][1][1]
        fill_center(at, edges[name].at[ANG + HALF], packed_piece(name, 1), EDGE)
    fill_center(EDGE, views.at[HALF * ANG + HALF], HALF * ROWS, ROWS)
    center_ref[...] = warped[HALF, pl.ds(first_row(0), OUT), :]
    sums = shifted_views(
        edge[...],
        lambda s: edge_rows((s + HALF) * ROWS, ROWS),
        lambda name, q: edge_rows(packed_piece(name, q), EDGE),
        center_ref[...],
        warped,
        side,
    )

    parts = []
    for x in sums:
        for _ in range(3):
            part = x.astype(jnp.bfloat16)
            parts.append(part)
            x = x - part.astype(F32)
    spread = dot(jnp.concatenate(parts, axis=0), scatter[...])

    def total(inside, at):
        high, middle, low = (spread[(at + i) * OUT : (at + i + 1) * OUT] for i in range(3))
        return jnp.concatenate([inside[0], inside[1], zero], axis=1) + ((low + middle) + high)

    data_sum = total(data_in, 0)
    source_sum = total(source_in, 3)

    wide = 3 * LANES

    def before(x):
        return pltpu.roll(x, 1, 1)

    def after(x):
        return pltpu.roll(x, wide - 1, 1)

    def over(x):
        return pltpu.roll(x, 1, 0)

    def under(x):
        return pltpu.roll(x, OUT - 1, 0)

    at = first_row(0)
    here = jnp.concatenate([center_slab[i, pl.ds(at, OUT), :] for i in range(3)], axis=1)
    higher = jnp.concatenate([center_slab[i, pl.ds(at - 1, OUT), :] for i in range(3)], axis=1)
    lane = lax.broadcasted_iota(jnp.int32, (OUT, wide), 1)
    local_row = lax.broadcasted_iota(jnp.int32, (OUT, wide), 0) - 2
    column = jnp.where(lane < wide - 64, lane, lane - wide) + lax.axis_index(COL) * COLS
    row = local_row + lax.axis_index(ROW) * ROWS
    across = here - before(here)
    vertical = here - higher
    h_left = jnp.where((column >= 1) & (column <= total_cols - 1), jnp.exp(-across * across), 0.0)
    v_up = jnp.where((row >= 1) & (row <= total_rows - 1), jnp.exp(-vertical * vertical), 0.0)
    h_right = after(h_left)
    v_down = under(v_up)
    coeff = DAMPING + data_sum * (0.25 / VIEWS)
    source = source_sum * (-0.5 / VIEWS)
    precond = coeff + SMOOTH * (h_left + h_right + v_up + v_down)
    inverse = 1.0 / precond

    def neighbours(x):
        total = h_left * before(x) + h_right * after(x) + v_up * over(x) + v_down * under(x)
        return SMOOTH * inverse * total

    zed = source * inverse
    near = neighbours(zed)
    nxt = neighbours(near)

    def block(x):
        return x[:, :COLS]

    zed, near, nxt, precond = block(zed), block(near), block(nxt), block(precond)
    zed_out[...] = zed
    near_out[...] = near
    next_out[...] = nxt
    precond_out[...] = precond
    mine = (block(local_row) >= 0) & (block(local_row) < ROWS)

    def inner(x, y):
        return jnp.sum(jnp.where(mine, precond * x * y, 0.0), keepdims=True)

    zz = inner(zed, zed)
    zn = inner(zed, near)
    kappa = jnp.clip(zn / jnp.where(zz > 0, zz, 1.0), -1.0, 1.0)
    y = near - kappa * zed
    g = nxt - kappa * near
    numbers = (
        (0, inner(y, y)),
        (1, inner(y, g)),
        (32, 2.0 * inner(y, zed)),
        (33, inner(y, near) + inner(zed, g)),
        (64, zz),
        (65, zn),
        (96, kappa),
        (97, kappa),
    )
    place = lax.broadcasted_iota(jnp.int32, (1, LANES), 1)
    out = jnp.zeros((1, LANES), F32)
    for where, number in numbers:
        out = jnp.where(place == where, number, out)
    message[...] = out
    turned[...] = pltpu.roll(out, 2, 1)


def finish(messages, zed_ref, near_ref, next_ref, precond_ref, increment, residual):
    all_of = messages[...]
    total = jnp.sum(all_of, axis=0, keepdims=True)
    zz = total[:, 64:65] + total[:, 66:67]
    zn = total[:, 65:66] + total[:, 67:68]
    kappa = zn / zz
    delta = pltpu.roll(all_of, 32, 1) - kappa
    linear = pltpu.roll(all_of, 96, 1)
    quad = pltpu.roll(all_of, 64, 1)
    moved = jnp.sum(all_of + delta * (linear + delta * quad), axis=0, keepdims=True)
    yy = moved[:, 0:1] + moved[:, 2:3]
    yny = moved[:, 1:2] + moved[:, 3:4]
    step0 = zz / (zz - zn)
    beta = step0 * step0 * yy / zz
    step1 = yy / (yy - yny - step0 * yy * yy / zz)
    rows = pl.ds(2, ROWS)
    zed = zed_ref[rows, :]
    near = near_ref[rows, :]
    nxt = next_ref[rows, :]
    y = near - kappa * zed
    g = nxt - kappa * near
    increment[...] = step0 * zed + step1 * (step0 * y + beta * zed)
    residual[...] = precond_ref[rows, :] * (
        step0 * y - step1 * (step0 * (y - g) + beta * (zed - near))
    )


def call(kernel, outs, scratch=(), name=None):
    return pl.pallas_call(
        kernel,
        out_shape=outs,
        scratch_shapes=list(scratch),
        compiler_params=pltpu.CompilerParams(vmem_limit_bytes=24 * 1024 * 1024),
        name=name,
    )


def swap(array, axis, start):
    pairs = []
    for i in range(start, lax.axis_size(axis) - 1, 2):
        pairs += [(i, i + 1), (i + 1, i)]
    return lax.ppermute(array, axis, pairs)


def shards(views):
    rows, cols = lax.axis_size(ROW), lax.axis_size(COL)
    left_inner, right_inner, edge_matrix, center, scatter = (jnp.asarray(x) for x in tables())
    bf16 = jnp.bfloat16
    struct = jax.ShapeDtypeStruct

    edge = struct((PIECES * ANG, EDGE, COLS), bf16)
    room = pltpu.VMEM(edge.shape, bf16)
    pair, after = call(pack_rows, (edge, edge), (room, room), name="pack_rows")(
        views[HALF * ANG :, :EDGE, :], views[: (HALF + 1) * ANG, ROWS - EDGE :, :]
    )
    pair = swap(pair, ROW, 0)
    after = swap(after, ROW, 1)
    shared = struct((SHARED, LANES), bf16)
    own, to_left, to_right, pack = call(
        pack_own,
        (struct((ANG * ROWS, LANES), bf16), shared, shared, struct((ANG, COLS, LANES), bf16)),
        name="pack_own",
    )(views)
    room = pltpu.VMEM(shared.shape, bf16)
    above, below, own, pair, after = call(
        pack_edges,
        (edge, edge, struct((PACKED, LANES), bf16), shared, shared),
        (room, room),
        name="pack_edges",
    )(pair, after, pack, own, to_left, to_right)
    after = swap(after, COL, 1)
    pair = swap(pair, COL, 0)
    slab = pltpu.VMEM((ANG, SLAB, LANES), F32)
    tile = pltpu.VMEM((OUT, LANES), F32)
    sums = struct((2, OUT, LANES), F32)
    data, source = call(both_sums, (sums, sums), (slab, slab, tile), name="inner_sums")(
        views, above, below, left_inner, right_inner
    )
    field = struct((OUT, COLS), F32)
    zed, near, nxt, precond, message, turned = call(
        functools.partial(outer_sums, rows * ROWS, cols * COLS),
        (field, field, field, field, struct((1, LANES), F32), struct((1, LANES), F32)),
        (
            slab,
            slab,
            tile,
            pltpu.VMEM((3, SLAB, LANES), F32),
            pltpu.VMEM((PACKED, LANES), bf16),
            pltpu.VMEM((PACKED, LANES), bf16),
        ),
        name="outer_sums",
    )(views, above, below, own, after, pair, data, source, edge_matrix, center, scatter)
    message = message + swap(turned, ROW, 0)
    n = rows * cols // 2
    messages = lax.all_to_all(
        jnp.broadcast_to(message[None], (n, 1, LANES)), ("chip", COL), 0, 0, tiled=True
    ).reshape(n, LANES)
    block = struct((ROWS, COLS), F32)
    return call(finish, (block, block), name="finish")(messages, zed, near, nxt, precond)


def solution(mesh):
    rows, cols = mesh.devices.shape
    finer = Mesh(mesh.devices.reshape(rows // 2, 2, cols), (*ROW, COL))
    return jax.shard_map(
        shards,
        mesh=finer,
        in_specs=(P(None, ROW, COL),),
        out_specs=(P(ROW, COL), P(ROW, COL)),
        check_vma=False,
    )
```

```python
import functools

import jax
import jax.numpy as jnp
import ml_dtypes
import numpy as np
from jax import lax
from jax.experimental import pallas as pl
from jax.experimental.pallas import tpu as pltpu
from jax.sharding import Mesh
from jax.sharding import PartitionSpec as P

ANG = 9
VIEWS = 81
HALF = ANG // 2
D0 = 3
ROWS = 64
COLS = 256
EDGE = 16
OUT = 72
SLAB = 96
PIECES = 3
PACKED = ANG * ROWS + 2 * PIECES * EDGE
PAIRS = ((-4, -3), (-2, -1), (1, 2), (3, 4))
SHARED = len(PAIRS) * ROWS
CUTS = ((0, 18), (18, 12), (30, 15))
SPARE = tuple((p, *cut, there) for cut, (p, there) in zip(CUTS, ((0, 45), (0, 109), (1, 45))))
LANES = 128
SMOOTH = 2.0
DAMPING = 0.1
ROW = ("chip", "core")
COL = "col"
F32 = jnp.float32


def lane_first(t, c):
    return D0 * t * (t + 1) // 2 + c


def lane_last(t, c):
    a = abs(t)
    return 64 + D0 * a * (a + 1) // 2 + c - (COLS - D0 * a - D0)


def lane_here(t, c):
    return 45 + 2 * (-t - 1) + c if t < 0 else 109 + 2 * (t - 1) + c - (COLS - 2)


def edge_source(t, c):
    if c < 0:
        return lane_last(t, COLS + c)
    if c >= COLS:
        return 2 * LANES + lane_first(t, c - COLS)
    if t >= 0 and c <= D0 * t + D0 - 1:
        return LANES + lane_first(t, c)
    if t <= 0 and c >= COLS - D0 * abs(t) - D0:
        return LANES + lane_last(t, c)
    return LANES + lane_here(t, c)


def edge_pixels():
    for t in range(-HALF, HALF + 1):
        for column in range(-2, D0 * -t + 1 if t < 0 else 0):
            yield t, column
        for column in range(COLS - 1 - D0 * t if t > 0 else COLS, COLS + 2):
            yield t, column


def tables():
    inner = np.zeros((2, 2, HALF, COLS, 2 * LANES), np.float32)
    for tile in (0, 1):
        for a in range(1, HALF + 1):
            for sign in (0, 1):
                t = a if sign else -a
                for j in range(LANES):
                    c = tile * LANES + j + D0 * t
                    if 1 <= c < COLS - 1:
                        inner[tile, sign, a - 1, c, j] += 1
                        inner[tile, sign, a - 1, c + 1, LANES + j] += t
                        inner[tile, sign, a - 1, c - 1, LANES + j] -= t
    edge = np.zeros((3 * LANES, 2 * LANES), np.float32)
    center = np.zeros((LANES + COLS + LANES, 2 * LANES), np.float32)
    scatter = np.zeros((LANES, 3 * LANES), np.float32)

    def center_source(c):
        if c < 0:
            return lane_last(0, COLS + c)
        return LANES + c if c < COLS else LANES + COLS + lane_first(0, c - COLS)

    for lane, (t, col) in enumerate(edge_pixels()):
        c = col + D0 * t
        edge[edge_source(t, c), lane] += 1
        if t:
            edge[edge_source(t, c + 1), LANES + lane] += t
            edge[edge_source(t, c - 1), LANES + lane] -= t
        center[center_source(col), lane] = 1
        scatter[lane, col % (3 * LANES)] = 1
    for col in (-3, -2, -1, COLS, COLS + 1, COLS + 2):
        center[center_source(col), LANES + col % LANES] = 1
    return tuple(x.astype(ml_dtypes.bfloat16) for x in (*inner, edge, center, scatter))


def dot(a, b):
    return jnp.dot(a, b, preferred_element_type=F32)


def is_even(axis):
    return lax.rem(lax.axis_index(axis), 2) == 0


def pack_rows(tops, bottoms, send_pair, send_next, ups_out, downs_out):
    even = is_even(ROW)
    index = lax.broadcasted_iota(jnp.int32, (EDGE, COLS), 0)

    def put(ups, q, ti, rows):
        (ups_out if ups else downs_out)[q * ANG + ti] = rows.astype(jnp.bfloat16)

    for ti in range(ANG):

        def first(s, ti=ti):
            return tops[s * ANG + ti].astype(F32)

        def last(s, ti=ti):
            return bottoms[(s + HALF) * ANG + ti].astype(F32)

        put(True, 0, ti, first(4))
        put(True, 1, ti, jnp.where(index < 12, first(3), pltpu.roll(first(0), 12, 0)))
        put(True, 2, ti, jnp.where(index < 9, first(2), pltpu.roll(first(1), 9, 0)))
        put(False, 0, ti, last(-4))
        put(False, 1, ti, jnp.where(index < 4, pltpu.roll(last(0), 4, 0), last(-3)))
        put(False, 2, ti, jnp.where(index < 7, pltpu.roll(last(-1), 7, 0), last(-2)))

    @pl.when(even)
    def _():
        send_pair[...] = downs_out[...]
        send_next[...] = ups_out[...]

    @pl.when(jnp.logical_not(even))
    def _():
        send_pair[...] = ups_out[...]
        send_next[...] = downs_out[...]


PLACES = {
    ("above", 0): ((-4, 0),),
    ("above", 1): ((-3, 0), (0, 12)),
    ("above", 2): ((-2, 0), (-1, 9)),
    ("below", 0): ((4, ROWS),),
    ("below", 1): ((3, ROWS), (0, EDGE + ROWS - 12)),
    ("below", 2): ((2, ROWS), (1, ROWS - 9)),
}


def packed_piece(side, q):
    return ANG * ROWS + ((0 if side == "above" else PIECES) + q) * EDGE


def piece_places():
    slots = ((1, 109), (2, 45), (2, 109), (3, 45), (3, 109))
    places = {}
    for n, (name, cut) in enumerate((name, cut) for name in PLACES for cut in CUTS):
        p, there = slots[n % len(slots)]
        row = p * ROWS + n // len(slots) * EDGE
        places.setdefault(name, []).append((row, *cut, there))
    return places


def share(first_of, second_of, to_left, to_right, at, spare=()):
    lane = lax.broadcasted_iota(jnp.int32, first_of.shape, 1)
    rows = pl.ds(at, first_of.shape[0])
    for out, turn in ((to_left, 0), (to_right, 64)):
        low = pltpu.roll(first_of, 64, 1) if turn else first_of
        high = second_of if turn else pltpu.roll(second_of, 64, 1)
        both = jnp.where(lane < 64, low, high)
        for pack, start, count, there in spare:
            moved = pltpu.roll(pack, (there - start - turn) % LANES, 1)
            both = jnp.where((lane >= there) & (lane < there + count), moved, both)
        out[rows, :] = both.astype(jnp.bfloat16)


def pack_own(views, own, to_left, to_right, pack):
    column = lax.broadcasted_iota(jnp.int32, (COLS, LANES), 0)
    lane = lax.broadcasted_iota(jnp.int32, (COLS, LANES), 1)
    for t in range(-HALF, HALF + 1):
        hit = jnp.zeros((COLS, LANES), F32)
        if t >= 0:
            bound = D0 * t + D0
            hit = jnp.where((column < bound) & (lane - column == lane_first(t, 0)), 1.0, hit)
        if t <= 0:
            start = COLS - D0 * abs(t) - D0
            apart = lane_last(t, start) - start
            hit = jnp.where((column >= start) & (lane - column == apart), 1.0, hit)
        if t:
            near = column < 2 if t < 0 else column >= COLS - 2
            apart = lane_here(t, 0)
            hit = jnp.where(near & (lane - column == apart), 1.0, hit)
        pack[t + HALF] = hit.astype(jnp.bfloat16)

    def packed(s):
        total = dot(views[(s + HALF) * ANG], pack[0])
        for ti in range(1, ANG):
            total = total + dot(views[(s + HALF) * ANG + ti], pack[ti])
        own[(s + HALF) * ROWS : (s + HALF + 1) * ROWS, :] = total.astype(jnp.bfloat16)
        return total

    middle = packed(0)
    for p, (low, high) in enumerate(PAIRS):
        spare = [(middle, *lanes) for q, *lanes in SPARE if q == p]
        share(packed(low), packed(high), to_left, to_right, p * ROWS, spare)


def pack_edges(
    got_next, got_pair, pack, own_in, left_in, right_in,
    above, below, own, send_pair, send_next, to_left, to_right,
):
    even = is_even(ROW)

    @pl.when(even)
    def _():
        below[...] = got_pair[...]
        above[...] = got_next[...]

    @pl.when(jnp.logical_not(even))
    def _():
        below[...] = got_next[...]
        above[...] = got_pair[...]

    own[: ANG * ROWS, :] = own_in[...]
    edges = {"above": above, "below": below}
    total = jnp.zeros((len(PLACES) * EDGE, LANES), F32)
    for ti in range(ANG):
        rows = [edges[side][q * ANG + ti] for side, q in PLACES]
        total = total + dot(jnp.concatenate(rows, axis=0), pack[ti])
    parts = {}
    places = piece_places()
    for i, (side, q) in enumerate(PLACES):
        piece = total[i * EDGE : (i + 1) * EDGE]
        own[pl.ds(packed_piece(side, q), EDGE), :] = piece.astype(jnp.bfloat16)
        for row, *lanes in places[side, q]:
            parts.setdefault(row, []).append((piece, *lanes))
    lane = lax.broadcasted_iota(jnp.int32, (EDGE, LANES), 1)
    for out, block, turn in ((to_left, left_in, 0), (to_right, right_in, 64)):
        out[...] = block[...]
        for row, group in parts.items():
            both = block[row : row + EDGE, :].astype(F32)
            for piece, start, count, there in group:
                moved = pltpu.roll(piece, (there - start - turn) % LANES, 1)
                both = jnp.where((lane >= there) & (lane < there + count), moved, both)
            out[row : row + EDGE, :] = both.astype(jnp.bfloat16)
    even = is_even(COL)

    @pl.when(even)
    def _():
        send_pair[...] = to_right[...]
        send_next[...] = to_left[...]

    @pl.when(jnp.logical_not(even))
    def _():
        send_pair[...] = to_left[...]
        send_next[...] = to_right[...]


def unshare(source, high, out):
    def rows_at(at, count):
        return source[pl.ds(at, count), :].astype(F32)

    for p, pair in enumerate(PAIRS):
        for half, s in enumerate(pair):
            rows = rows_at(p * ROWS, ROWS)
            if half != high:
                rows = pltpu.roll(rows, 64, 1)
            out[pl.ds((s + HALF) * ROWS, ROWS), :] = rows.astype(jnp.bfloat16)

    def join(parts, to, count):
        lane = lax.broadcasted_iota(jnp.int32, (count, LANES), 1)
        whole = jnp.zeros((count, LANES), F32)
        for row, start, lanes, there in parts:
            at = start + 64 * high
            rows = pltpu.roll(rows_at(row, count), (at - there) % LANES, 1)
            whole = jnp.where((lane >= at) & (lane < at + lanes), rows, whole)
        out[pl.ds(to, count), :] = whole.astype(jnp.bfloat16)

    join([(p * ROWS, *lanes) for p, *lanes in SPARE], HALF * ROWS, ROWS)
    for (side, q), parts in piece_places().items():
        join(parts, packed_piece(side, q), EDGE)


def first_row(s):
    return D0 * s - 2 if s > 0 else EDGE - 2 + D0 * s


def own_row(s):
    return 0 if s > 0 else EDGE


def accumulate(s, warped, side, center, data, source):
    at = first_row(s)
    value = warped[pl.ds(at, OUT), :]
    slope = float(s) * (warped[pl.ds(at + 1, OUT), :] - warped[pl.ds(at - 1, OUT), :])
    if side is not None:
        side_part = side[pl.ds(at, OUT), :]
        slope = slope + side_part if s else side_part
    error = value - center
    robust = lax.rsqrt(1.0 + error * error)
    weighted = robust * slope
    return data + weighted * slope, source + weighted * error


def fill(slab, at, array):
    slab[pl.ds(at, array.shape[0]), :] = array


def zero_tails(slabs):
    for i in range(ANG):
        slabs[i, pl.ds(ROWS, SLAB - ROWS), :] = jnp.zeros((SLAB - ROWS, LANES), F32)


def fill_pieces(parts_of, outs):
    for (side, q), places in PLACES.items():
        parts = parts_of(side, q)
        for s, at in places:
            for out, part in zip(outs, parts):
                fill(out.at[s + HALF], at, part)


def halves(both):
    return both[:, :LANES], both[:, LANES:]


def shifted_views(matrix, own, piece, center, warped, side):
    span = range(-HALF, HALF + 1)
    rows = [own(s) for s in span] + [piece(name, q) for name, q in PLACES]
    both = dot(jnp.concatenate(rows, axis=0), matrix)
    first = {key: ANG * ROWS + i * EDGE for i, key in enumerate(PLACES)}

    def part(at, count):
        return both[at : at + count, :LANES], both[at : at + count, LANES:]

    fill_pieces(lambda name, q: part(first[name, q], EDGE), (warped, side))
    data = source = jnp.zeros((OUT, LANES), F32)
    for s in span:
        w, d = warped.at[s + HALF], side.at[s + HALF]
        shifted, slope = part((s + HALF) * ROWS, ROWS)
        fill(w, own_row(s), shifted)
        fill(d, own_row(s), slope)
        data, source = accumulate(s, w, d, center, data, source)
    return data, source


def inner_sums(tile, views, edges, inner, data_out, source_out, warped, side, center_ref):
    zero_tails(warped)
    zero_tails(side)
    lanes = slice(tile * LANES, (tile + 1) * LANES)
    fill_pieces(
        lambda name, q: (edges[name][q * ANG + HALF][:, lanes].astype(F32),), (warped,)
    )
    data = source = jnp.zeros((OUT, LANES), F32)
    for s in (0, -4, -3, -2, -1, 1, 2, 3, 4):
        w = warped.at[s + HALF]
        fill(w, own_row(s), views[(s + HALF) * ANG + HALF][:, lanes].astype(F32))
        if s == 0:
            center_ref[...] = w[pl.ds(first_row(0), OUT), :]
        data, source = accumulate(s, w, None, center_ref[...], data, source)
    data_out[...] = data
    source_out[...] = source

    def body(a, carry, sign):
        ti = HALF + 1 + a if sign else HALF - 1 - a
        data, source = shifted_views(
            inner[sign, a],
            lambda s: views[(s + HALF) * ANG + ti],
            lambda name, q: edges[name][q * ANG + ti],
            center_ref[...],
            warped,
            side,
        )
        data_out[...] += data
        source_out[...] += source
        return carry

    for sign in (0, 1):
        lax.fori_loop(0, HALF, functools.partial(body, sign=sign), 0, unroll=True)


def both_sums(views, above, below, left, right, data_out, source_out, *scratch):
    edges = {"above": above, "below": below}
    for tile, inner in enumerate((left, right)):
        inner_sums(tile, views, edges, inner, data_out.at[tile], source_out.at[tile], *scratch)


def outer_sums(
    total_rows,
    total_cols,
    views,
    above,
    below,
    own,
    got_next,
    got_pair,
    data_in,
    source_in,
    edge,
    edge_center,
    scatter,
    zed_out,
    near_out,
    next_out,
    precond_out,
    message,
    turned,
    warped,
    side,
    center_ref,
    center_slab,
    left,
    right,
):
    even = is_even(COL)

    @pl.when(even)
    def _():
        unshare(got_next, 1, left)
        unshare(got_pair, 0, right)

    @pl.when(jnp.logical_not(even))
    def _():
        unshare(got_pair, 1, left)
        unshare(got_next, 0, right)

    edges = {"above": above, "below": below}
    zero_tails(warped)
    zero_tails(side)
    zero = jnp.zeros((OUT, LANES), F32)

    def edge_rows(row, count):
        return jnp.concatenate([x[pl.ds(row, count), :] for x in (left, own, right)], axis=1)

    def fill_center(at, ref, row, count):
        fill(center_slab.at[0], at, ref[:, :LANES].astype(F32))
        fill(center_slab.at[1], at, ref[:, LANES:].astype(F32))
        around = (left[pl.ds(row, count), :], ref[...], right[pl.ds(row, count), :])
        both = dot(jnp.concatenate(around, axis=1), edge_center[...])
        fill(warped.at[HALF], at, both[:, :LANES])
        fill(center_slab.at[2], at, both[:, LANES:])

    for name in ("above", "below"):
        at = PLACES[name, 1][1][1]
        fill_center(at, edges[name].at[ANG + HALF], packed_piece(name, 1), EDGE)
    fill_center(EDGE, views.at[HALF * ANG + HALF], HALF * ROWS, ROWS)
    center_ref[...] = warped[HALF, pl.ds(first_row(0), OUT), :]
    sums = shifted_views(
        edge[...],
        lambda s: edge_rows((s + HALF) * ROWS, ROWS),
        lambda name, q: edge_rows(packed_piece(name, q), EDGE),
        center_ref[...],
        warped,
        side,
    )

    parts = []
    for x in sums:
        for _ in range(3):
            part = x.astype(jnp.bfloat16)
            parts.append(part)
            x = x - part.astype(F32)
    spread = dot(jnp.concatenate(parts, axis=0), scatter[...])

    def total(inside, at):
        high, middle, low = (spread[(at + i) * OUT : (at + i + 1) * OUT] for i in range(3))
        return jnp.concatenate([inside[0], inside[1], zero], axis=1) + ((low + middle) + high)

    data_sum = total(data_in, 0)
    source_sum = total(source_in, 3)

    wide = 3 * LANES

    def before(x):
        return pltpu.roll(x, 1, 1)

    def after(x):
        return pltpu.roll(x, wide - 1, 1)

    def over(x):
        return pltpu.roll(x, 1, 0)

    def under(x):
        return pltpu.roll(x, OUT - 1, 0)

    at = first_row(0)
    here = jnp.concatenate([center_slab[i, pl.ds(at, OUT), :] for i in range(3)], axis=1)
    higher = jnp.concatenate([center_slab[i, pl.ds(at - 1, OUT), :] for i in range(3)], axis=1)
    lane = lax.broadcasted_iota(jnp.int32, (OUT, wide), 1)
    local_row = lax.broadcasted_iota(jnp.int32, (OUT, wide), 0) - 2
    column = jnp.where(lane < wide - 64, lane, lane - wide) + lax.axis_index(COL) * COLS
    row = local_row + lax.axis_index(ROW) * ROWS
    across = here - before(here)
    vertical = here - higher
    h_left = jnp.where((column >= 1) & (column <= total_cols - 1), jnp.exp(-across * across), 0.0)
    v_up = jnp.where((row >= 1) & (row <= total_rows - 1), jnp.exp(-vertical * vertical), 0.0)
    h_right = after(h_left)
    v_down = under(v_up)
    coeff = DAMPING + data_sum * (0.25 / VIEWS)
    source = source_sum * (-0.5 / VIEWS)
    precond = coeff + SMOOTH * (h_left + h_right + v_up + v_down)
    inverse = 1.0 / precond

    def neighbours(x):
        total = h_left * before(x) + h_right * after(x) + v_up * over(x) + v_down * under(x)
        return SMOOTH * inverse * total

    zed = source * inverse
    near = neighbours(zed)
    nxt = neighbours(near)

    def block(x):
        return x[:, :COLS]

    zed, near, nxt, precond = block(zed), block(near), block(nxt), block(precond)
    zed_out[...] = zed
    near_out[...] = near
    next_out[...] = nxt
    precond_out[...] = precond
    mine = (block(local_row) >= 0) & (block(local_row) < ROWS)

    def inner(x, y):
        return jnp.sum(jnp.where(mine, precond * x * y, 0.0), keepdims=True)

    zz = inner(zed, zed)
    zn = inner(zed, near)
    kappa = jnp.clip(zn / jnp.where(zz > 0, zz, 1.0), -1.0, 1.0)
    y = near - kappa * zed
    g = nxt - kappa * near
    numbers = (
        (0, inner(y, y)),
        (1, inner(y, g)),
        (32, 2.0 * inner(y, zed)),
        (33, inner(y, near) + inner(zed, g)),
        (64, zz),
        (65, zn),
        (96, kappa),
        (97, kappa),
    )
    place = lax.broadcasted_iota(jnp.int32, (1, LANES), 1)
    out = jnp.zeros((1, LANES), F32)
    for where, number in numbers:
        out = jnp.where(place == where, number, out)
    message[...] = out
    turned[...] = pltpu.roll(out, 2, 1)


def finish(messages, zed_ref, near_ref, next_ref, precond_ref, increment, residual):
    all_of = messages[...]
    total = jnp.sum(all_of, axis=0, keepdims=True)
    zz = total[:, 64:65] + total[:, 66:67]
    zn = total[:, 65:66] + total[:, 67:68]
    kappa = zn / zz
    delta = pltpu.roll(all_of, 32, 1) - kappa
    linear = pltpu.roll(all_of, 96, 1)
    quad = pltpu.roll(all_of, 64, 1)
    moved = jnp.sum(all_of + delta * (linear + delta * quad), axis=0, keepdims=True)
    yy = moved[:, 0:1] + moved[:, 2:3]
    yny = moved[:, 1:2] + moved[:, 3:4]
    step0 = zz / (zz - zn)
    beta = step0 * step0 * yy / zz
    step1 = yy / (yy - yny - step0 * yy * yy / zz)
    rows = pl.ds(2, ROWS)
    zed = zed_ref[rows, :]
    near = near_ref[rows, :]
    nxt = next_ref[rows, :]
    y = near - kappa * zed
    g = nxt - kappa * near
    increment[...] = step0 * zed + step1 * (step0 * y + beta * zed)
    residual[...] = precond_ref[rows, :] * (
        step0 * y - step1 * (step0 * (y - g) + beta * (zed - near))
    )


def call(kernel, outs, scratch=(), name=None):
    return pl.pallas_call(
        kernel,
        out_shape=outs,
        scratch_shapes=list(scratch),
        compiler_params=pltpu.CompilerParams(vmem_limit_bytes=24 * 1024 * 1024),
        name=name,
    )


def swap(array, axis, start):
    pairs = []
    for i in range(start, lax.axis_size(axis) - 1, 2):
        pairs += [(i, i + 1), (i + 1, i)]
    return lax.ppermute(array, axis, pairs)


def shards(views):
    rows, cols = lax.axis_size(ROW), lax.axis_size(COL)
    left_inner, right_inner, edge_matrix, center, scatter = (jnp.asarray(x) for x in tables())
    bf16 = jnp.bfloat16
    struct = jax.ShapeDtypeStruct

    edge = struct((PIECES * ANG, EDGE, COLS), bf16)
    room = pltpu.VMEM(edge.shape, bf16)
    pair, after = call(pack_rows, (edge, edge), (room, room), name="pack_rows")(
        views[HALF * ANG :, :EDGE, :], views[: (HALF + 1) * ANG, ROWS - EDGE :, :]
    )
    pair = swap(pair, ROW, 0)
    after = swap(after, ROW, 1)
    shared = struct((SHARED, LANES), bf16)
    own, to_left, to_right, pack = call(
        pack_own,
        (struct((ANG * ROWS, LANES), bf16), shared, shared, struct((ANG, COLS, LANES), bf16)),
        name="pack_own",
    )(views)
    room = pltpu.VMEM(shared.shape, bf16)
    above, below, own, pair, after = call(
        pack_edges,
        (edge, edge, struct((PACKED, LANES), bf16), shared, shared),
        (room, room),
        name="pack_edges",
    )(after, pair, pack, own, to_left, to_right)
    after = swap(after, COL, 1)
    pair = swap(pair, COL, 0)
    slab = pltpu.VMEM((ANG, SLAB, LANES), F32)
    tile = pltpu.VMEM((OUT, LANES), F32)
    sums = struct((2, OUT, LANES), F32)
    data, source = call(both_sums, (sums, sums), (slab, slab, tile), name="inner_sums")(
        views, above, below, left_inner, right_inner
    )
    field = struct((OUT, COLS), F32)
    zed, near, nxt, precond, message, turned = call(
        functools.partial(outer_sums, rows * ROWS, cols * COLS),
        (field, field, field, field, struct((1, LANES), F32), struct((1, LANES), F32)),
        (
            slab,
            slab,
            tile,
            pltpu.VMEM((3, SLAB, LANES), F32),
            pltpu.VMEM((PACKED, LANES), bf16),
            pltpu.VMEM((PACKED, LANES), bf16),
        ),
        name="outer_sums",
    )(views, above, below, own, after, pair, data, source, edge_matrix, center, scatter)
    message = message + swap(turned, ROW, 0)
    n = rows * cols // 2
    messages = lax.all_to_all(
        jnp.broadcast_to(message[None], (n, 1, LANES)), ("chip", COL), 0, 0, tiled=True
    ).reshape(n, LANES)
    block = struct((ROWS, COLS), F32)
    return call(finish, (block, block), name="finish")(messages, zed, near, nxt, precond)


def solution(mesh):
    rows, cols = mesh.devices.shape
    finer = Mesh(mesh.devices.reshape(rows // 2, 2, cols), (*ROW, COL))
    return jax.shard_map(
        shards,
        mesh=finer,
        in_specs=(P(None, ROW, COL),),
        out_specs=(P(ROW, COL), P(ROW, COL)),
        check_vma=False,
    )
```
